32 devices in a mesh: seq: 4 (over y, x), shard: 8 (over z, core).
Axes of the slice: x: 2, y: 2, z: 4, core: 2. Of those that a mesh axis runs over, the one named last changes fastest.
Arguments:
- tokens: bfloat16 [8, 2048, 1024], P('shard', 'seq'), may hold values from -6 to 6
- order: int32 [8, 2048], P('shard'), may hold values from 0 to 2047, each once within a row
- seq_lengths: int32 [8, 3], P('shard'), may hold values from 1 to 1365, 2048 in all within a row
- attn_gain: bfloat16 [1024], P('shard'), may hold values from 0.5 to 1.5
- w_query: bfloat16 [1024, 1024], P('shard'), may hold values from -0.1875 to 0.1875
- w_key: bfloat16 [1024, 512], P('shard'), may hold values from -0.1875 to 0.1875
- w_value: bfloat16 [1024, 512], P('shard'), may hold values from -0.1875 to 0.1875
- query_gain: bfloat16 [64], replicated, may hold values from 1.1953125 to 1.796875
- key_gain: bfloat16 [64], replicated, may hold values from 1.1953125 to 1.796875
- w_out: bfloat16 [1024, 1024], P('shard'), may hold values from -1 to 1
- ffn_gain: bfloat16 [1024], P('shard'), may hold values from 0.5 to 1.5
- w_gate: bfloat16 [1024, 4608], P('shard'), may hold values from -0.1875 to 0.1875
- w_up: bfloat16 [1024, 4608], P('shard'), may hold values from -0.1875 to 0.1875
- w_down: bfloat16 [4608, 1024], P('shard'), may hold values from -0.09375 to 0.09375
- cotangent: bfloat16 [8, 2048, 1024], P('shard', 'seq'), may hold values from -6 to 6
Outputs:
- block_out: bfloat16 [8, 2048, 1024], P('shard', 'seq')
- d_tokens: bfloat16 [8, 2048, 1024], P('shard', 'seq')
- d_attn_gain: float32 [1024], P('shard')
- d_w_query: float32 [1024, 1024], P('shard')
- d_w_key: float32 [1024, 512], P('shard')
- d_w_value: float32 [1024, 512], P('shard')
- d_query_gain: float32 [64], replicated
- d_key_gain: float32 [64], replicated
- d_w_out: float32 [1024, 1024], P('shard')
- d_ffn_gain: float32 [1024], P('shard')
- d_w_gate: float32 [1024, 4608], P('shard')
- d_w_up: float32 [1024, 4608], P('shard')
- d_w_down: float32 [4608, 1024], P('shard')
The draws below stay inside these ranges and needn't reach their ends.
Inputs may be any that keep to these rules, and one draw needn't show every extreme that they name: Each row is a permutation of the 2048 tokens of one group: order[j] is the given-order token at dealt position j. `seq_lengths`: each row sums to 2048; its longest sequence has exactly 1365 tokens.
All inputs are finite; a program needn't handle non-finite values.
Results may differ from the reference program's by a relative error of at most 0.02.
Values may be sent and summed in bfloat16 or wider, within the bound.
A program may use at most 256 MiB of HBM per device.

```python
import math
import jax
import jax.numpy as jnp
import numpy as np
from jax import lax

D = 1024
HEADS = 16
KV_HEADS = 8
HEAD_DIM = 64
FF = 4608
SEQS = 3
GROUP_TOK = 2048
GROUPS = 8
MOST = 1365


def block_levels(rng, dims, cuts, smallest, largest):
    def one(axis_at, shards_of):
        steps = jax.random.uniform(jax.random.fold_in(jax.random.fold_in(rng, 6), axis_at), (shards_of,), jnp.float32, smallest / len(cuts), largest / len(cuts))
        return jnp.repeat(jnp.exp(steps), dims[axis_at] // shards_of).reshape((-1,) + (1,) * (len(dims) - axis_at - 1))

    level = one(*cuts[0])
    for cut in cuts[1:]:
        level = level * one(*cut)
    return level


def length_profile(number_of, total, bound, skew):
    loads = [(1 << 20) // math.isqrt(standing ** skew) + 1 for standing in range(2, number_of + 1)]
    spare, counts = total - bound - (number_of - 1), [1] * (number_of - 1)
    while spare > 0:
        candidates = [i for i in range(number_of - 1) if counts[i] < bound]
        whole, remaining = sum([loads[i] for i in candidates]), spare
        for i in candidates:
            extra = min(bound - counts[i], max(1, remaining * loads[i] // whole), spare)
            counts[i] = counts[i] + extra
            spare = spare - extra
    return np.array([bound] + counts)


def uneven(key, number_of, total, limit, slope):
    if number_of == 2:
        one = jax.random.randint(key, (), max(1, total - limit), min(limit, total - 1) + 1)
        return jnp.stack([one, total - one])
    sizes = jnp.asarray(length_profile(number_of, total, limit, slope), jnp.int32)
    pairs = (number_of - 1) // 2
    donor, sink = sizes[1:1 + 2 * pairs:2], sizes[2:2 + 2 * pairs:2]
    room = jnp.minimum(donor - 1, limit - sink)
    passed = jax.random.randint(jax.random.fold_in(key, 1), (pairs,), 0, 1 << 20) % (room + 1)
    sizes = sizes.at[1:1 + 2 * pairs:2].set(donor - passed).at[2:2 + 2 * pairs:2].set(sink + passed)
    return sizes[jax.random.permutation(jax.random.fold_in(key, 2), number_of)]


def scatter_about(key, extent, scale, most, cuts=(), kind=jnp.bfloat16):
    gain = block_levels(key, extent, cuts, -0.22, 0.18) if cuts else 1.0
    entries = jax.random.normal(key, extent, jnp.float32) * scale * gain
    return jnp.minimum(jnp.maximum(entries, -most), most).astype(kind)


def setup_inputs(seed: int = 0) -> dict:
    arg_keys = jax.random.split(jax.random.key(seed), 16)
    return {
        "tokens": scatter_about(arg_keys[0], (GROUPS, GROUP_TOK, D), 1.0, 6.0, ((0, 8), (1, 4))),
        "order": jax.vmap(lambda own: jax.random.permutation(own, GROUP_TOK))(jax.random.split(arg_keys[1], GROUPS)).reshape((GROUPS, GROUP_TOK)).astype(jnp.int32),
        "seq_lengths": jax.vmap(lambda own: uneven(own, SEQS, GROUP_TOK, MOST, 2))(jax.random.split(arg_keys[2], GROUPS)).reshape((GROUPS, SEQS)).astype(jnp.int32),
        "attn_gain": jnp.clip(1.0 + 0.1 * jax.random.normal(arg_keys[3], (D,), jnp.float32), 0.5, 1.5).astype(jnp.bfloat16),
        "w_query": scatter_about(arg_keys[4], (D, HEADS * HEAD_DIM), D ** -0.5, 0.1875, ((0, 8),)),
        "w_key": scatter_about(arg_keys[5], (D, KV_HEADS * HEAD_DIM), D ** -0.5, 0.1875, ((0, 8),)),
        "w_value": scatter_about(arg_keys[6], (D, KV_HEADS * HEAD_DIM), D ** -0.5, 0.1875, ((0, 8),)),
        "query_gain": jnp.clip(jax.random.uniform(arg_keys[7], (HEAD_DIM,), jnp.float32, 1.1953125, 1.796875), 1.1953125, 1.796875).astype(jnp.bfloat16),
        "key_gain": jnp.clip(jax.random.uniform(arg_keys[8], (HEAD_DIM,), jnp.float32, 1.1953125, 1.796875), 1.1953125, 1.796875).astype(jnp.bfloat16),
        "w_out": scatter_about(arg_keys[9], (HEADS * HEAD_DIM, D), (HEADS * HEAD_DIM // 32) ** -0.5, 1.0, ((0, 8),)),
        "ffn_gain": jnp.clip(1.0 + 0.1 * jax.random.normal(arg_keys[10], (D,), jnp.float32), 0.5, 1.5).astype(jnp.bfloat16),
        "w_gate": scatter_about(arg_keys[11], (D, FF), D ** -0.5, 0.1875, ((0, 8),)),
        "w_up": scatter_about(arg_keys[12], (D, FF), D ** -0.5, 0.1875, ((0, 8),)),
        "w_down": scatter_about(arg_keys[13], (FF, D), FF ** -0.5, 0.09375, ((0, 8),)),
        "cotangent": scatter_about(arg_keys[14], (GROUPS, GROUP_TOK, D), 1.0, 6.0, ((0, 8), (1, 4))),
    }


EPSILON = 1e-05
ROPE_BASE = 1000000.0
MASKED = -1e+30

@jax.custom_vjp
def low(v):
    return lax.optimization_barrier(v.astype(jnp.bfloat16)).astype(jnp.float32)

@jax.custom_vjp
def low_back(v):
    return v

def low_keep(v):
    return (low(v), None)

def low_pass(kept, grad):
    return (grad,)

def back_keep(v):
    return (v, None)

def back_low(kept, grad):
    return (low(grad),)
low.defvjp(low_keep, low_pass)
low_back.defvjp(back_keep, back_low)

def matmul(left_arg, right_arg):
    return jnp.dot(left_arg, right_arg, precision=lax.Precision.HIGHEST)

def rms_norm(values, scale_gain):
    return values * lax.rsqrt(lax.optimization_barrier(jnp.mean(values * values, axis=-1, keepdims=True)) + EPSILON) * scale_gain

def rotary(values, places):
    half_dim = values.shape[-1] // 2
    frequency = ROPE_BASE ** (-2.0 * jnp.arange(half_dim, dtype=jnp.float32) / values.shape[-1])
    angles = places.astype(jnp.float32)[:, None] * frequency[None, :]
    cosine_table = jnp.concatenate([jnp.cos(angles), jnp.cos(angles)], axis=-1)[:, None, :]
    sine_table = jnp.concatenate([jnp.sin(angles), jnp.sin(angles)], axis=-1)[:, None, :]
    turned = jnp.concatenate([-values[..., half_dim:], values[..., :half_dim]], axis=-1)
    return values * cosine_table + turned * sine_table

def layout(lengths_row, token_count):
    seq_ends = jnp.cumsum(lengths_row).astype(jnp.int32)
    dealt_index = jnp.arange(token_count, dtype=jnp.int32)
    segment = lax.optimization_barrier(jnp.sum((dealt_index[:, None] >= seq_ends[None, :]).astype(jnp.int32), axis=1)).astype(jnp.int32)
    starts = (seq_ends - lengths_row).astype(jnp.int32)
    match_table = segment[:, None] == jnp.arange(lengths_row.shape[0], dtype=jnp.int32)[None, :]
    seq_begin = lax.optimization_barrier(jnp.sum(jnp.where(match_table, starts[None, :], 0), axis=1)).astype(jnp.int32)
    return (segment, dealt_index, dealt_index - seq_begin)

def attend(queries, key_rows, value_rows, segment, dealt_index):
    token_count, heads_all, head_dim = queries.shape
    kv_count = key_rows.shape[1]
    repeat = heads_all // kv_count
    score_scale = head_dim ** (-0.5)
    block_rows = min(512, token_count)
    grouped = queries.reshape(token_count // block_rows, block_rows, kv_count, repeat, head_dim)
    seg_blocks = segment.reshape(-1, block_rows)
    index_blocks = dealt_index.reshape(-1, block_rows)

    def one_block(pieces):
        query_block, seg_query, index_query = pieces
        scores = jnp.einsum('qgrd,kgd->grqk', query_block, key_rows, precision=lax.Precision.HIGHEST) * score_scale
        scores = low_back(scores)
        allowed = (seg_query[:, None] == segment[None, :]) & (index_query[:, None] >= dealt_index[None, :])
        scores = jnp.where(allowed[None, None], scores, MASKED)
        highest = lax.optimization_barrier(jnp.max(scores, axis=-1, keepdims=True))
        exp_scores = jnp.exp(scores - highest)
        probability = low(exp_scores / lax.optimization_barrier(jnp.sum(exp_scores, axis=-1, keepdims=True)))
        return jnp.einsum('grqk,kgd->qgrd', probability, value_rows, precision=lax.Precision.HIGHEST)
    out_blocks = lax.map(jax.checkpoint(one_block), (grouped, seg_blocks, index_blocks))
    return out_blocks.reshape(token_count, heads_all * head_dim)

def group_forward(group_tokens, weight_set, dealt_order, lengths_row):
    attn_gain, w_query, w_key, w_value, query_gain, key_gain, w_out, ffn_gain, w_gate, w_up, w_down = weight_set
    token_count = group_tokens.shape[0]
    head_dim = query_gain.shape[0]
    segment, dealt_index, places = layout(lengths_row, token_count)
    inverse = jnp.zeros((token_count,), jnp.int32).at[dealt_order].set(dealt_index)
    dealt_rows = jnp.take(group_tokens, dealt_order, axis=0)
    normed = low(rms_norm(dealt_rows, attn_gain))
    q_raw = low_back(matmul(normed, w_query))
    k_raw = low_back(matmul(normed, w_key))
    value_rows = low_back(low(matmul(normed, w_value)))
    queries = q_raw.reshape(token_count, -1, head_dim)
    queries = low_back(low(rotary(rms_norm(queries, query_gain), places)))
    key_rows = k_raw.reshape(token_count, -1, head_dim)
    key_rows = low_back(low(rotary(rms_norm(key_rows, key_gain), places)))
    value_rows = value_rows.reshape(token_count, -1, head_dim)
    attended = low_back(low(attend(queries, key_rows, value_rows, segment, dealt_index)))
    middle = dealt_rows + low_back(matmul(attended, w_out))
    normed_ffn = low(rms_norm(middle, ffn_gain))
    gate_proj = low_back(matmul(normed_ffn, w_gate))
    up_proj = low_back(matmul(normed_ffn, w_up))
    hidden = low(jax.nn.silu(gate_proj) * up_proj)
    result = middle + matmul(hidden, w_down)
    return jnp.take(result, inverse, axis=0)

def reference(tokens, order, seq_lengths, attn_gain, w_query, w_key, w_value, query_gain, key_gain, w_out, ffn_gain, w_gate, w_up, w_down, cotangent):
    weight_set = tuple((weight_arg.astype(jnp.float32) for weight_arg in (attn_gain, w_query, w_key, w_value, query_gain, key_gain, w_out, ffn_gain, w_gate, w_up, w_down)))
    inputs = tokens.astype(jnp.float32)

    def forward(all_tokens, weights_in):

        def per_group(pieces):
            return jax.checkpoint(group_forward)(pieces[0], weights_in, pieces[1], pieces[2])
        return lax.map(per_group, (all_tokens, order, seq_lengths))
    outputs, pull_back = jax.vjp(forward, inputs, weight_set)
    d_inputs, d_weights = pull_back(cotangent.astype(jnp.float32))
    return (outputs.astype(jnp.bfloat16), d_inputs.astype(jnp.bfloat16), d_weights[0], d_weights[1], d_weights[2], d_weights[3], d_weights[4], d_weights[5], d_weights[6], d_weights[7], d_weights[8], d_weights[9], d_weights[10])
```

```python
import functools

import jax
import jax.numpy as jnp
from jax import lax
from jax.experimental import pallas as pl
from jax.experimental.pallas import tpu as pltpu
from jax.sharding import PartitionSpec as P

EPSILON = 1e-05
ROPE_BASE = 1000000.0
LOG2E = 1.4426950408889634
ROWS = 256
LANES = 128
F32 = jnp.float32
BF16 = jnp.bfloat16
VMEM_LIMIT = 58 * 1024 * 1024


def dot_nn(left, right):
    return jnp.dot(left, right, preferred_element_type=F32)


def dot_nt(left, right):
    return lax.dot_general(left, right, (((1,), (1,)), ((), ())), preferred_element_type=F32)


def dot_tn(left, right):
    return lax.dot_general(left, right, (((0,), (0,)), ((), ())), preferred_element_type=F32)


def vmem():
    return pl.BlockSpec(memory_space=pltpu.VMEM)


def smem():
    return pl.BlockSpec(memory_space=pltpu.SMEM)


def params():
    return pltpu.CompilerParams(vmem_limit_bytes=VMEM_LIMIT)


def lane_iota(rows, columns):
    return lax.broadcasted_iota(jnp.int32, (rows, columns), 1)


def row_iota(rows, columns):
    return lax.broadcasted_iota(jnp.int32, (rows, columns), 0)


def at_rows(block, rows=ROWS):
    return pl.ds(pl.multiple_of(block * rows, rows), rows)


def pair_ones(head_dim):
    return (
        row_iota(LANES, LANES) // head_dim == lane_iota(LANES, LANES) // head_dim
    ).astype(BF16)


def head_mean(values, ones, head_dim):
    high = values.astype(BF16)
    low = (values - high.astype(F32)).astype(BF16)
    return (dot_nn(high, ones) + dot_nn(low, ones)) * (1.0 / head_dim)


def turn(values, cosine, sine_up, sine_down, head_dim, sign=1.0):
    half = head_dim // 2
    up = pltpu.roll(values, LANES - half, 1) * sine_up
    down = pltpu.roll(values, half, 1) * sine_down
    return values * cosine + sign * (up + down)


def spread_heads(pair, group, head_dim, low_lanes):
    moved = pltpu.roll(pair, head_dim, 1)
    if group == 0:
        return jnp.where(low_lanes, pair, 0.0), jnp.where(low_lanes, moved, 0.0)
    return jnp.where(low_lanes, 0.0, moved), jnp.where(low_lanes, 0.0, pair)


def qkv_kernel(
    head_dim, x_ref, w_ref, gain_ref, ocol_ref, cos_ref, su_ref, sd_ref, qg_ref, kg_ref,
    normed_ref, qx_ref, k_ref, v_ref, kt_ref, vt_ref, rawq_ref, rawk_ref, raw_ref,
):
    all_rows = x_ref.shape[0]
    width = raw_ref.shape[1]
    blocks = all_rows // ROWS
    pairs = rawq_ref.shape[1] // LANES

    def project(i, carry):
        rows = at_rows(i)
        x = x_ref[rows, :].astype(F32)
        r1 = lax.rsqrt(jnp.mean(x * x, axis=1, keepdims=True) + EPSILON)
        normed = (x * r1 * gain_ref[...]).astype(BF16)
        normed_ref[rows, :] = normed
        raw_ref[rows, :] = dot_nn(normed, w_ref[:, :width]).astype(BF16)
        return carry

    lax.fori_loop(0, blocks, project, 0)
    ones = pair_ones(head_dim)
    low_lanes = lane_iota(ROWS, LANES) < head_dim

    def deal(i, carry):
        rows = at_rows(i)
        pick = (ocol_ref[rows, :] == lane_iota(ROWS, all_rows)).astype(F32).astype(BF16)
        dealt = dot_nn(pick, raw_ref[...])
        cosine, su, sd = cos_ref[rows, :], su_ref[rows, :], sd_ref[rows, :]
        for g in range(pairs):
            raw = dealt[:, g * LANES:(g + 1) * LANES]
            rawq_ref[rows, g * LANES:(g + 1) * LANES] = raw.astype(BF16)
            rq = lax.rsqrt(head_mean(raw * raw, ones, head_dim) + EPSILON)
            pair = turn(raw * rq * qg_ref[...], cosine, su, sd, head_dim)
            for r, one in enumerate(spread_heads(pair, g, head_dim, low_lanes)):
                qx_ref[2 * g + r, rows, :] = one.astype(BF16)
        raw = dealt[:, pairs * LANES:(pairs + 1) * LANES]
        rawk_ref[rows, :] = raw.astype(BF16)
        rk = lax.rsqrt(head_mean(raw * raw, ones, head_dim) + EPSILON)
        keys = turn(raw * rk * kg_ref[...], cosine, su, sd, head_dim)
        k_ref[rows, :] = keys.astype(BF16)
        kt_ref[:, rows] = jnp.transpose(keys).astype(BF16)
        values = dealt[:, (pairs + 1) * LANES:]
        v_ref[rows, :] = values.astype(BF16)
        vt_ref[:, rows] = jnp.transpose(values).astype(BF16)
        return carry

    lax.fori_loop(0, blocks, deal, 0)


def qkv(x, w, gain, ocol, cosine, su, sd, qg, kg, head_dim):
    all_rows, width = x.shape
    out = lambda *dims: jax.ShapeDtypeStruct(dims, BF16)
    return pl.pallas_call(
        functools.partial(qkv_kernel, head_dim),
        out_shape=(
            out(all_rows, width), out(4, all_rows, LANES), out(all_rows, LANES), out(all_rows, LANES),
            out(LANES, all_rows), out(LANES, all_rows), out(all_rows, 2 * LANES), out(all_rows, LANES),
        ),
        in_specs=[vmem()] * 9,
        out_specs=(vmem(),) * 8,
        scratch_shapes=[pltpu.VMEM((all_rows, 4 * LANES), BF16)],
        compiler_params=params(),
        cost_estimate=pl.CostEstimate(flops=2 * all_rows * (width + all_rows) * 512, bytes_accessed=16 << 20, transcendentals=0),
        name="qkv",
    )(x, w, gain, ocol, cosine, su, sd, qg, kg)


def row_starts(lens_ref, index):
    start = jnp.zeros_like(index)
    end = lens_ref[0, 0]
    for s in range(1, lens_ref.shape[1]):
        start = jnp.where(index >= end, end, start)
        end = end + lens_ref[0, s]
    return start


def attend_kernel(head_dim, group, lens_ref, orow_ref, qx_ref, k_ref, vt_ref, given_ref, dealt_ref, lse_ref):
    all_rows = k_ref.shape[0]
    blocks = all_rows // ROWS
    scale = LOG2E * head_dim ** -0.5

    def query_block(i, carry):
        rows = at_rows(i)
        q_index = i * ROWS + lane_iota(1, ROWS)
        start = row_starts(lens_ref, q_index)
        first = row_starts(lens_ref, i * ROWS) // ROWS
        queries = [qx_ref[r, rows, :] for r in range(2)]

        def step(j, state):
            columns = at_rows(j)
            k_index = j * ROWS + row_iota(ROWS, ROWS)
            keep = (k_index <= q_index) & (k_index >= start)
            keys = k_ref[columns, :]
            values = vt_ref[group * head_dim:(group + 1) * head_dim, columns]
            new = []
            for r in range(2):
                total, mass = state[2 * r], state[2 * r + 1]
                weights = jnp.where(keep, jnp.exp2(dot_nt(keys, queries[r]) * scale), 0.0)
                mass = mass + jnp.sum(weights, axis=0, keepdims=True)
                total = total + dot_nn(values, weights.astype(BF16))
                new += [total, mass]
            return tuple(new)

        zero = (jnp.zeros((head_dim, ROWS), F32), jnp.zeros((1, ROWS), F32)) * 2
        state = lax.fori_loop(first, i + 1, step, zero)
        pair = jnp.concatenate([state[0] / state[1], state[2] / state[3]], axis=0)
        dealt_ref[rows, :] = jnp.transpose(pair).astype(BF16)
        for r in range(2):
            lse_ref[r:r + 1, rows] = jnp.log2(state[2 * r + 1])
        return carry

    lax.fori_loop(0, blocks, query_block, 0)

    def undeal(i, carry):
        rows = at_rows(i)
        pick = (orow_ref[...] == i * ROWS + row_iota(ROWS, all_rows)).astype(F32).astype(BF16)
        given_ref[rows, :] = dot_nn(pick, dealt_ref[...]).astype(BF16)
        return carry

    lax.fori_loop(0, blocks, undeal, 0)


def attend(group, lens, orow, qx, k, vt, head_dim):
    all_rows = k.shape[0]
    whole = lambda *dims: pl.BlockSpec(dims, lambda i: (0,) * len(dims))
    return pl.pallas_call(
        functools.partial(attend_kernel, head_dim, group),
        grid=(1,),
        out_shape=(
            jax.ShapeDtypeStruct((all_rows, LANES), BF16),
            jax.ShapeDtypeStruct((all_rows, LANES), BF16),
            jax.ShapeDtypeStruct((2, all_rows), F32),
        ),
        in_specs=[
            smem(), whole(1, all_rows),
            pl.BlockSpec((2, all_rows, LANES), lambda i: (group, 0, 0)),
            whole(all_rows, LANES), whole(LANES, all_rows),
        ],
        out_specs=(whole(all_rows, LANES), whole(all_rows, LANES), whole(2, all_rows)),
        compiler_params=params(),
        cost_estimate=pl.CostEstimate(flops=12 << 30, bytes_accessed=4 << 20, transcendentals=5 << 20),
        name="attend",
    )(lens, orow, qx, k, vt)


def attend_back_kernel(
    head_dim, lens_ref, ocol_ref, orow_ref, qx_ref, k_ref, v_ref, kt_ref, lse0_ref, lse1_ref, o0_ref, o1_ref,
    d0_ref, d1_ref, d2_ref, d3_ref, rawq_ref, rawk_ref, cos_ref, su_ref, sd_ref, qg_ref, kg_ref, w_ref,
    grad_ref, gain_ref, n0_ref, n1_ref, n2_ref, n3_ref,
    dgiven_ref, dx_ref, delta_ref, dk_ref, dv_ref, draw_ref,
):
    all_rows = k_ref.shape[0]
    blocks = all_rows // ROWS
    exponent = LOG2E * head_dim ** -0.5
    scale = head_dim ** -0.5
    low_lanes = lane_iota(ROWS, LANES) < head_dim
    tok = d0_ref.shape[0]
    for d, ref in enumerate((d0_ref, d1_ref, d2_ref, d3_ref)):
        dgiven_ref[d * tok:(d + 1) * tok, :] = ref[...]
    dk_ref[...] = jnp.zeros_like(dk_ref)
    dv_ref[...] = jnp.zeros_like(dv_ref)
    gain_ref[...] = jnp.zeros_like(gain_ref)

    def deal(i, carry):
        rows = at_rows(i)
        pick = (ocol_ref[rows, :] == lane_iota(ROWS, all_rows)).astype(F32).astype(BF16)
        dealt = dot_nn(pick, dgiven_ref[...])
        for g, o_ref in enumerate((o0_ref, o1_ref)):
            pair = dealt[:, g * LANES:(g + 1) * LANES]
            for r, one in enumerate(spread_heads(pair, g, head_dim, low_lanes)):
                dx_ref[2 * g + r, rows, :] = one.astype(BF16)
            across = jnp.transpose(pair * o_ref[rows, :].astype(F32))
            for r in range(2):
                delta_ref[2 * g + r:2 * g + r + 1, rows] = jnp.sum(
                    across[r * head_dim:(r + 1) * head_dim], axis=0, keepdims=True
                )
        return carry

    lax.fori_loop(0, blocks, deal, 0)
    ones = pair_ones(head_dim)

    def query_block(i, carry):
        rows = at_rows(i)
        q_index = i * ROWS + lane_iota(1, ROWS)
        start = row_starts(lens_ref, q_index)
        first = row_starts(lens_ref, i * ROWS) // ROWS

        def step(j, state):
            columns = at_rows(j)
            k_index = j * ROWS + row_iota(ROWS, ROWS)
            keep = (k_index <= q_index) & (k_index >= start)
            keys = k_ref[columns, :]
            values = v_ref[columns, :]
            new = []
            dk, dv = dk_ref[columns, :], dv_ref[columns, :]
            for h in range(4):
                g = h // 2
                queries = qx_ref[h, rows, :]
                grads = dx_ref[h, rows, :]
                lse = (lse0_ref, lse1_ref)[g][h % 2:h % 2 + 1, rows]
                weights = jnp.where(keep, jnp.exp2(dot_nt(keys, queries) * exponent - lse), 0.0)
                d_weights = dot_nt(values, grads)
                d_scores = (weights * (d_weights - delta_ref[h:h + 1, rows])).astype(BF16)
                dv = dv + dot_nn(weights.astype(BF16), grads)
                dk = dk + dot_nn(d_scores, queries)
                new.append(state[h] + dot_nn(kt_ref[g * head_dim:(g + 1) * head_dim, columns], d_scores))
            dk_ref[columns, :] = dk
            dv_ref[columns, :] = dv
            return tuple(new)

        state = lax.fori_loop(first, i + 1, step, (jnp.zeros((head_dim, ROWS), F32),) * 4)
        cosine, su, sd = cos_ref[rows, :], su_ref[rows, :], sd_ref[rows, :]
        for g in range(2):
            pair = jnp.transpose(jnp.concatenate(state[2 * g:2 * g + 2], axis=0)) * scale
            lanes = slice(g * LANES, (g + 1) * LANES)
            draw, gain = norm_back(
                pair, rawq_ref[rows, lanes].astype(F32), qg_ref[...], cosine, su, sd, ones, head_dim
            )
            draw_ref[rows, lanes] = draw
            gain_ref[0:1, :] += gain
        return carry

    lax.fori_loop(0, blocks, query_block, 0)

    def key_block(i, carry):
        rows = at_rows(i)
        cosine, su, sd = cos_ref[rows, :], su_ref[rows, :], sd_ref[rows, :]
        draw, gain = norm_back(
            dk_ref[rows, :] * scale, rawk_ref[rows, :].astype(F32), kg_ref[...], cosine, su, sd, ones, head_dim
        )
        draw_ref[rows, 2 * LANES:3 * LANES] = draw
        draw_ref[rows, 3 * LANES:] = dv_ref[rows, :].astype(BF16)
        gain_ref[1:2, :] += gain
        return carry

    lax.fori_loop(0, blocks, key_block, 0)
    width = draw_ref.shape[1]
    for d, ref in enumerate((n0_ref, n1_ref, n2_ref, n3_ref)):

        def undeal(i, carry, d=d, ref=ref):
            rows = at_rows(d * (tok // ROWS) + i)
            pick = (
                (orow_ref[...] == d * tok + i * ROWS + row_iota(ROWS, all_rows)).astype(F32).astype(BF16)
            )
            grads = dot_nn(pick, draw_ref[...]).astype(BF16)
            grad_ref[rows, :] = grads
            ref[at_rows(i), :] = dot_nt(grads, w_ref[:, :width]).astype(BF16)
            return carry

        lax.fori_loop(0, tok // ROWS, undeal, 0)


def norm_back(pair, raw, gain, cosine, su, sd, ones, head_dim):
    pair = pair.astype(BF16).astype(F32)
    u = turn(pair, cosine, su, sd, head_dim, -1.0)
    r = lax.rsqrt(head_mean(raw * raw, ones, head_dim) + EPSILON)
    unit = raw * r
    scaled = u * gain
    draw = r * (scaled - unit * head_mean(scaled * unit, ones, head_dim))
    return draw.astype(BF16), jnp.sum(u * unit, axis=0, keepdims=True)


def attend_back(lens, ocol, orow, qx, k, v, kt, lses, dealts, grads, rawq, rawk, cosine, su, sd, qg, kg, w, head_dim):
    all_rows = k.shape[0]
    tok = grads[0].shape[0]
    width = w.shape[0]
    return pl.pallas_call(
        functools.partial(attend_back_kernel, head_dim),
        out_shape=(
            jax.ShapeDtypeStruct((all_rows, 4 * LANES), BF16),
            jax.ShapeDtypeStruct((2, LANES), F32),
        ) + (jax.ShapeDtypeStruct((tok, width), BF16),) * 4,
        in_specs=[smem()] + [vmem()] * 22,
        out_specs=(vmem(),) * 6,
        scratch_shapes=[
            pltpu.VMEM((all_rows, 2 * LANES), BF16),
            pltpu.VMEM((4, all_rows, LANES), BF16),
            pltpu.VMEM((4, all_rows), F32),
            pltpu.VMEM((all_rows, LANES), F32),
            pltpu.VMEM((all_rows, LANES), F32),
            pltpu.VMEM((all_rows, 4 * LANES), BF16),
        ],
        compiler_params=params(),
        cost_estimate=pl.CostEstimate(flops=40 << 30, bytes_accessed=12 << 20, transcendentals=10 << 20),
        name="attend_back",
    )(lens, ocol, orow, qx, k, v, kt, *lses, *dealts, *grads, rawq, rawk, cosine, su, sd, qg, kg, w)


def ffn_kernel(
    per, me_ref, *refs
):
    att = refs[:8]
    x_ref, cot_ref, wo_ref, gain_ref, wgu_ref, wd_ref = refs[8:14]
    nf_ref, hid_ref, dg_ref, du_ref, mid_ref = refs[14:19]
    dn_refs, bo_refs = refs[19:23], refs[23:27]
    i = pl.program_id(0)
    me = me_ref[0]
    hidden_units = hid_ref.shape[1]
    middle = x_ref[...].astype(F32)
    for d in range(4):
        block = jnp.concatenate([att[2 * d][...], att[2 * d + 1][...]], axis=1)
        middle = middle + dot_nn(block, wo_ref[at_rows(jnp.bitwise_xor(me, d), 2 * LANES), :])
    r2 = lax.rsqrt(jnp.mean(middle * middle, axis=1, keepdims=True) + EPSILON)
    nf = (middle * r2 * gain_ref[...]).astype(BF16)
    nf_ref[...] = nf
    wg, wu = wgu_ref[:, :hidden_units], wgu_ref[:, hidden_units:]
    gate = dot_nn(nf, wg)
    up = dot_nn(nf, wu)
    s = jax.nn.sigmoid(gate)
    silu = gate * s
    hidden = (silu * up).astype(BF16)
    hid_ref[...] = hidden
    d_hidden = dot_nt(cot_ref[...], wd_ref[...])
    d_gate = (d_hidden * up * s * (1.0 + gate * (1.0 - s))).astype(BF16)
    d_up = (d_hidden * silu).astype(BF16)
    dg_ref[...] = d_gate
    du_ref[...] = d_up
    dn = (dot_nt(d_gate, wg) + dot_nt(d_up, wu)).astype(BF16)
    bo = dot_nn(hidden, wd_ref[...]).astype(BF16)
    for d in range(4):

        @pl.when(i // per == d)
        def _(d=d):
            dn_refs[d][...] = dn
            bo_refs[d][...] = bo

    @pl.when(i < per)
    def _():
        mid_ref[...] = middle


def ffn(me, att, x, cot, wo, gain, wgu, wd, tok):
    all_rows, width = x.shape
    units = wd.shape[0]
    per = tok // ROWS
    steps = all_rows // ROWS
    fixed = lambda a: pl.BlockSpec(a.shape, lambda i: (0, 0), pipeline_mode=pl.Buffered(1))
    rows = lambda c: pl.BlockSpec((ROWS, c), lambda i: (i, 0))
    crossed = lambda d: pl.BlockSpec(
        (ROWS, LANES), lambda i: (jnp.bitwise_xor(i // per, d) * per + i % per, 0)
    )
    held = lambda d: pl.BlockSpec((ROWS, width), lambda i: (jnp.clip(i - d * per, 0, per - 1), 0))
    out = lambda r, c, t=BF16: jax.ShapeDtypeStruct((r, c), t)
    return pl.pallas_call(
        functools.partial(ffn_kernel, per),
        grid=(steps,),
        out_shape=(
            out(all_rows, width), out(all_rows, units), out(all_rows, units), out(all_rows, units),
            out(tok, width, F32),
        ) + (out(tok, width),) * 8,
        in_specs=[smem()] + [crossed(d) for d in range(4) for _ in range(2)]
        + [rows(width), rows(width), fixed(wo), fixed(gain), fixed(wgu), fixed(wd)],
        out_specs=(rows(width), rows(units), rows(units), rows(units), held(0))
        + tuple(held(d) for d in range(4)) * 2,
        compiler_params=params(),
        cost_estimate=pl.CostEstimate(flops=2 * all_rows * width * (width + 6 * units), bytes_accessed=50 << 20, transcendentals=0),
        name="ffn",
    )(me, *att, x, cot, wo, gain, wgu, wd)


def middle_kernel(me_ref, n0_ref, n1_ref, n2_ref, n3_ref, cot_ref, mid_ref, gain_ref, wo_ref,
                  dmid_ref, branch_ref, a0_ref, a1_ref, a2_ref, a3_ref):
    me = me_ref[0]
    middle = mid_ref[...]
    d_normed = (
        n0_ref[...].astype(F32) + n1_ref[...].astype(F32) + n2_ref[...].astype(F32) + n3_ref[...].astype(F32)
    )
    r2 = lax.rsqrt(jnp.mean(middle * middle, axis=1, keepdims=True) + EPSILON)
    scaled = d_normed * gain_ref[...]
    pull = jnp.mean(scaled * middle, axis=1, keepdims=True)
    d_middle = cot_ref[...].astype(F32) + r2 * scaled - middle * (r2 * r2 * r2 * pull)
    dmid_ref[...] = d_middle
    branch = d_middle.astype(BF16)
    branch_ref[...] = branch
    for d, ref in enumerate((a0_ref, a1_ref, a2_ref, a3_ref)):
        ref[...] = dot_nt(branch, wo_ref[at_rows(jnp.bitwise_xor(me, d), 2 * LANES), :]).astype(BF16)


def middle_back(me, parts, cot, middle, gain, wo):
    tok, width = middle.shape
    fixed = lambda a: pl.BlockSpec(a.shape, lambda i: (0, 0), pipeline_mode=pl.Buffered(1))
    rows = lambda c: pl.BlockSpec((ROWS, c), lambda i: (i, 0))
    out = lambda c, t: jax.ShapeDtypeStruct((tok, c), t)
    return pl.pallas_call(
        middle_kernel,
        grid=(tok // ROWS,),
        out_shape=(out(width, F32), out(width, BF16)) + (out(2 * LANES, BF16),) * 4,
        in_specs=[smem()] + [rows(width)] * 6 + [fixed(gain), fixed(wo)],
        out_specs=(rows(width), rows(width)) + (rows(2 * LANES),) * 4,
        compiler_params=params(),
        cost_estimate=pl.CostEstimate(flops=2 * tok * width * width, bytes_accessed=12 << 20, transcendentals=0),
        name="middle_back",
    )(me, *parts, cot, middle, gain, wo)


def swap(array, distance):
    return lax.ppermute(array, "seq", [(s, s ^ distance) for s in range(4)])


def gather_rows(block):
    half = block.shape[0] // 2
    one, two = swap(block, 1), swap(block, 2)
    return [block, one, two, swap(one[:half], 2), swap(two[half:], 1)]


def body(
    tokens, order, seq_lengths, attn_gain, w_query, w_key, w_value, query_gain, key_gain,
    w_out, ffn_gain, w_gate, w_up, w_down, cotangent,
):
    tok = tokens.shape[1]
    ways = lax.axis_size("seq")
    shards = lax.axis_size("shard")
    all_rows = tok * ways
    head_dim = query_gain.shape[0]
    me = lax.axis_index("seq")
    me_arr = me.astype(jnp.int32)[None]
    own = lambda a, axis: lax.dynamic_slice_in_dim(a, me * (a.shape[axis] // ways), a.shape[axis] // ways, axis)
    depth = w_gate.shape[0]
    units = w_gate.shape[1] // ways
    piece = units // shards

    gains = jnp.stack([attn_gain, ffn_gain], axis=1)
    w_first = jnp.concatenate(
        [own(w_query, 1), own(w_key, 1), own(w_value, 1), gains, jnp.zeros((depth, LANES - 2), BF16)], axis=1
    )
    w_qkv = lax.all_gather(w_first, "shard", axis=0, tiled=True)
    w_o = lax.all_gather(w_out, "shard", axis=0, tiled=True)
    cut = lambda w: own(w.reshape(depth, shards, ways, piece), 2).reshape(depth, units)
    w_gu = lax.all_gather(jnp.concatenate([cut(w_gate), cut(w_up)], axis=1), "shard", axis=0, tiled=True)
    w_d = lax.all_gather(own(w_down, 0), "shard", axis=0, tiled=True)
    first_cols = 4 * LANES
    gain_rows = jnp.transpose(w_qkv[:, first_cols:first_cols + 2]).astype(F32)
    gain_a, gain_f = gain_rows[0:1], gain_rows[1:2]

    dealt_index = jnp.arange(all_rows, dtype=jnp.int32)
    ends = jnp.cumsum(seq_lengths[0])
    start = jnp.zeros_like(dealt_index)
    for s in range(seq_lengths.shape[1] - 1):
        start = jnp.where(dealt_index >= ends[s], ends[s], start)
    places = (dealt_index - start).astype(F32)
    lane = jnp.arange(LANES, dtype=jnp.int32) % head_dim
    half = head_dim // 2
    frequency = ROPE_BASE ** (-2.0 * jnp.arange(half, dtype=F32) / head_dim)
    angles = places[:, None] * frequency[None, :]
    cosine = jnp.tile(jnp.cos(angles), (1, LANES // half))
    sine = jnp.tile(jnp.sin(angles), (1, LANES // half))
    sine_up = jnp.where(lane[None, :] < half, -sine, 0.0)
    sine_down = jnp.where(lane[None, :] < half, 0.0, sine)
    relative = jnp.bitwise_xor(order[0], me.astype(jnp.int32) * tok)
    ocol, orow = relative[:, None], relative[None, :]
    q_gain = jnp.tile(query_gain.astype(F32), LANES // head_dim)[None, :]
    k_gain = jnp.tile(key_gain.astype(F32), LANES // head_dim)[None, :]

    x_all = jnp.concatenate(gather_rows(tokens[0]), axis=0)
    normed, qx, k, v, kt, vt, rawq, rawk = qkv(
        x_all, w_qkv, gain_a, ocol, cosine, sine_up, sine_down, q_gain, k_gain, head_dim
    )
    cot = cotangent[0]
    cot_all = jnp.concatenate(gather_rows(cot), axis=0)

    att, dealts, lses = [], [], []
    for g in range(2):
        given, dealt, lse = attend(g, seq_lengths, orow, qx, k, vt, head_dim)
        att.append([given] + [swap(given, d) for d in (1, 2, 3)])
        dealts.append(dealt)
        lses.append(lse)
    att = [att[g][d] for d in range(4) for g in range(2)]

    nf, hidden, d_gate, d_up, middle, *blocks = ffn(
        me_arr, att, x_all, cot_all, w_o, gain_f, w_gu, w_d, tok
    )
    dn, bo = blocks[:4], blocks[4:]
    dn = [dn[0]] + [swap(dn[d], d) for d in (1, 2, 3)]
    rows_product = lambda a, b: dot_tn(a, b).astype(BF16)
    d_wd = lax.psum_scatter(rows_product(hidden, cot_all), "shard", scatter_dimension=0, tiled=True)
    d_wgu = lax.psum_scatter(
        jnp.concatenate([rows_product(nf, d_gate), rows_product(nf, d_up)], axis=1),
        "shard", scatter_dimension=0, tiled=True,
    )

    d_middle, branch, *d_att = middle_back(me_arr, dn, cot, middle, gain_f, w_o)
    d_att = [d_att[0]] + [swap(d_att[d], d) for d in (1, 2, 3)]
    bo = [bo[0]] + [swap(bo[d], d) for d in (1, 2, 3)]
    block_out = (middle + sum(b.astype(F32) for b in bo)).astype(BF16)
    att_own = jnp.concatenate(
        [att[2 * d + g][d * tok:(d + 1) * tok] for d in range(4) for g in range(2)], axis=1
    )
    d_wo = rows_product(att_own, branch).reshape(ways, 2 * LANES, -1)
    d_wo = jnp.take(d_wo, jnp.bitwise_xor(jnp.arange(ways), me), axis=0).reshape(ways * 2 * LANES, -1)
    d_wo = lax.psum_scatter(d_wo, "shard", scatter_dimension=0, tiled=True)

    grads, head_gains, *dm = attend_back(
        seq_lengths, ocol, orow, qx, k, v, kt, lses, dealts, d_att, rawq, rawk,
        cosine, sine_up, sine_down, q_gain, k_gain, w_qkv, head_dim,
    )
    dm = [dm[0]] + [swap(dm[d], d) for d in (1, 2, 3)]
    d_wqkv = lax.psum_scatter(rows_product(normed, grads), "shard", scatter_dimension=0, tiled=True)
    x = tokens[0].astype(F32)
    d_normed = sum(b.astype(F32) for b in dm)
    r1 = lax.rsqrt(jnp.mean(x * x, axis=1, keepdims=True) + EPSILON)
    scaled = d_normed * gain_a
    d_tokens = (
        d_middle + r1 * scaled - x * (r1 * r1 * r1 * jnp.mean(scaled * x, axis=1, keepdims=True))
    ).astype(BF16)

    def whole(part):
        return lax.all_gather(part, "seq", axis=0)

    d_wqkv = whole(d_wqkv)
    side = lambda a: jnp.moveaxis(a, 0, 1).reshape(depth, -1).astype(F32)
    d_wq, d_wk, d_wv = side(d_wqkv[:, :, :256]), side(d_wqkv[:, :, 256:384]), side(d_wqkv[:, :, 384:512])
    d_wgu = whole(d_wgu).reshape(ways, depth, 2, shards, piece)
    d_wgu = jnp.transpose(d_wgu, (2, 1, 3, 0, 4)).reshape(2, depth, -1).astype(F32)
    d_wd = whole(d_wd).reshape(-1, d_wd.shape[1]).astype(F32)
    d_wo_total = lax.psum(d_wo, "seq").astype(F32)
    dot_rows = lambda w, d: jnp.sum(w.astype(F32) * d, axis=1)
    d_attn_gain = (dot_rows(w_query, d_wq) + dot_rows(w_key, d_wk) + dot_rows(w_value, d_wv)) / attn_gain.astype(F32)
    d_ffn_gain = (dot_rows(w_gate, d_wgu[0]) + dot_rows(w_up, d_wgu[1])) / ffn_gain.astype(F32)
    head_gains = lax.psum(head_gains, ("seq", "shard"))
    head_gains = head_gains[:, :head_dim] + head_gains[:, head_dim:]
    return (
        block_out[None], d_tokens[None], d_attn_gain, d_wq, d_wk, d_wv, head_gains[0], head_gains[1],
        d_wo_total, d_ffn_gain, d_wgu[0], d_wgu[1], d_wd,
    )


def solution(mesh):
    rows, flat, wide = P("shard", None), P("shard"), P("shard", "seq", None)
    in_specs = (
        wide, rows, rows, flat, rows, rows, rows, P(), P(), rows, flat, rows, rows, rows, wide,
    )
    out_specs = (wide, wide, flat, rows, rows, rows, P(), P(), rows, flat, rows, rows, rows)
    return jax.shard_map(body, mesh=mesh, in_specs=in_specs, out_specs=out_specs, check_vma=False)
```

```python
import functools

import jax
import jax.numpy as jnp
from jax import lax
from jax.experimental import pallas as pl
from jax.experimental.pallas import tpu as pltpu
from jax.sharding import PartitionSpec as P

EPSILON = 1e-05
ROPE_BASE = 1000000.0
LOG2E = 1.4426950408889634
ROWS = 256
LANES = 128
F32 = jnp.float32
BF16 = jnp.bfloat16
COST = pl.CostEstimate(flops=1 << 20, bytes_accessed=1 << 16, transcendentals=0)
VMEM_LIMIT = 58 * 1024 * 1024


def dot_nn(left, right):
    return jnp.dot(left, right, preferred_element_type=F32)


def dot_nt(left, right):
    return lax.dot_general(left, right, (((1,), (1,)), ((), ())), preferred_element_type=F32)


def dot_tn(left, right):
    return lax.dot_general(left, right, (((0,), (0,)), ((), ())), preferred_element_type=F32)


def vmem():
    return pl.BlockSpec(memory_space=pltpu.VMEM)


def smem():
    return pl.BlockSpec(memory_space=pltpu.SMEM)


def params():
    return pltpu.CompilerParams(vmem_limit_bytes=VMEM_LIMIT)


def lane_iota(rows, columns):
    return lax.broadcasted_iota(jnp.int32, (rows, columns), 1)


def row_iota(rows, columns):
    return lax.broadcasted_iota(jnp.int32, (rows, columns), 0)


def at_rows(block, rows=ROWS):
    return pl.ds(pl.multiple_of(block * rows, rows), rows)


def pair_ones(head_dim):
    return (
        row_iota(LANES, LANES) // head_dim == lane_iota(LANES, LANES) // head_dim
    ).astype(BF16)


def head_mean(values, ones, head_dim):
    high = values.astype(BF16)
    low = (values - high.astype(F32)).astype(BF16)
    return (dot_nn(high, ones) + dot_nn(low, ones)) * (1.0 / head_dim)


def turn(values, cosine, sine_up, sine_down, head_dim, sign=1.0):
    half = head_dim // 2
    up = pltpu.roll(values, LANES - half, 1) * sine_up
    down = pltpu.roll(values, half, 1) * sine_down
    return values * cosine + sign * (up + down)


def spread_heads(pair, group, head_dim, low_lanes):
    moved = pltpu.roll(pair, head_dim, 1)
    if group == 0:
        return jnp.where(low_lanes, pair, 0.0), jnp.where(low_lanes, moved, 0.0)
    return jnp.where(low_lanes, 0.0, moved), jnp.where(low_lanes, 0.0, pair)


def first_kernel(me_ref, q_ref, k_ref, v_ref, ga_ref, gf_ref, out_ref):
    at = 0
    for ref in (q_ref, k_ref, v_ref):
        size = ref.shape[1] // 4
        out_ref[:, at:at + size] = ref[:, pl.ds(pl.multiple_of(me_ref[0] * size, size), size)]
        at += size
    depth = out_ref.shape[0]
    row = row_iota(LANES, depth)
    gains = jnp.where(row == 0, ga_ref[...].astype(F32), jnp.where(row == 1, gf_ref[...].astype(F32), 0.0))
    out_ref[:, at:] = jnp.transpose(gains).astype(BF16)


def first_weights(me, w_query, w_key, w_value, attn_gain, ffn_gain):
    depth = w_query.shape[0]
    width = (w_query.shape[1] + w_key.shape[1] + w_value.shape[1]) // 4 + LANES
    return pl.pallas_call(
        first_kernel,
        out_shape=jax.ShapeDtypeStruct((depth, width), BF16),
        in_specs=[smem()] + [vmem()] * 5,
        out_specs=vmem(),
        compiler_params=params(),
        cost_estimate=COST,
        name="first_weights",
    )(me, w_query, w_key, w_value, attn_gain[None], ffn_gain[None])


def qkv_kernel(
    head_dim, x0_ref, x1_ref, x2_ref, x3a_ref, x3b_ref, w_ref, ocol_ref, cos_ref, su_ref, sd_ref,
    qg_ref, kg_ref, normed_ref, qx_ref, k_ref, v_ref, vx_ref, kt_ref, rawq_ref, rawk_ref, gain_ref, raw_ref,
):
    i = pl.program_id(0)
    tok = x0_ref.shape[0]
    all_rows, width = raw_ref.shape
    pairs = rawq_ref.shape[1] // LANES

    @pl.when(i == 0)
    def _():
        gain_ref[...] = jnp.transpose(w_ref[:, width:].astype(F32))[:8]

    def project(x, rows):
        x = x.astype(F32)
        r1 = lax.rsqrt(jnp.mean(x * x, axis=1, keepdims=True) + EPSILON)
        normed = (x * r1 * gain_ref[0:1, :]).astype(BF16)
        normed_ref[...] = normed
        raw_ref[rows, :] = dot_nn(normed, w_ref[:, :width]).astype(BF16)

    for d, refs in enumerate(((x0_ref,), (x1_ref,), (x2_ref,), (x3a_ref, x3b_ref))):

        @pl.when(i == d)
        def _(d=d, refs=refs):
            project(jnp.concatenate([ref[...] for ref in refs], axis=1), slice(d * tok, (d + 1) * tok))

    @pl.when(i >= 4)
    def _():
        ones = pair_ones(head_dim)
        low_lanes = lane_iota(tok, LANES) < head_dim
        pick = (ocol_ref[...] == lane_iota(tok, all_rows)).astype(F32).astype(BF16)
        dealt = dot_nn(pick, raw_ref[...])
        cosine, su, sd = cos_ref[...], su_ref[...], sd_ref[...]
        for g in range(pairs):
            raw = dealt[:, g * LANES:(g + 1) * LANES]
            rawq_ref[:, g * LANES:(g + 1) * LANES] = raw.astype(BF16)
            rq = lax.rsqrt(head_mean(raw * raw, ones, head_dim) + EPSILON)
            pair = turn(raw * rq * qg_ref[...], cosine, su, sd, head_dim)
            for r, one in enumerate(spread_heads(pair, g, head_dim, low_lanes)):
                qx_ref[2 * g + r] = one.astype(BF16)
        raw = dealt[:, pairs * LANES:(pairs + 1) * LANES]
        rawk_ref[...] = raw.astype(BF16)
        rk = lax.rsqrt(head_mean(raw * raw, ones, head_dim) + EPSILON)
        keys = turn(raw * rk * kg_ref[...], cosine, su, sd, head_dim)
        k_ref[...] = keys.astype(BF16)
        kt_ref[...] = jnp.transpose(keys).astype(BF16)
        values = dealt[:, (pairs + 1) * LANES:]
        v_ref[...] = values.astype(BF16)
        vx_ref[0] = jnp.where(low_lanes, values, 1.0).astype(BF16)
        vx_ref[1] = jnp.where(low_lanes, 1.0, values).astype(BF16)


def fixed(array):
    return pl.BlockSpec(array.shape, lambda i: (0,) * array.ndim, pipeline_mode=pl.Buffered(1))


def qkv(xs, w, ocol, cosine, su, sd, qg, kg, head_dim):
    tok, width = xs[0].shape
    all_rows = 4 * tok
    out = lambda *dims: jax.ShapeDtypeStruct(dims, BF16)
    late = lambda c: pl.BlockSpec((tok, c), lambda i: (jnp.maximum(i - 4, 0), 0))
    heads = lambda n: pl.BlockSpec((n, tok, LANES), lambda i: (0, jnp.maximum(i - 4, 0), 0))
    return pl.pallas_call(
        functools.partial(qkv_kernel, head_dim),
        grid=(8,),
        out_shape=(
            out(all_rows, width), out(4, all_rows, LANES), out(all_rows, LANES), out(all_rows, LANES),
            out(2, all_rows, LANES), out(LANES, all_rows), out(all_rows, 2 * LANES), out(all_rows, LANES),
            jax.ShapeDtypeStruct((8, width), F32),
        ),
        in_specs=[fixed(x) for x in xs] + [fixed(w), late(1)] + [late(LANES)] * 3 + [fixed(qg), fixed(kg)],
        out_specs=(
            pl.BlockSpec((tok, width), lambda i: (jnp.minimum(i, 3), 0)),
            heads(4), late(LANES), late(LANES), heads(2),
            pl.BlockSpec((LANES, tok), lambda i: (0, jnp.maximum(i - 4, 0))), late(2 * LANES), late(LANES),
            pl.BlockSpec((8, width), lambda i: (0, 0)),
        ),
        scratch_shapes=[pltpu.VMEM((all_rows, 4 * LANES), BF16)],
        compiler_params=params(),
        cost_estimate=COST,
        name="qkv",
    )(*xs, w, ocol, cosine, su, sd, qg, kg)


def row_starts(lens_ref, index):
    start = jnp.zeros_like(index)
    end = lens_ref[0, 0]
    for s in range(1, lens_ref.shape[1]):
        start = jnp.where(index >= end, end, start)
        end = end + lens_ref[0, s]
    return start


def attend_kernel(head_dim, group, block, lens_ref, orow_ref, qx_ref, k_ref, vx_ref, *refs):
    given_ref, dealt_ref, lse_ref = refs[-3:]
    all_rows = k_ref.shape[0]
    scale = LOG2E * head_dim ** -0.5
    low_lanes = lane_iota(block, LANES) < head_dim
    mass_row = head_dim if group == 0 else 0

    def query_block(i, carry):
        rows = at_rows(i, block)
        q_index = i * block + row_iota(block, 1)
        start = row_starts(lens_ref, q_index)
        first = row_starts(lens_ref, i * block) // block
        clear = jnp.minimum((row_starts(lens_ref, i * block + block - 1) + block - 1) // block, i)
        queries = [qx_ref[r, rows, :] for r in range(2)]

        def step(j, state, masked):
            columns = at_rows(j, block)
            keys, values = k_ref[columns, :], vx_ref[0, columns, :]
            k_index = j * block + lane_iota(block, block)
            keep = (k_index <= q_index) & (k_index >= start)
            new = []
            for r in range(2):
                weights = jnp.exp2(dot_nt(queries[r], keys) * scale)
                if masked:
                    weights = jnp.where(keep, weights, 0.0)
                new.append(state[r] + dot_nn(weights.astype(BF16), values))
            return tuple(new)

        state = (jnp.zeros((block, LANES), F32),) * 2
        state = lax.fori_loop(first, clear, functools.partial(step, masked=True), state)
        state = lax.fori_loop(clear, i, functools.partial(step, masked=False), state)
        state = step(i, state, True)
        out = []
        for r in range(2):
            lse_ref[r:r + 1, rows] = jnp.log2(jnp.transpose(state[r])[mass_row:mass_row + 1, :])
            out.append(state[r] / pltpu.roll(state[r], head_dim, 1))
        if group == 0:
            pair = jnp.where(low_lanes, out[0], pltpu.roll(out[1], head_dim, 1))
        else:
            pair = jnp.where(low_lanes, pltpu.roll(out[0], head_dim, 1), out[1])
        dealt_ref[rows, :] = pair.astype(BF16)
        return carry

    lax.fori_loop(0, all_rows // block, query_block, 0)

    def undeal(i, carry):
        rows = at_rows(i, block)
        pick = (orow_ref[...] == i * block + row_iota(block, all_rows)).astype(F32).astype(BF16)
        given_ref[rows, :] = dot_nn(pick, dealt_ref[...]).astype(BF16)
        return carry

    lax.fori_loop(0, all_rows // block, undeal, 0)


def attend(group, lens, orow, qx, k, vx, head_dim, after):
    all_rows = k.shape[0]
    whole = lambda *dims: pl.BlockSpec(dims, lambda i: (0,) * len(dims))
    return pl.pallas_call(
        functools.partial(attend_kernel, head_dim, group, all_rows // 4),
        grid=(1,),
        out_shape=(
            jax.ShapeDtypeStruct((all_rows, LANES), BF16),
            jax.ShapeDtypeStruct((all_rows, LANES), BF16),
            jax.ShapeDtypeStruct((2, all_rows), F32),
        ),
        in_specs=[
            smem(), whole(1, all_rows),
            pl.BlockSpec((2, all_rows, LANES), lambda i: (group, 0, 0)),
            whole(all_rows, LANES),
            pl.BlockSpec((1, all_rows, LANES), lambda i: (group, 0, 0)),
        ] + anywhere(after),
        out_specs=(whole(all_rows, LANES), whole(all_rows, LANES), whole(2, all_rows)),
        compiler_params=params(),
        cost_estimate=COST,
        name="attend",
    )(lens, orow, qx, k, vx, *after)


def attend_back_kernel(head_dim, *refs):
    (lens_ref, ocol_ref, qx_ref, k_ref, v_ref, kt_ref, lse0_ref, lse1_ref, o0_ref, o1_ref,
     d0_ref, d1_ref, d2_ref, d3_ref, rawq_ref, rawk_ref, cos_ref, su_ref, sd_ref, qg_ref, kg_ref) = refs[:21]
    draw_ref, gain_ref, dgiven_ref, dx_ref, delta_ref, dk_ref, dv_ref = refs[-7:]
    all_rows = k_ref.shape[0]
    blocks = all_rows // ROWS
    exponent = LOG2E * head_dim ** -0.5
    scale = head_dim ** -0.5
    low_lanes = lane_iota(ROWS, LANES) < head_dim
    tok = d0_ref.shape[0]
    for d, ref in enumerate((d0_ref, d1_ref, d2_ref, d3_ref)):
        dgiven_ref[d * tok:(d + 1) * tok, :] = ref[...]
    dk_ref[...] = jnp.zeros_like(dk_ref)
    dv_ref[...] = jnp.zeros_like(dv_ref)
    gain_ref[...] = jnp.zeros_like(gain_ref)

    def deal(i, carry):
        rows = at_rows(i)
        pick = (ocol_ref[rows, :] == lane_iota(ROWS, all_rows)).astype(F32).astype(BF16)
        dealt = dot_nn(pick, dgiven_ref[...])
        for g, o_ref in enumerate((o0_ref, o1_ref)):
            pair = dealt[:, g * LANES:(g + 1) * LANES]
            for r, one in enumerate(spread_heads(pair, g, head_dim, low_lanes)):
                dx_ref[2 * g + r, rows, :] = one.astype(BF16)
            across = jnp.transpose(pair * o_ref[rows, :].astype(F32))
            for r in range(2):
                delta_ref[2 * g + r:2 * g + r + 1, rows] = jnp.sum(
                    across[r * head_dim:(r + 1) * head_dim], axis=0, keepdims=True
                )
        return carry

    lax.fori_loop(0, blocks, deal, 0)
    ones = pair_ones(head_dim)

    def query_block(i, carry):
        rows = at_rows(i)
        q_index = i * ROWS + lane_iota(1, ROWS)
        start = row_starts(lens_ref, q_index)
        first = row_starts(lens_ref, i * ROWS) // ROWS

        def step(j, state):
            columns = at_rows(j)
            k_index = j * ROWS + row_iota(ROWS, ROWS)
            keep = (k_index <= q_index) & (k_index >= start)
            keys = k_ref[columns, :]
            values = v_ref[columns, :]
            new = []
            dk, dv = dk_ref[columns, :], dv_ref[columns, :]
            for h in range(4):
                g = h // 2
                queries = qx_ref[h, rows, :]
                grads = dx_ref[h, rows, :]
                lse = (lse0_ref, lse1_ref)[g][h % 2:h % 2 + 1, rows]
                weights = jnp.where(keep, jnp.exp2(dot_nt(keys, queries) * exponent - lse), 0.0)
                d_weights = dot_nt(values, grads)
                d_scores = (weights * (d_weights - delta_ref[h:h + 1, rows])).astype(BF16)
                dv = dv + dot_nn(weights.astype(BF16), grads)
                dk = dk + dot_nn(d_scores, queries)
                new.append(state[h] + dot_nn(kt_ref[g * head_dim:(g + 1) * head_dim, columns], d_scores))
            dk_ref[columns, :] = dk
            dv_ref[columns, :] = dv
            return tuple(new)

        state = lax.fori_loop(first, i + 1, step, (jnp.zeros((head_dim, ROWS), F32),) * 4)
        cosine, su, sd = cos_ref[rows, :], su_ref[rows, :], sd_ref[rows, :]
        for g in range(2):
            pair = jnp.transpose(jnp.concatenate(state[2 * g:2 * g + 2], axis=0)) * scale
            lanes = slice(g * LANES, (g + 1) * LANES)
            draw, gain = norm_back(
                pair, rawq_ref[rows, lanes].astype(F32), qg_ref[...], cosine, su, sd, ones, head_dim
            )
            draw_ref[rows, lanes] = draw
            gain_ref[0:1, :] += gain
        return carry

    lax.fori_loop(0, blocks, query_block, 0)

    def key_block(i, carry):
        rows = at_rows(i)
        cosine, su, sd = cos_ref[rows, :], su_ref[rows, :], sd_ref[rows, :]
        draw, gain = norm_back(
            dk_ref[rows, :] * scale, rawk_ref[rows, :].astype(F32), kg_ref[...], cosine, su, sd, ones, head_dim
        )
        draw_ref[rows, 2 * LANES:3 * LANES] = draw
        draw_ref[rows, 3 * LANES:] = dv_ref[rows, :].astype(BF16)
        gain_ref[1:2, :] += gain
        return carry

    lax.fori_loop(0, blocks, key_block, 0)


def rows_back_kernel(orow_ref, draw_ref, *refs):
    grad_ref, refs = refs[-5], refs[-4:]
    i = pl.program_id(0)
    all_rows = draw_ref.shape[0]
    rows = grad_ref.shape[0]
    pick = (orow_ref[...] == i * rows + row_iota(rows, all_rows)).astype(F32).astype(BF16)
    grads = dot_nn(pick, draw_ref[...]).astype(BF16)
    grad_ref[...] = grads
    for d, ref in enumerate(refs):

        @pl.when(i == d)
        def _(ref=ref):
            ref[...] = grads


def norm_back(pair, raw, gain, cosine, su, sd, ones, head_dim):
    pair = pair.astype(BF16).astype(F32)
    u = turn(pair, cosine, su, sd, head_dim, -1.0)
    r = lax.rsqrt(head_mean(raw * raw, ones, head_dim) + EPSILON)
    unit = raw * r
    scaled = u * gain
    draw = r * (scaled - unit * head_mean(scaled * unit, ones, head_dim))
    return draw.astype(BF16), jnp.sum(u * unit, axis=0, keepdims=True)


def anywhere(arrays):
    return [pl.BlockSpec(memory_space=pl.ANY)] * len(arrays)


def attend_back(lens, ocol, qx, k, v, kt, lses, dealts, grads, rawq, rawk, cosine, su, sd, qg, kg, head_dim, after):
    all_rows = k.shape[0]
    return pl.pallas_call(
        functools.partial(attend_back_kernel, head_dim),
        out_shape=(
            jax.ShapeDtypeStruct((all_rows, 4 * LANES), BF16),
            jax.ShapeDtypeStruct((2, LANES), F32),
        ),
        in_specs=[smem()] + [vmem()] * 20 + anywhere(after),
        out_specs=(vmem(),) * 2,
        scratch_shapes=[
            pltpu.VMEM((all_rows, 2 * LANES), BF16),
            pltpu.VMEM((4, all_rows, LANES), BF16),
            pltpu.VMEM((4, all_rows), F32),
            pltpu.VMEM((all_rows, LANES), F32),
            pltpu.VMEM((all_rows, LANES), F32),
        ],
        compiler_params=params(),
        cost_estimate=COST,
        name="attend_back",
    )(lens, ocol, qx, k, v, kt, *lses, *dealts, *grads, rawq, rawk, cosine, su, sd, qg, kg, *after)


def rows_back(orow, draw, after):
    all_rows, width = draw.shape
    tok = all_rows // 4
    block = pl.BlockSpec((tok, width), lambda i: (i, 0))
    return pl.pallas_call(
        rows_back_kernel,
        grid=(4,),
        out_shape=(jax.ShapeDtypeStruct(draw.shape, BF16),) + (jax.ShapeDtypeStruct((tok, width), BF16),) * 4,
        in_specs=[fixed(orow), fixed(draw)] + anywhere(after),
        out_specs=(block,) + (pl.BlockSpec((tok, width), lambda i: (0, 0)),) * 4,
        compiler_params=params(),
        cost_estimate=COST,
        name="rows_back",
    )(orow, draw, *after)


def tokens_kernel(me_ref, g0_ref, g1_ref, g2_ref, g3_ref, w_ref, x_ref, mid_ref, gain_ref, *refs):
    out_ref = refs[-1]
    me = me_ref[0]
    d_normed = jnp.zeros(x_ref.shape, F32)
    span, width = 2 * LANES, 8 * LANES
    for d, ref in enumerate((g0_ref, g1_ref, g2_ref, g3_ref)):
        other = jnp.bitwise_xor(me, d)
        take = lambda at, size: w_ref[:, pl.ds(pl.multiple_of(at + other * size, size), size)]
        weights = jnp.concatenate([take(0, span), take(width, LANES), take(width + 4 * LANES, LANES)], axis=1)
        d_normed = d_normed + dot_nt(ref[...], weights)
    x = x_ref[...].astype(F32)
    r1 = lax.rsqrt(jnp.mean(x * x, axis=1, keepdims=True) + EPSILON)
    scaled = d_normed * gain_ref[...]
    pull = jnp.mean(scaled * x, axis=1, keepdims=True)
    out_ref[...] = (mid_ref[...] + r1 * scaled - x * (r1 * r1 * r1 * pull)).astype(BF16)


def tokens_back(me, grads, w, x, d_middle, gain, after):
    tok, width = x.shape
    rows = lambda c: pl.BlockSpec((ROWS, c), lambda i: (i, 0))
    return pl.pallas_call(
        tokens_kernel,
        grid=(tok // ROWS,),
        out_shape=jax.ShapeDtypeStruct((tok, width), BF16),
        in_specs=[smem()] + [rows(grads[0].shape[1])] * 4 + [fixed(w), rows(width), rows(width), fixed(gain)] + anywhere(after),
        out_specs=rows(width),
        compiler_params=params(),
        cost_estimate=COST,
        name="tokens_back",
    )(me, *grads, w, x, d_middle, gain, *after)


def ffn_kernel(per, blocks, n_carried, *refs):
    me_ref, att, refs = refs[0], refs[1:9], list(refs[9:])
    take = lambda n: [refs.pop(0) for _ in range(n)]
    xs = [take(2 if d == 3 else 1) for d in blocks]
    cots = [take(2 if d == 3 else 1) for d in blocks]
    wo_ref, gain_ref, wgu_ref, wd_ref = take(4)
    diag = take(2) if blocks == (1, 2) else None
    take(n_carried)
    nf_ref, hid_ref, dgu_ref, cot_ref = take(4)
    i = pl.program_id(0)
    me = me_ref[0]
    hidden_units = hid_ref.shape[1]
    which = i // per

    def read(lists):
        parts = [jnp.concatenate([ref[...] for ref in one], axis=1) for one in lists]
        return parts[0] if len(parts) == 1 else jnp.where(which == 0, parts[0], parts[1])

    middle = read(xs).astype(F32)
    for d in range(4):
        block = jnp.concatenate([att[2 * d][...], att[2 * d + 1][...]], axis=1)
        middle = middle + dot_nn(block, wo_ref[at_rows(jnp.bitwise_xor(me, d), 2 * LANES), :])
    r2 = lax.rsqrt(jnp.mean(middle * middle, axis=1, keepdims=True) + EPSILON)
    nf = (middle * r2 * gain_ref[...]).astype(BF16)
    nf_ref[...] = nf
    cot = read(cots)
    cot_ref[...] = cot
    wg, wu = wgu_ref[:, :hidden_units], wgu_ref[:, hidden_units:]
    gate = dot_nn(nf, wg)
    up = dot_nn(nf, wu)
    s = jax.nn.sigmoid(gate)
    silu = gate * s
    hidden = (silu * up).astype(BF16)
    hid_ref[...] = hidden
    d_hidden = dot_nt(cot, wd_ref[...])
    d_gate = (d_hidden * up * s * (1.0 + gate * (1.0 - s))).astype(BF16)
    d_up = (d_hidden * silu).astype(BF16)
    dgu_ref[:, :hidden_units] = d_gate
    dgu_ref[:, hidden_units:] = d_up
    dn = dot_nt(d_gate, wg) + dot_nt(d_up, wu)
    bo = dot_nn(hidden, wd_ref[...])
    half = dn.shape[1] // 2
    if blocks == (3,):
        dna_ref, dnb_ref, bo_ref = take(3)
        dna_ref[...] = dn[:, :half].astype(BF16)
        dnb_ref[...] = dn[:, half:].astype(BF16)
        bo_ref[...] = bo.astype(BF16)
    elif blocks == (0,):
        dn_ref, bo_ref, mid_ref = take(3)
        dn_ref[...] = dn.astype(BF16)
        bo_ref[...] = bo.astype(BF16)
        mid_ref[...] = middle
    else:
        dn1_ref, dn2_ref, bo1_ref, bo2_ref = take(4)

        @pl.when(which == 0)
        def _():
            dn1_ref[:, :half] = dn[:, :half].astype(BF16)
            dn1_ref[:, half:] = (dn[:, half:] + diag[1][...].astype(F32)).astype(BF16)
            bo1_ref[...] = bo.astype(BF16)

        @pl.when(which == 1)
        def _():
            dn2_ref[:, :half] = (dn[:, :half] + diag[0][...].astype(F32)).astype(BF16)
            dn2_ref[:, half:] = dn[:, half:].astype(BF16)
            bo2_ref[...] = bo.astype(BF16)


def ffn(me, blocks, att, xs, cots, wo, gain, wgu, wd, diag, carried):
    all_rows = att[0].shape[0]
    width, units = wo.shape[1], wd.shape[0]
    tok = all_rows // 4
    per = tok // ROWS
    block_of = lambda i: blocks[0] + (i // per) * (blocks[-1] - blocks[0])
    everywhere = lambda c: pl.BlockSpec((ROWS, c), lambda i: (block_of(i) * per + i % per, 0))
    crossed = lambda d: pl.BlockSpec(
        (ROWS, LANES), lambda i: (jnp.bitwise_xor(block_of(i), d) * per + i % per, 0)
    )
    held = lambda n, c: pl.BlockSpec((ROWS, c), lambda i: (jnp.clip(i - n * per, 0, per - 1), 0))
    out = lambda r, c, t=BF16: jax.ShapeDtypeStruct((r, c), t)
    pieces = lambda arrays: [held(n, a.shape[1]) for n, d in enumerate(blocks) for a in arrays[d]]
    shapes = [out(all_rows, width), out(all_rows, units), out(all_rows, 2 * units), out(all_rows, width)]
    specs = [everywhere(width), everywhere(units), everywhere(2 * units), everywhere(width)]
    if blocks == (3,):
        shapes += [out(tok, width // 2)] * 2 + [out(tok, width)]
        specs += [held(0, width // 2)] * 2 + [held(0, width)]
    elif blocks == (0,):
        shapes += [out(tok, width)] * 2 + [out(tok, width, F32)]
        specs += [held(0, width)] * 3
    else:
        shapes += [out(tok, width)] * 4
        specs += [held(0, width), held(1, width)] * 2
    diag_specs = [held(1, width // 2), held(0, width // 2)] if diag else []
    operands = (
        [me] + list(att) + [a for d in blocks for a in xs[d]] + [a for d in blocks for a in cots[d]]
        + [wo, gain, wgu, wd] + list(diag) + list(carried)
    )
    first = len(operands) - len(carried)
    return pl.pallas_call(
        functools.partial(ffn_kernel, per, blocks, len(carried)),
        grid=(len(blocks) * per,),
        out_shape=tuple(shapes),
        in_specs=[smem()] + [crossed(d) for d in range(4) for _ in range(2)] + pieces(xs) + pieces(cots)
        + [fixed(wo), fixed(gain), fixed(wgu), fixed(wd)] + diag_specs + anywhere(carried),
        out_specs=tuple(specs),
        input_output_aliases={first + n: n for n in range(len(carried))},
        compiler_params=params(),
        cost_estimate=COST,
        name="ffn",
    )(*operands)


def weights_kernel(left_ref, right_ref, out_ref):
    out_ref[...] = dot_tn(left_ref[...], right_ref[...]).astype(BF16)


def weights_back(left, right, steps):
    rows, depth = left.shape
    return pl.pallas_call(
        weights_kernel,
        grid=(steps,),
        out_shape=jax.ShapeDtypeStruct((depth, right.shape[1]), BF16),
        in_specs=[pl.BlockSpec((rows, depth // steps), lambda i: (0, i)), fixed(right)],
        out_specs=pl.BlockSpec((depth // steps, right.shape[1]), lambda i: (i, 0)),
        compiler_params=params(),
        cost_estimate=COST,
        name="weights_back",
    )(left, right)


def last_kernel(period, normed_ref, grads_ref, o0_ref, o1_ref, o2_ref, o3_ref, gain_ref, out_ref):
    width, extra = grads_ref.shape[1], o0_ref.shape[1]
    out_ref[:, :width] = dot_tn(normed_ref[...], grads_ref[...]).astype(BF16)
    total = o0_ref[...].astype(F32)
    for ref in (o1_ref, o2_ref, o3_ref):
        total = total + ref[...].astype(F32)
    out_ref[:, width:width + extra] = total.astype(BF16)
    place = row_iota(out_ref.shape[0], LANES) % period
    gains = jnp.where(place == 0, gain_ref[0:1, :], jnp.where(place == 1, gain_ref[1:2, :], 0.0))
    out_ref[:, width + extra:] = gains.astype(BF16)


def last_weights(normed, grads, parts, gains, shards):
    rows, depth = normed.shape
    steps, extra = 4, parts[0].shape[1]
    block = lambda c: pl.BlockSpec((depth // steps, c), lambda i: (i, 0))
    return pl.pallas_call(
        functools.partial(last_kernel, depth // shards),
        grid=(steps,),
        out_shape=jax.ShapeDtypeStruct((depth, grads.shape[1] + extra + LANES), BF16),
        in_specs=[pl.BlockSpec((rows, depth // steps), lambda i: (0, i)), fixed(grads)] + [block(extra)] * 4 + [fixed(gains)],
        out_specs=block(grads.shape[1] + extra + LANES),
        compiler_params=params(),
        cost_estimate=COST,
        name="last_weights",
    )(normed, grads, *parts, gains)


def middle_kernel(*refs):
    me_ref, dn_refs = refs[0], refs[1:4]
    cot_ref, mid_ref, gain_ref, wo_ref = refs[4:8]
    dmid_ref, branch_ref, da_refs = refs[-6], refs[-5], refs[-4:]
    me = me_ref[0]
    tok = mid_ref.shape[0]

    def rows_of(i, carry):
        rows = at_rows(i)
        middle = mid_ref[rows, :]
        d_normed = dn_refs[0][rows, :].astype(F32)
        for ref in dn_refs[1:]:
            d_normed = d_normed + ref[rows, :].astype(F32)
        r2 = lax.rsqrt(jnp.mean(middle * middle, axis=1, keepdims=True) + EPSILON)
        scaled = d_normed * gain_ref[...]
        pull = jnp.mean(scaled * middle, axis=1, keepdims=True)
        d_middle = cot_ref[rows, :].astype(F32) + r2 * scaled - middle * (r2 * r2 * r2 * pull)
        dmid_ref[rows, :] = d_middle
        branch_ref[rows, :] = d_middle.astype(BF16)
        return carry

    lax.fori_loop(0, tok // ROWS, rows_of, 0)
    span = 2 * LANES
    for d in range(4):
        there = pl.ds(pl.multiple_of(jnp.bitwise_xor(me, d) * span, span), span)
        da_refs[d][...] = dot_nt(branch_ref[...], wo_ref[there, :]).astype(BF16)


def out_kernel(me_ref, *refs):
    att_refs, branch_ref, outs = refs[:8], refs[8], refs[9:]
    span = 2 * LANES
    for d in range(4):
        there = pl.ds(pl.multiple_of(jnp.bitwise_xor(me_ref[0], d) * span, span), span)
        rows = jnp.concatenate([att_refs[2 * d][...], att_refs[2 * d + 1][...]], axis=1)
        for e in range(4):
            columns = pl.ds(pl.multiple_of(jnp.bitwise_xor(me_ref[0], e) * span, span), span)
            outs[e][there, :] = dot_tn(rows, branch_ref[:, columns]).astype(BF16)


def out_weights(me, att, branch):
    tok, width = branch.shape
    whole = lambda r, c: pl.BlockSpec((r, c), lambda i: (0, 0))
    own = lambda d: pl.BlockSpec((tok, LANES), lambda i: (d, 0))
    return pl.pallas_call(
        out_kernel,
        grid=(1,),
        out_shape=(jax.ShapeDtypeStruct((width, width // 4), BF16),) * 4,
        in_specs=[smem()] + [own(d) for d in range(4) for _ in range(2)] + [whole(tok, width)],
        out_specs=(whole(width, width // 4),) * 4,
        compiler_params=params(),
        cost_estimate=COST,
        name="out_weights",
    )(me, *att, branch)


def middle_back(me, parts, cot, middle, gain, wo, after):
    tok, width = middle.shape
    whole = lambda r, c: pl.BlockSpec((r, c), lambda i: (0, 0))
    out = lambda r, c, t=BF16: jax.ShapeDtypeStruct((r, c), t)
    return pl.pallas_call(
        middle_kernel,
        grid=(1,),
        out_shape=(out(tok, width, F32), out(tok, width)) + (out(tok, 2 * LANES),) * 4,
        in_specs=[smem()] + [whole(tok, width)] * 5 + [whole(1, width), whole(*wo.shape)] + anywhere(after),
        out_specs=(whole(tok, width),) * 2 + (whole(tok, 2 * LANES),) * 4,
        compiler_params=params(),
        cost_estimate=COST,
        name="middle_back",
    )(me, *parts, cot, middle, gain, wo, *after)


def swap(array, distance):
    return lax.ppermute(array, "seq", [(s, s ^ distance) for s in range(4)])


def gather_rows(block, meanwhile):
    half = block.shape[1] // 2
    one, two = swap(block, 1), swap(block, 2)
    one, two, meanwhile = lax.optimization_barrier((one, two, meanwhile))
    return [meanwhile, [one], [two], [swap(one[:, :half], 2), swap(two[:, half:], 1)]]


def after(value, *others):
    return lax.optimization_barrier((value, others))[0]


def body(
    tokens, order, seq_lengths, attn_gain, w_query, w_key, w_value, query_gain, key_gain,
    w_out, ffn_gain, w_gate, w_up, w_down, cotangent,
):
    tok = tokens.shape[1]
    ways = lax.axis_size("seq")
    shards = lax.axis_size("shard")
    all_rows = tok * ways
    head_dim = query_gain.shape[0]
    me = lax.axis_index("seq")
    me_arr = me.astype(jnp.int32)[None]
    own = lambda a, axis: lax.dynamic_slice_in_dim(a, me * (a.shape[axis] // ways), a.shape[axis] // ways, axis)
    depth = w_gate.shape[0]
    units = w_gate.shape[1] // ways
    piece = units // shards

    dealt_index = jnp.arange(all_rows, dtype=jnp.int32)
    ends = jnp.cumsum(seq_lengths[0])
    start = jnp.zeros_like(dealt_index)
    for s in range(seq_lengths.shape[1] - 1):
        start = jnp.where(dealt_index >= ends[s], ends[s], start)
    places = (dealt_index - start).astype(F32)
    lane = jnp.arange(LANES, dtype=jnp.int32) % head_dim
    half = head_dim // 2
    frequency = ROPE_BASE ** (-2.0 * jnp.arange(half, dtype=F32) / head_dim)
    angles = places[:, None] * frequency[None, :]
    cosine = jnp.tile(jnp.cos(angles), (1, LANES // half))
    sine = jnp.tile(jnp.sin(angles), (1, LANES // half))
    sine_up = jnp.where(lane[None, :] < half, -sine, 0.0)
    sine_down = jnp.where(lane[None, :] < half, 0.0, sine)
    relative = jnp.bitwise_xor(order[0], me.astype(jnp.int32) * tok)
    ocol, orow = relative[:, None], relative[None, :]
    q_gain = jnp.tile(query_gain.astype(F32), LANES // head_dim)[None, :]
    k_gain = jnp.tile(key_gain.astype(F32), LANES // head_dim)[None, :]

    tables = (cosine, sine_up, sine_down, ocol, orow, q_gain, k_gain)

    xs = gather_rows(tokens[0], tables)
    w_first = first_weights(me_arr, w_query, w_key, w_value, attn_gain, ffn_gain)
    w_qkv = lax.all_gather(w_first, "shard", axis=0, tiled=True)
    w_o = lax.all_gather(w_out, "shard", axis=0, tiled=True)
    cut = lambda w: own(w.reshape(depth, shards, ways, piece), 2).reshape(depth, units)
    w_gate_now, w_up_now, w_down_now = after((w_gate, w_up, w_down), tables)
    w_gu = lax.all_gather(jnp.concatenate([cut(w_gate_now), cut(w_up_now)], axis=1), "shard", axis=0, tiled=True)
    w_d = lax.all_gather(own(w_down_now, 0), "shard", axis=0, tiled=True)

    cosine, sine_up, sine_down, ocol, orow, q_gain, k_gain = xs[0]
    xs = [[tokens[0]]] + xs[1:]
    normed, qx, k, v, vx, kt, rawq, rawk, gains = qkv(
        [x for one in xs for x in one], w_qkv, ocol, cosine, sine_up, sine_down, q_gain, k_gain, head_dim
    )
    cot = cotangent[0]
    cots = [[cot]] + gather_rows(after(cot, xs[3]), ())[1:]
    gain_a, gain_f = gains[0:1], gains[1:2]
    w_rows = jnp.concatenate(after([w_query, w_key, w_value], xs[3]), axis=1)
    w_all = lax.all_gather(w_rows, "shard", axis=0, tiled=True)

    att, dealts, lses = [], [], []
    for g in range(2):
        given, dealt, lse = attend(g, seq_lengths, orow, qx, k, vx, head_dim, cots[3] if g else [])
        att.append([given] + [swap(given, d) for d in (1, 2, 3)])
        dealts.append(dealt)
        lses.append(lse)
    att = [att[g][d] for d in range(4) for g in range(2)]

    feed = lambda blocks, diag, carried: ffn(
        me_arr, blocks, att, xs, cots, w_o, gain_f, w_gu, w_d, diag, carried
    )
    *carried, dn3a, dn3b, bo3 = feed((3,), (), ())
    diag = (swap(dn3a, 1), swap(dn3b, 2))
    *carried, dn0, bo0, middle = feed((0,), (), carried)
    bo3 = swap(after(bo3, diag), 3)
    *carried, dn1, dn2, bo1, bo2 = feed((1, 2), diag, carried)
    nf, hidden, d_gu, cot_all = carried
    dn1, dn2 = after((dn1, dn2), bo3)
    dn = (dn0, swap(dn1, 1), swap(dn2, 2))
    scatter = lambda a: lax.psum_scatter(a, "shard", scatter_dimension=0, tiled=True)
    p_wd, p_wgu = weights_back(hidden, cot_all, 3), weights_back(nf, d_gu, 4)
    p_wd, p_wgu = after((p_wd, p_wgu), dn)
    d_wd, d_wgu = scatter(p_wd), scatter(p_wgu)

    d_middle, branch, *d_att = middle_back(me_arr, dn, cot, middle, gain_f, w_o, (p_wd, p_wgu, w_all))
    p_wo = out_weights(me_arr, att, branch)
    d_att = [d_att[0]] + [swap(d_att[d], d) for d in (1, 2, 3)]
    draw, head_gains = attend_back(
        seq_lengths, ocol, qx, k, v, kt, lses, dealts, d_att, rawq, rawk,
        cosine, sine_up, sine_down, q_gain, k_gain, head_dim, (d_wd,),
    )
    bo1, bo2, *p_wo = after([bo1, bo2] + list(p_wo), d_att)
    bo = [bo0, swap(bo1, 1), swap(bo2, 2), bo3]
    p_wo = [p_wo[0]] + [swap(p_wo[d], d) for d in (1, 2, 3)]
    grads, *d_raw = rows_back(orow, draw, bo[1:3] + p_wo[1:])
    block_out = (middle + sum(b.astype(F32) for b in after(bo, grads))).astype(BF16)
    d_raw = [d_raw[0]] + [swap(d_raw[d], d) for d in (1, 2, 3)]
    p_last = last_weights(normed, grads, p_wo, head_gains, shards)
    d_last = scatter(after(p_last, d_wgu))
    d_tokens = tokens_back(me_arr, d_raw, w_all, tokens[0], d_middle, gain_a, (p_last,))
    d_wgu, d_wd = after((d_wgu, d_wd), d_raw, p_last)

    odd, high = me % 2 == 1, me // 2 == 1

    def in_order(parts):
        parts = list(parts)
        for a, b, which in ((0, 1, odd), (2, 3, odd), (0, 2, high), (1, 3, high)):
            parts[a], parts[b] = jnp.where(which, parts[b], parts[a]), jnp.where(which, parts[a], parts[b])
        return parts

    def quarters(part):
        return in_order([part] + [swap(part, d) for d in (1, 2, 3)])

    d_wd = quarters(d_wd)
    d_wd = jnp.concatenate(d_wd, axis=0).astype(F32)
    columns = lambda parts, at: jnp.stack(
        [p[:, at:at + units].reshape(depth, shards, piece) for p in parts], axis=2
    ).reshape(depth, -1).astype(F32)
    d_wgu = quarters(d_wgu)
    d_wg, d_wu = columns(d_wgu, 0), columns(d_wgu, units)
    last = quarters(after(d_last, d_wgu))
    beside = lambda parts, lo, hi: jnp.concatenate([p[:, lo:hi] for p in parts], axis=1).astype(F32)
    d_wq, d_wk, d_wv = beside(last, 0, 256), beside(last, 256, 384), beside(last, 384, 512)
    d_wo = beside(last, 512, 768)
    dot_rows = lambda w, d: jnp.sum(w.astype(F32) * d, axis=1)
    d_attn_gain = (dot_rows(w_query, d_wq) + dot_rows(w_key, d_wk) + dot_rows(w_value, d_wv)) / attn_gain.astype(F32)
    d_ffn_gain = (dot_rows(w_gate, d_wg) + dot_rows(w_up, d_wu)) / ffn_gain.astype(F32)
    head_gains = sum(p[0:2, 768:768 + LANES].astype(F32) for p in last)
    head_gains = head_gains[:, :head_dim] + head_gains[:, head_dim:]
    return (
        block_out[None], d_tokens[None], d_attn_gain, d_wq, d_wk, d_wv, head_gains[0], head_gains[1],
        d_wo, d_ffn_gain, d_wg, d_wu, d_wd,
    )


def solution(mesh):
    rows, flat, wide = P("shard", None), P("shard"), P("shard", "seq", None)
    in_specs = (
        wide, rows, rows, flat, rows, rows, rows, P(), P(), rows, flat, rows, rows, rows, wide,
    )
    out_specs = (wide, wide, flat, rows, rows, rows, P(), P(), rows, flat, rows, rows, rows)
    return jax.shard_map(body, mesh=mesh, in_specs=in_specs, out_specs=out_specs, check_vma=False)
```

```python
import functools

import jax
import jax.numpy as jnp
from jax import lax
from jax.experimental import pallas as pl
from jax.experimental.pallas import tpu as pltpu
from jax.sharding import PartitionSpec as P

EPSILON = 1e-05
ROPE_BASE = 1000000.0
LOG2E = 1.4426950408889634
ROWS = 256
LANES = 128
F32 = jnp.float32
BF16 = jnp.bfloat16
COST = pl.CostEstimate(flops=1 << 20, bytes_accessed=1 << 16, transcendentals=0)
VMEM_LIMIT = 58 * 1024 * 1024


def dot_nn(left, right):
    return jnp.dot(left, right, preferred_element_type=F32)


def dot_nt(left, right):
    return lax.dot_general(left, right, (((1,), (1,)), ((), ())), preferred_element_type=F32)


def dot_tn(left, right):
    return lax.dot_general(left, right, (((0,), (0,)), ((), ())), preferred_element_type=F32)


def vmem():
    return pl.BlockSpec(memory_space=pltpu.VMEM)


def smem():
    return pl.BlockSpec(memory_space=pltpu.SMEM)


def params():
    return pltpu.CompilerParams(vmem_limit_bytes=VMEM_LIMIT)


def lane_iota(rows, columns):
    return lax.broadcasted_iota(jnp.int32, (rows, columns), 1)


def row_iota(rows, columns):
    return lax.broadcasted_iota(jnp.int32, (rows, columns), 0)


def at_rows(block, rows=ROWS):
    return pl.ds(pl.multiple_of(block * rows, rows), rows)


def pair_ones(head_dim):
    return (
        row_iota(LANES, LANES) // head_dim == lane_iota(LANES, LANES) // head_dim
    ).astype(BF16)


def head_mean(values, ones, head_dim):
    high = values.astype(BF16)
    low = (values - high.astype(F32)).astype(BF16)
    return (dot_nn(high, ones) + dot_nn(low, ones)) * (1.0 / head_dim)


def turn(values, cosine, sine_up, sine_down, head_dim, sign=1.0):
    half = head_dim // 2
    up = pltpu.roll(values, LANES - half, 1) * sine_up
    down = pltpu.roll(values, half, 1) * sine_down
    return values * cosine + sign * (up + down)


def spread_heads(pair, group, head_dim, low_lanes):
    moved = pltpu.roll(pair, head_dim, 1)
    if group == 0:
        return jnp.where(low_lanes, pair, 0.0), jnp.where(low_lanes, moved, 0.0)
    return jnp.where(low_lanes, 0.0, moved), jnp.where(low_lanes, 0.0, pair)


def first_kernel(me_ref, q_ref, k_ref, v_ref, ga_ref, gf_ref, out_ref):
    at = 0
    for ref in (q_ref, k_ref, v_ref):
        size = ref.shape[1] // 4
        out_ref[:, at:at + size] = ref[:, pl.ds(pl.multiple_of(me_ref[0] * size, size), size)]
        at += size
    depth = out_ref.shape[0]
    row = row_iota(LANES, depth)
    gains = jnp.where(row == 0, ga_ref[...].astype(F32), jnp.where(row == 1, gf_ref[...].astype(F32), 0.0))
    out_ref[:, at:] = jnp.transpose(gains).astype(BF16)


def first_weights(me, w_query, w_key, w_value, attn_gain, ffn_gain):
    depth = w_query.shape[0]
    width = (w_query.shape[1] + w_key.shape[1] + w_value.shape[1]) // 4 + LANES
    return pl.pallas_call(
        first_kernel,
        out_shape=jax.ShapeDtypeStruct((depth, width), BF16),
        in_specs=[smem()] + [vmem()] * 5,
        out_specs=vmem(),
        compiler_params=params(),
        cost_estimate=COST,
        name="first_weights",
    )(me, w_query, w_key, w_value, attn_gain[None], ffn_gain[None])


def cut_kernel(shards, me_ref, gate_ref, up_ref, down_ref, wo_ref, out_ref):
    whole, units = gate_ref.shape[1], down_ref.shape[1]
    piece, span = units // shards, whole // shards
    for at, ref in ((0, gate_ref), (units, up_ref)):
        turned = pltpu.roll(ref[...].astype(F32), whole - piece * me_ref[0], 1)
        parts = [turned[:, span * k:span * k + piece] for k in range(shards)]
        out_ref[:, at:at + units] = jnp.concatenate(parts, axis=1).astype(BF16)
    out_ref[:, 2 * units:3 * units] = down_ref[...]
    width = wo_ref.shape[1]
    out_ref[:, 3 * units:3 * units + width] = wo_ref[...]
    out_ref[:, 3 * units + width:] = jnp.zeros((out_ref.shape[0], units - width), BF16)


def cut_weights(me, w_gate, w_up, w_down, w_out, shards):
    depth, whole = w_gate.shape
    return pl.pallas_call(
        functools.partial(cut_kernel, shards),
        out_shape=jax.ShapeDtypeStruct((depth, whole), BF16),
        in_specs=[smem()] + [vmem()] * 4,
        out_specs=vmem(),
        compiler_params=params(),
        cost_estimate=COST,
        name="cut_weights",
    )(me, w_gate, w_up, w_down, w_out)


def join_kernel(shards, me_ref, p0_ref, p1_ref, p2_ref, p3_ref, gate_ref, up_ref, dgate_ref, dup_ref, dot_ref, st_ref):
    for d, ref in enumerate((p0_ref, p1_ref, p2_ref, p3_ref)):
        st_ref[d] = ref[...]
    units = p0_ref.shape[1] // 2
    piece = units // shards
    quarters = [st_ref[jnp.bitwise_xor(me_ref[0], q)] for q in range(4)]
    total = 0.0
    for at, w_ref, out_ref in ((0, gate_ref, dgate_ref), (units, up_ref, dup_ref)):
        parts = [q[:, at:at + units].astype(F32) for q in quarters]
        parts = [q[:, piece * k:piece * (k + 1)] for k in range(shards) for q in parts]
        joined = jnp.concatenate(parts, axis=1)
        out_ref[...] = joined
        total = total + jnp.sum(joined * w_ref[...].astype(F32), axis=1, keepdims=True)
    dot_ref[...] = total


def join_weights(me, parts, w_gate, w_up, shards):
    depth, whole = w_gate.shape
    return pl.pallas_call(
        functools.partial(join_kernel, shards),
        out_shape=(jax.ShapeDtypeStruct((depth, whole), F32),) * 2 + (jax.ShapeDtypeStruct((depth, 1), F32),),
        in_specs=[smem()] + [vmem()] * 6,
        out_specs=(vmem(),) * 3,
        scratch_shapes=[pltpu.VMEM((4,) + parts[0].shape, BF16)],
        compiler_params=params(),
        cost_estimate=COST,
        name="join_weights",
    )(me, *parts, w_gate, w_up)


def join_last_kernel(me_ref, p0_ref, p1_ref, p2_ref, p3_ref, q_ref, k_ref, v_ref,
                     dq_ref, dk_ref, dv_ref, do_ref, dot_ref, gain_ref):
    at = 0
    parts = (p0_ref, p1_ref, p2_ref, p3_ref)
    total = jnp.zeros(dot_ref.shape, F32)
    for out_ref, w_ref in ((dq_ref, q_ref), (dk_ref, k_ref), (dv_ref, v_ref), (do_ref, None)):
        size = out_ref.shape[1] // 4
        for d, ref in enumerate(parts):
            there = pl.ds(pl.multiple_of(jnp.bitwise_xor(me_ref[0], d) * size, size), size)
            part = ref[:, at:at + size].astype(F32)
            out_ref[:, there] = part
            if w_ref is not None:
                total = total + jnp.sum(part * w_ref[:, there].astype(F32), axis=1, keepdims=True)
        at += size
    dot_ref[...] = total
    gains = jnp.zeros(gain_ref.shape, F32)
    for ref in parts:
        gains = gains + ref[0:16, at:].astype(F32)[:8]
    gain_ref[...] = gains


def join_last(me, parts, w_query, w_key, w_value, out_width):
    depth = w_query.shape[0]
    out = lambda c: jax.ShapeDtypeStruct((depth, c), F32)
    return pl.pallas_call(
        join_last_kernel,
        out_shape=(
            out(w_query.shape[1]), out(w_key.shape[1]), out(w_value.shape[1]), out(out_width), out(1),
            jax.ShapeDtypeStruct((8, LANES), F32),
        ),
        in_specs=[smem()] + [vmem()] * 7,
        out_specs=(vmem(),) * 6,
        compiler_params=params(),
        cost_estimate=COST,
        name="join_last",
    )(me, *parts, w_query, w_key, w_value)


def table_kernel(half, me_ref, lens_ref, order_ref, freq_ref, cos_ref, up_ref, down_ref, ocol_ref, orow_ref):
    all_rows = order_ref.shape[1]
    groups = LANES // half
    rows = all_rows // groups
    lane = lane_iota(rows, LANES)
    index = lane // half * rows + row_iota(rows, LANES)
    angles = (index - row_starts(lens_ref, index)).astype(F32) * freq_ref[...]
    cosine, sine = jnp.cos(angles), jnp.sin(angles)
    first = lane % (2 * half) < half
    for q in range(groups):

        def spread(table, q=q):
            one = jnp.where(lane < half, pltpu.roll(table, LANES - half * q, 1) if q else table, 0.0)
            return one + pltpu.roll(one, half, 1) + pltpu.roll(one, 2 * half, 1) + pltpu.roll(one, 3 * half, 1)

        here = slice(q * rows, (q + 1) * rows)
        cos_ref[here, :] = spread(cosine)
        wide = spread(sine)
        up_ref[here, :] = jnp.where(first, -wide, 0.0)
        down_ref[here, :] = jnp.where(first, 0.0, wide)
    relative = jnp.bitwise_xor(order_ref[...], me_ref[0] * (all_rows // 4))
    orow_ref[...] = relative
    for c in range(all_rows // LANES):
        here = slice(c * LANES, (c + 1) * LANES)
        across = jnp.broadcast_to(relative[:, here].astype(F32), (LANES, LANES))
        ocol_ref[here, :] = jnp.transpose(across).astype(jnp.int32)


def make_tables(me, lens, order, head_dim):
    all_rows = order.shape[1]
    half = head_dim // 2
    frequency = ROPE_BASE ** (-2.0 * jnp.arange(half, dtype=F32) / head_dim)
    out = lambda r, c, t: jax.ShapeDtypeStruct((r, c), t)
    return pl.pallas_call(
        functools.partial(table_kernel, half),
        out_shape=(out(all_rows, LANES, F32),) * 3 + (out(all_rows, LANES, jnp.int32), out(1, all_rows, jnp.int32)),
        in_specs=[smem(), smem(), vmem(), vmem()],
        out_specs=(vmem(),) * 5,
        compiler_params=params(),
        cost_estimate=COST,
        name="make_tables",
    )(me, lens, order, jnp.tile(frequency, LANES // half)[None, :])


def qkv_kernel(
    head_dim, x0_ref, x1_ref, x2_ref, x3a_ref, x3b_ref, w_ref, ocol_ref, cos_ref, su_ref, sd_ref,
    qg_ref, kg_ref, normed_ref, qx_ref, k_ref, v_ref, vx_ref, kt_ref, rawq_ref, rawk_ref, gain_ref, raw_ref,
):
    i = pl.program_id(0)
    tok = x0_ref.shape[0]
    all_rows, width = raw_ref.shape
    pairs = rawq_ref.shape[1] // LANES

    @pl.when(i == 0)
    def _():
        gain_ref[...] = jnp.transpose(w_ref[:, width:].astype(F32))[:8]

    def project(x, rows):
        x = x.astype(F32)
        r1 = lax.rsqrt(jnp.mean(x * x, axis=1, keepdims=True) + EPSILON)
        normed = (x * r1 * gain_ref[0:1, :]).astype(BF16)
        normed_ref[...] = normed
        raw_ref[rows, :] = dot_nn(normed, w_ref[:, :width]).astype(BF16)

    for d, refs in enumerate(((x0_ref,), (x1_ref,), (x2_ref,), (x3a_ref, x3b_ref))):

        @pl.when(i == d)
        def _(d=d, refs=refs):
            project(jnp.concatenate([ref[...] for ref in refs], axis=1), slice(d * tok, (d + 1) * tok))

    @pl.when(i >= 4)
    def _():
        ones = pair_ones(head_dim)
        low_lanes = lane_iota(tok, LANES) < head_dim
        pick = (ocol_ref[:, 0:1] == lane_iota(tok, all_rows)).astype(F32).astype(BF16)
        dealt = dot_nn(pick, raw_ref[...])
        cosine, su, sd = cos_ref[...], su_ref[...], sd_ref[...]
        for g in range(pairs):
            raw = dealt[:, g * LANES:(g + 1) * LANES]
            rawq_ref[:, g * LANES:(g + 1) * LANES] = raw.astype(BF16)
            rq = lax.rsqrt(head_mean(raw * raw, ones, head_dim) + EPSILON)
            pair = turn(raw * rq * qg_ref[...], cosine, su, sd, head_dim)
            for r, one in enumerate(spread_heads(pair, g, head_dim, low_lanes)):
                qx_ref[2 * g + r] = one.astype(BF16)
        raw = dealt[:, pairs * LANES:(pairs + 1) * LANES]
        rawk_ref[...] = raw.astype(BF16)
        rk = lax.rsqrt(head_mean(raw * raw, ones, head_dim) + EPSILON)
        keys = turn(raw * rk * kg_ref[...], cosine, su, sd, head_dim)
        k_ref[...] = keys.astype(BF16)
        kt_ref[...] = jnp.transpose(keys).astype(BF16)
        values = dealt[:, (pairs + 1) * LANES:]
        v_ref[...] = values.astype(BF16)
        vx_ref[0] = jnp.where(low_lanes, values, 1.0).astype(BF16)
        vx_ref[1] = jnp.where(low_lanes, 1.0, values).astype(BF16)


def fixed(array):
    return pl.BlockSpec(array.shape, lambda i: (0,) * array.ndim, pipeline_mode=pl.Buffered(1))


def qkv(xs, w, ocol, cosine, su, sd, qg, kg, head_dim):
    tok, width = xs[0].shape
    all_rows = 4 * tok
    out = lambda *dims: jax.ShapeDtypeStruct(dims, BF16)
    late = lambda c: pl.BlockSpec((tok, c), lambda i: (jnp.maximum(i - 4, 0), 0))
    heads = lambda n: pl.BlockSpec((n, tok, LANES), lambda i: (0, jnp.maximum(i - 4, 0), 0))
    return pl.pallas_call(
        functools.partial(qkv_kernel, head_dim),
        grid=(8,),
        out_shape=(
            out(all_rows, width), out(4, all_rows, LANES), out(all_rows, LANES), out(all_rows, LANES),
            out(2, all_rows, LANES), out(LANES, all_rows), out(all_rows, 2 * LANES), out(all_rows, LANES),
            jax.ShapeDtypeStruct((8, width), F32),
        ),
        in_specs=[fixed(x) for x in xs] + [fixed(w)] + [late(LANES)] * 4 + [fixed(qg), fixed(kg)],
        out_specs=(
            pl.BlockSpec((tok, width), lambda i: (jnp.minimum(i, 3), 0)),
            heads(4), late(LANES), late(LANES), heads(2),
            pl.BlockSpec((LANES, tok), lambda i: (0, jnp.maximum(i - 4, 0))), late(2 * LANES), late(LANES),
            pl.BlockSpec((8, width), lambda i: (0, 0)),
        ),
        scratch_shapes=[pltpu.VMEM((all_rows, 4 * LANES), BF16)],
        compiler_params=params(),
        cost_estimate=COST,
        name="qkv",
    )(*xs, w, ocol, cosine, su, sd, qg, kg)


def row_starts(lens_ref, index):
    start = jnp.zeros_like(index)
    end = lens_ref[0, 0]
    for s in range(1, lens_ref.shape[1]):
        start = jnp.where(index >= end, end, start)
        end = end + lens_ref[0, s]
    return start


def attend_kernel(head_dim, group, block, lens_ref, orow_ref, qx_ref, k_ref, vx_ref, *refs):
    given_ref, dealt_ref, lse_ref = refs[-3:]
    all_rows = k_ref.shape[0]
    scale = LOG2E * head_dim ** -0.5
    low_lanes = lane_iota(block, LANES) < head_dim
    mass_row = head_dim if group == 0 else 0

    def query_block(i, carry):
        rows = at_rows(i, block)
        q_index = i * block + row_iota(block, 1)
        start = row_starts(lens_ref, q_index)
        first = row_starts(lens_ref, i * block) // block
        clear = jnp.minimum((row_starts(lens_ref, i * block + block - 1) + block - 1) // block, i)
        queries = [qx_ref[r, rows, :] for r in range(2)]

        def step(j, state, masked):
            columns = at_rows(j, block)
            keys, values = k_ref[columns, :], vx_ref[0, columns, :]
            k_index = j * block + lane_iota(block, block)
            keep = (k_index <= q_index) & (k_index >= start)
            new = []
            for r in range(2):
                weights = jnp.exp2(dot_nt(queries[r], keys) * scale)
                if masked:
                    weights = jnp.where(keep, weights, 0.0)
                new.append(state[r] + dot_nn(weights.astype(BF16), values))
            return tuple(new)

        state = (jnp.zeros((block, LANES), F32),) * 2
        state = lax.fori_loop(first, clear, functools.partial(step, masked=True), state)
        state = lax.fori_loop(clear, i, functools.partial(step, masked=False), state)
        state = step(i, state, True)
        out = []
        for r in range(2):
            lse_ref[r:r + 1, rows] = jnp.log2(jnp.transpose(state[r])[mass_row:mass_row + 1, :])
            out.append(state[r] / pltpu.roll(state[r], head_dim, 1))
        if group == 0:
            pair = jnp.where(low_lanes, out[0], pltpu.roll(out[1], head_dim, 1))
        else:
            pair = jnp.where(low_lanes, pltpu.roll(out[0], head_dim, 1), out[1])
        dealt_ref[rows, :] = pair.astype(BF16)
        return carry

    lax.fori_loop(0, all_rows // block, query_block, 0)

    def undeal(i, carry):
        rows = at_rows(i, block)
        pick = (orow_ref[...] == i * block + row_iota(block, all_rows)).astype(F32).astype(BF16)
        given_ref[rows, :] = dot_nn(pick, dealt_ref[...]).astype(BF16)
        return carry

    lax.fori_loop(0, all_rows // block, undeal, 0)


def attend(group, lens, orow, qx, k, vx, head_dim, after):
    all_rows = k.shape[0]
    whole = lambda *dims: pl.BlockSpec(dims, lambda i: (0,) * len(dims))
    return pl.pallas_call(
        functools.partial(attend_kernel, head_dim, group, all_rows // 4),
        grid=(1,),
        out_shape=(
            jax.ShapeDtypeStruct((all_rows, LANES), BF16),
            jax.ShapeDtypeStruct((all_rows, LANES), BF16),
            jax.ShapeDtypeStruct((2, all_rows), F32),
        ),
        in_specs=[
            smem(), whole(1, all_rows),
            pl.BlockSpec((2, all_rows, LANES), lambda i: (group, 0, 0)),
            whole(all_rows, LANES),
            pl.BlockSpec((1, all_rows, LANES), lambda i: (group, 0, 0)),
        ] + anywhere(after),
        out_specs=(whole(all_rows, LANES), whole(all_rows, LANES), whole(2, all_rows)),
        compiler_params=params(),
        cost_estimate=COST,
        name="attend",
    )(lens, orow, qx, k, vx, *after)


def attend_back_kernel(head_dim, *refs):
    (lens_ref, ocol_ref, qx_ref, k_ref, v_ref, kt_ref, lse0_ref, lse1_ref, o0_ref, o1_ref,
     d0_ref, d1_ref, d2_ref, d3_ref, rawq_ref, rawk_ref, cos_ref, su_ref, sd_ref, qg_ref, kg_ref) = refs[:21]
    draw_ref, gain_ref, dgiven_ref, dx_ref, delta_ref, dk_ref, dv_ref = refs[-7:]
    all_rows = k_ref.shape[0]
    blocks = all_rows // ROWS
    exponent = LOG2E * head_dim ** -0.5
    scale = head_dim ** -0.5
    low_lanes = lane_iota(ROWS, LANES) < head_dim
    tok = d0_ref.shape[0]
    for d, ref in enumerate((d0_ref, d1_ref, d2_ref, d3_ref)):
        dgiven_ref[d * tok:(d + 1) * tok, :] = ref[...]
    dk_ref[...] = jnp.zeros_like(dk_ref)
    dv_ref[...] = jnp.zeros_like(dv_ref)
    gain_ref[...] = jnp.zeros_like(gain_ref)

    def deal(i, carry):
        rows = at_rows(i)
        pick = (ocol_ref[rows, 0:1] == lane_iota(ROWS, all_rows)).astype(F32).astype(BF16)
        dealt = dot_nn(pick, dgiven_ref[...])
        for g, o_ref in enumerate((o0_ref, o1_ref)):
            pair = dealt[:, g * LANES:(g + 1) * LANES]
            for r, one in enumerate(spread_heads(pair, g, head_dim, low_lanes)):
                dx_ref[2 * g + r, rows, :] = one.astype(BF16)
            across = jnp.transpose(pair * o_ref[rows, :].astype(F32))
            for r in range(2):
                delta_ref[2 * g + r:2 * g + r + 1, rows] = jnp.sum(
                    across[r * head_dim:(r + 1) * head_dim], axis=0, keepdims=True
                )
        return carry

    lax.fori_loop(0, blocks, deal, 0)
    ones = pair_ones(head_dim)

    def query_block(i, carry):
        rows = at_rows(i)
        q_index = i * ROWS + lane_iota(1, ROWS)
        start = row_starts(lens_ref, q_index)
        first = row_starts(lens_ref, i * ROWS) // ROWS

        def step(j, state):
            columns = at_rows(j)
            k_index = j * ROWS + row_iota(ROWS, ROWS)
            keep = (k_index <= q_index) & (k_index >= start)
            keys = k_ref[columns, :]
            values = v_ref[columns, :]
            new = []
            dk, dv = dk_ref[columns, :], dv_ref[columns, :]
            for h in range(4):
                g = h // 2
                queries = qx_ref[h, rows, :]
                grads = dx_ref[h, rows, :]
                lse = (lse0_ref, lse1_ref)[g][h % 2:h % 2 + 1, rows]
                weights = jnp.where(keep, jnp.exp2(dot_nt(keys, queries) * exponent - lse), 0.0)
                d_weights = dot_nt(values, grads)
                d_scores = (weights * (d_weights - delta_ref[h:h + 1, rows])).astype(BF16)
                dv = dv + dot_nn(weights.astype(BF16), grads)
                dk = dk + dot_nn(d_scores, queries)
                new.append(state[h] + dot_nn(kt_ref[g * head_dim:(g + 1) * head_dim, columns], d_scores))
            dk_ref[columns, :] = dk
            dv_ref[columns, :] = dv
            return tuple(new)

        state = lax.fori_loop(first, i + 1, step, (jnp.zeros((head_dim, ROWS), F32),) * 4)
        cosine, su, sd = cos_ref[rows, :], su_ref[rows, :], sd_ref[rows, :]
        for g in range(2):
            pair = jnp.transpose(jnp.concatenate(state[2 * g:2 * g + 2], axis=0)) * scale
            lanes = slice(g * LANES, (g + 1) * LANES)
            draw, gain = norm_back(
                pair, rawq_ref[rows, lanes].astype(F32), qg_ref[...], cosine, su, sd, ones, head_dim
            )
            draw_ref[rows, lanes] = draw
            gain_ref[0:1, :] += gain
        return carry

    lax.fori_loop(0, blocks, query_block, 0)

    def key_block(i, carry):
        rows = at_rows(i)
        cosine, su, sd = cos_ref[rows, :], su_ref[rows, :], sd_ref[rows, :]
        draw, gain = norm_back(
            dk_ref[rows, :] * scale, rawk_ref[rows, :].astype(F32), kg_ref[...], cosine, su, sd, ones, head_dim
        )
        draw_ref[rows, 2 * LANES:3 * LANES] = draw
        draw_ref[rows, 3 * LANES:] = dv_ref[rows, :].astype(BF16)
        gain_ref[1:2, :] += gain
        return carry

    lax.fori_loop(0, blocks, key_block, 0)


def rows_back_kernel(period, orow_ref, draw_ref, normed_ref, o0_ref, o1_ref, o2_ref, o3_ref, gain_ref, *refs):
    d_refs, out_ref, grad_ref = refs[-6:-2], refs[-2], refs[-1]
    i = pl.program_id(0)
    all_rows, width = draw_ref.shape
    rows = all_rows // 4
    for d, ref in enumerate(d_refs):

        @pl.when(i == d)
        def _(d=d, ref=ref):
            pick = (orow_ref[...] == d * rows + row_iota(rows, all_rows)).astype(F32).astype(BF16)
            grads = dot_nn(pick, draw_ref[...]).astype(BF16)
            grad_ref[d * rows:(d + 1) * rows, :] = grads
            ref[...] = grads

    @pl.when(i >= 4)
    def _():
        extra = o0_ref.shape[1]
        out_ref[:, :width] = dot_tn(normed_ref[...], grad_ref[...]).astype(BF16)
        total = o0_ref[...].astype(F32)
        for ref in (o1_ref, o2_ref, o3_ref):
            total = total + ref[...].astype(F32)
        out_ref[:, width:width + extra] = total.astype(BF16)
        place = row_iota(out_ref.shape[0], LANES) % period
        gains = jnp.where(place == 0, gain_ref[0:1, :], jnp.where(place == 1, gain_ref[1:2, :], 0.0))
        out_ref[:, width + extra:] = gains.astype(BF16)


def norm_back(pair, raw, gain, cosine, su, sd, ones, head_dim):
    pair = pair.astype(BF16).astype(F32)
    u = turn(pair, cosine, su, sd, head_dim, -1.0)
    r = lax.rsqrt(head_mean(raw * raw, ones, head_dim) + EPSILON)
    unit = raw * r
    scaled = u * gain
    draw = r * (scaled - unit * head_mean(scaled * unit, ones, head_dim))
    return draw.astype(BF16), jnp.sum(u * unit, axis=0, keepdims=True)


def anywhere(arrays):
    return [pl.BlockSpec(memory_space=pl.ANY)] * len(arrays)


def attend_back(lens, ocol, qx, k, v, kt, lses, dealts, grads, rawq, rawk, cosine, su, sd, qg, kg, head_dim, after):
    all_rows = k.shape[0]
    return pl.pallas_call(
        functools.partial(attend_back_kernel, head_dim),
        out_shape=(
            jax.ShapeDtypeStruct((all_rows, 4 * LANES), BF16),
            jax.ShapeDtypeStruct((2, LANES), F32),
        ),
        in_specs=[smem()] + [vmem()] * 20 + anywhere(after),
        out_specs=(vmem(),) * 2,
        scratch_shapes=[
            pltpu.VMEM((all_rows, 2 * LANES), BF16),
            pltpu.VMEM((4, all_rows, LANES), BF16),
            pltpu.VMEM((4, all_rows), F32),
            pltpu.VMEM((all_rows, LANES), F32),
            pltpu.VMEM((all_rows, LANES), F32),
        ],
        compiler_params=params(),
        cost_estimate=COST,
        name="attend_back",
    )(lens, ocol, qx, k, v, kt, *lses, *dealts, *grads, rawq, rawk, cosine, su, sd, qg, kg, *after)


def rows_back(orow, draw, normed, parts, gains, shards, after):
    all_rows, width = draw.shape
    depth, extra = normed.shape[1], parts[0].shape[1]
    tok = all_rows // 4
    late = lambda c: pl.BlockSpec((depth // 4, c), lambda i: (jnp.maximum(i - 4, 0), 0))
    wide = width + extra + LANES
    return pl.pallas_call(
        functools.partial(rows_back_kernel, depth // shards),
        grid=(8,),
        out_shape=(jax.ShapeDtypeStruct((tok, width), BF16),) * 4 + (jax.ShapeDtypeStruct((depth, wide), BF16),),
        in_specs=[fixed(orow), fixed(draw), pl.BlockSpec((all_rows, depth // 4), lambda i: (0, jnp.maximum(i - 4, 0)))]
        + [late(extra)] * 4 + [fixed(gains)] + anywhere(after),
        out_specs=(pl.BlockSpec((tok, width), lambda i: (0, 0)),) * 4 + (late(wide),),
        scratch_shapes=[pltpu.VMEM((all_rows, width), BF16)],
        compiler_params=params(),
        cost_estimate=COST,
        name="rows_back",
    )(orow, draw, normed, *parts, gains, *after)


def tokens_kernel(me_ref, g0_ref, g1_ref, g2_ref, g3_ref, w_ref, x_ref, mid_ref, gain_ref, *refs):
    out_ref = refs[-1]
    me = me_ref[0]
    d_normed = jnp.zeros(x_ref.shape, F32)
    span, width = 2 * LANES, 8 * LANES
    for d, ref in enumerate((g0_ref, g1_ref, g2_ref, g3_ref)):
        other = jnp.bitwise_xor(me, d)
        take = lambda at, size: w_ref[:, pl.ds(pl.multiple_of(at + other * size, size), size)]
        weights = jnp.concatenate([take(0, span), take(width, LANES), take(width + 4 * LANES, LANES)], axis=1)
        d_normed = d_normed + dot_nt(ref[...], weights)
    x = x_ref[...].astype(F32)
    r1 = lax.rsqrt(jnp.mean(x * x, axis=1, keepdims=True) + EPSILON)
    scaled = d_normed * gain_ref[...]
    pull = jnp.mean(scaled * x, axis=1, keepdims=True)
    out_ref[...] = (mid_ref[...] + r1 * scaled - x * (r1 * r1 * r1 * pull)).astype(BF16)


def tokens_back(me, grads, w, x, d_middle, gain, after):
    tok, width = x.shape
    rows = lambda c: pl.BlockSpec((ROWS, c), lambda i: (i, 0))
    return pl.pallas_call(
        tokens_kernel,
        grid=(tok // ROWS,),
        out_shape=jax.ShapeDtypeStruct((tok, width), BF16),
        in_specs=[smem()] + [rows(grads[0].shape[1])] * 4 + [fixed(w), rows(width), rows(width), fixed(gain)] + anywhere(after),
        out_specs=rows(width),
        compiler_params=params(),
        cost_estimate=COST,
        name="tokens_back",
    )(me, *grads, w, x, d_middle, gain, *after)


def ffn_kernel(per, blocks, n_carried, *refs):
    refs = list(refs)
    take = lambda n: [refs.pop(0) for _ in range(n)]
    me_ref = take(1)[0]
    att = [take(2 if d < 3 else 2 * len(blocks)) for d in range(4)]
    xs = [take(2 if d == 3 else 1) for d in blocks]
    cots = [take(2 if d == 3 else 1) for d in blocks]
    wo_ref, gain_ref, wg_ref, wu_ref, wd_ref = take(5)
    diag = take(4) if blocks == (1, 2) else None
    take(n_carried)
    nf_ref, hid_ref, dgu_ref, cot_ref = take(4)
    i = pl.program_id(0)
    me = me_ref[0]
    hidden_units = hid_ref.shape[1]
    which = i // per

    def read(lists):
        parts = [jnp.concatenate([ref[...] for ref in one], axis=1) for one in lists]
        return parts[0] if len(parts) == 1 else jnp.where(which == 0, parts[0], parts[1])

    middle = read(xs).astype(F32)
    for d in range(4):
        block = read([att[d][2 * n:2 * n + 2] for n in range(len(att[d]) // 2)])
        middle = middle + dot_nn(block, wo_ref[at_rows(jnp.bitwise_xor(me, d), 2 * LANES), :middle.shape[1]])
    r2 = lax.rsqrt(jnp.mean(middle * middle, axis=1, keepdims=True) + EPSILON)
    nf = (middle * r2 * gain_ref[...]).astype(BF16)
    nf_ref[...] = nf
    cot = read(cots)
    cot_ref[...] = cot
    wg, wu = wg_ref[...], wu_ref[...]
    gate = dot_nn(nf, wg)
    up = dot_nn(nf, wu)
    s = jax.nn.sigmoid(gate)
    silu = gate * s
    hidden = (silu * up).astype(BF16)
    hid_ref[...] = hidden
    d_hidden = dot_nt(cot, wd_ref[...])
    d_gate = (d_hidden * up * s * (1.0 + gate * (1.0 - s))).astype(BF16)
    d_up = (d_hidden * silu).astype(BF16)
    dgu_ref[:, :hidden_units] = d_gate
    dgu_ref[:, hidden_units:] = d_up
    dn = dot_nt(d_gate, wg) + dot_nt(d_up, wu)
    bo = dot_nn(hidden, wd_ref[...])
    half = dn.shape[1] // 2
    if blocks == (3,):
        for ref, value in zip(take(4), (dn[:, :half], dn[:, half:], bo[:, :half], bo[:, half:])):
            ref[...] = value.astype(BF16)
    elif blocks == (0,):
        dn_ref, bo_ref, mid_ref = take(3)
        dn_ref[...] = dn.astype(BF16)
        bo_ref[...] = bo.astype(BF16)
        mid_ref[...] = middle
    else:
        dn1_ref, dn2_ref, bo1_ref, bo2_ref = take(4)

        @pl.when(which == 0)
        def _():
            for ref, value, extra in ((dn1_ref, dn, diag[1]), (bo1_ref, bo, diag[3])):
                ref[:, :half] = value[:, :half].astype(BF16)
                ref[:, half:] = (value[:, half:] + extra[...].astype(F32)).astype(BF16)

        @pl.when(which == 1)
        def _():
            for ref, value, extra in ((dn2_ref, dn, diag[0]), (bo2_ref, bo, diag[2])):
                ref[:, :half] = (value[:, :half] + extra[...].astype(F32)).astype(BF16)
                ref[:, half:] = value[:, half:].astype(BF16)


def ffn(me, blocks, att, xs, cots, gain, wide, wd, diag, carried, after):
    all_rows = att[0].shape[0]
    units, width = wd.shape
    tok = all_rows // 4
    per = tok // ROWS
    block_of = lambda i: blocks[0] + (i // per) * (blocks[-1] - blocks[0])
    everywhere = lambda c: pl.BlockSpec((ROWS, c), lambda i: (block_of(i) * per + i % per, 0))
    crossed = lambda d: pl.BlockSpec(
        (ROWS, LANES), lambda i: (jnp.bitwise_xor(block_of(i), d) * per + i % per, 0)
    )
    held = lambda n, c: pl.BlockSpec((ROWS, c), lambda i: (jnp.clip(i - n * per, 0, per - 1), 0))
    halves = {0: 1, 1: 1, 2: 0, 3: 0}
    last = []
    for n, d in enumerate(blocks):
        local = lambda i, n=n, d=d: ((3 - d) % 2 * per + jnp.clip(i - n * per, 0, per - 1), 0)
        last += [(att[6], crossed(3)), (att[7 + halves[d]], pl.BlockSpec((ROWS, LANES), local))]
    weight = lambda n: pl.BlockSpec((wide.shape[0], units), lambda i: (0, n), pipeline_mode=pl.Buffered(1))
    out = lambda r, c, t=BF16: jax.ShapeDtypeStruct((r, c), t)
    pieces = lambda arrays: [held(n, a.shape[1]) for n, d in enumerate(blocks) for a in arrays[d]]
    shapes = [out(all_rows, width), out(all_rows, units), out(all_rows, 2 * units), out(all_rows, width)]
    specs = [everywhere(width), everywhere(units), everywhere(2 * units), everywhere(width)]
    if blocks == (3,):
        shapes += [out(tok, width // 2)] * 4
        specs += [held(0, width // 2)] * 4
    elif blocks == (0,):
        shapes += [out(tok, width)] * 2 + [out(tok, width, F32)]
        specs += [held(0, width)] * 3
    else:
        shapes += [out(tok, width)] * 4
        specs += [held(0, width), held(1, width)] * 2
    diag_specs = [held(1, width // 2), held(0, width // 2)] * 2 if diag else []
    operands = (
        [me] + list(att[:6]) + [a for a, _ in last] + [a for d in blocks for a in xs[d]] + [a for d in blocks for a in cots[d]]
        + [wide, gain, wide, wide, wd] + list(diag) + list(carried) + list(after)
    )
    first = len(operands) - len(carried) - len(after)
    return pl.pallas_call(
        functools.partial(ffn_kernel, per, blocks, len(carried) + len(after)),
        grid=(len(blocks) * per,),
        out_shape=tuple(shapes),
        in_specs=[smem()] + [crossed(d) for d in range(3) for _ in range(2)] + [spec for _, spec in last]
        + pieces(xs) + pieces(cots) + [weight(3), fixed(gain), weight(0), weight(1), fixed(wd)] + diag_specs + anywhere(carried) + anywhere(after),
        out_specs=tuple(specs),
        input_output_aliases={first + n: n for n in range(len(carried))},
        compiler_params=params(),
        cost_estimate=COST,
        name="ffn",
    )(*operands)


def weights_kernel(left_ref, right_ref, out_ref):
    out_ref[...] = dot_tn(left_ref[...], right_ref[...]).astype(BF16)


def weights_back(left, right, steps):
    rows, depth = left.shape
    return pl.pallas_call(
        weights_kernel,
        grid=(steps,),
        out_shape=jax.ShapeDtypeStruct((depth, right.shape[1]), BF16),
        in_specs=[pl.BlockSpec((rows, depth // steps), lambda i: (0, i)), fixed(right)],
        out_specs=pl.BlockSpec((depth // steps, right.shape[1]), lambda i: (i, 0)),
        compiler_params=params(),
        cost_estimate=COST,
        name="weights_back",
    )(left, right)


def middle_kernel(*refs):
    me_ref, dn_refs = refs[0], refs[1:4]
    cot_ref, mid_ref, gain_ref, wo_ref = refs[4:8]
    dmid_ref, branch_ref, da_refs = refs[-6], refs[-5], refs[-4:]
    me = me_ref[0]
    tok = mid_ref.shape[0]

    def rows_of(i, carry):
        rows = at_rows(i)
        middle = mid_ref[rows, :]
        d_normed = dn_refs[0][rows, :].astype(F32)
        for ref in dn_refs[1:]:
            d_normed = d_normed + ref[rows, :].astype(F32)
        r2 = lax.rsqrt(jnp.mean(middle * middle, axis=1, keepdims=True) + EPSILON)
        scaled = d_normed * gain_ref[...]
        pull = jnp.mean(scaled * middle, axis=1, keepdims=True)
        d_middle = cot_ref[rows, :].astype(F32) + r2 * scaled - middle * (r2 * r2 * r2 * pull)
        dmid_ref[rows, :] = d_middle
        branch_ref[rows, :] = d_middle.astype(BF16)
        return carry

    lax.fori_loop(0, tok // ROWS, rows_of, 0)
    span = 2 * LANES
    for d in range(4):
        there = pl.ds(pl.multiple_of(jnp.bitwise_xor(me, d) * span, span), span)
        da_refs[d][...] = dot_nt(branch_ref[...], wo_ref[there, :branch_ref.shape[1]]).astype(BF16)


def out_kernel(me_ref, *refs):
    att_refs, branch_ref, outs = refs[:8], refs[8], refs[9:]
    span = 2 * LANES
    for d in range(4):
        there = pl.ds(pl.multiple_of(jnp.bitwise_xor(me_ref[0], d) * span, span), span)
        rows = jnp.concatenate([att_refs[2 * d][...], att_refs[2 * d + 1][...]], axis=1)
        for e in range(4):
            columns = pl.ds(pl.multiple_of(jnp.bitwise_xor(me_ref[0], e) * span, span), span)
            outs[e][there, :] = dot_tn(rows, branch_ref[:, columns]).astype(BF16)


def out_weights(me, att, branch):
    tok, width = branch.shape
    whole = lambda r, c: pl.BlockSpec((r, c), lambda i: (0, 0))
    own = lambda d: pl.BlockSpec((tok, LANES), lambda i: (d, 0))
    return pl.pallas_call(
        out_kernel,
        grid=(1,),
        out_shape=(jax.ShapeDtypeStruct((width, width // 4), BF16),) * 4,
        in_specs=[smem()] + [own(d) for d in (0, 0, 1, 1, 2, 2, 3, 1)] + [whole(tok, width)],
        out_specs=(whole(width, width // 4),) * 4,
        compiler_params=params(),
        cost_estimate=COST,
        name="out_weights",
    )(me, *att[:7], att[8], branch)


def middle_back(me, parts, cot, middle, gain, wide, after):
    tok, width = middle.shape
    wo = pl.BlockSpec((wide.shape[0], wide.shape[1] // 4), lambda i: (0, 3))
    whole = lambda r, c: pl.BlockSpec((r, c), lambda i: (0, 0))
    out = lambda r, c, t=BF16: jax.ShapeDtypeStruct((r, c), t)
    return pl.pallas_call(
        middle_kernel,
        grid=(1,),
        out_shape=(out(tok, width, F32), out(tok, width)) + (out(tok, 2 * LANES),) * 4,
        in_specs=[smem()] + [whole(tok, width)] * 5 + [whole(1, width), wo] + anywhere(after),
        out_specs=(whole(tok, width),) * 2 + (whole(tok, 2 * LANES),) * 4,
        compiler_params=params(),
        cost_estimate=COST,
        name="middle_back",
    )(me, *parts, cot, middle, gain, wide, *after)


def swap(array, distance):
    return lax.ppermute(array, "seq", [(s, s ^ distance) for s in range(4)])


def gather_rows(block, meanwhile):
    half = block.shape[1] // 2
    one, two = swap(block, 1), swap(block, 2)
    one, two, meanwhile = lax.optimization_barrier((one, two, meanwhile))
    return [meanwhile, [one], [two], [swap(one[:, :half], 2), swap(two[:, half:], 1)]]


def after(value, *others):
    return lax.optimization_barrier((value, others))[0]


def body(
    tokens, order, seq_lengths, attn_gain, w_query, w_key, w_value, query_gain, key_gain,
    w_out, ffn_gain, w_gate, w_up, w_down, cotangent,
):
    tok = tokens.shape[1]
    ways = lax.axis_size("seq")
    shards = lax.axis_size("shard")
    all_rows = tok * ways
    head_dim = query_gain.shape[0]
    me = lax.axis_index("seq")
    me_arr = me.astype(jnp.int32)[None]
    own = lambda a, axis: lax.dynamic_slice_in_dim(a, me * (a.shape[axis] // ways), a.shape[axis] // ways, axis)
    depth = w_gate.shape[0]
    units = w_gate.shape[1] // ways
    piece = units // shards

    cosine, sine_up, sine_down, ocol, orow = make_tables(me_arr, seq_lengths, order, head_dim)
    q_gain = jnp.tile(query_gain.astype(F32), LANES // head_dim)[None, :]
    k_gain = jnp.tile(key_gain.astype(F32), LANES // head_dim)[None, :]

    tables = (cosine, sine_up, sine_down, ocol, orow, q_gain, k_gain)

    xs = gather_rows(tokens[0], tables)
    w_first = first_weights(me_arr, w_query, w_key, w_value, attn_gain, ffn_gain)
    w_qkv = lax.all_gather(w_first, "shard", axis=0, tiled=True)
    w_cut = cut_weights(me_arr, w_gate, w_up, own(w_down, 0).reshape(depth, units), w_out, shards)
    w_wide = lax.all_gather(after(w_cut, xs[1]), "shard", axis=0, tiled=True)
    w_d = w_wide[:, 2 * units:3 * units].reshape(units, -1)

    cosine, sine_up, sine_down, ocol, orow, q_gain, k_gain = xs[0]
    xs = [[tokens[0]]] + xs[1:]
    normed, qx, k, v, vx, kt, rawq, rawk, gains = qkv(
        [x for one in xs for x in one], w_qkv, ocol, cosine, sine_up, sine_down, q_gain, k_gain, head_dim
    )
    cot = cotangent[0]
    cots = gather_rows(after(cot, xs[3]), gains)
    gains, cots = cots[0], [[cot]] + cots[1:]
    gain_a, gain_f = gains[0:1], gains[1:2]
    w_rows = jnp.concatenate(after([w_query, w_key, w_value], xs[3]), axis=1)
    w_all = lax.all_gather(w_rows, "shard", axis=0, tiled=True)

    att, dealts, lses = [], [], []
    for g in range(2):
        given, dealt, lse = attend(g, seq_lengths, orow, qx, k, vx, head_dim, [])
        one, two = swap(given, 1), swap(given, 2)
        half = given.shape[0] // 2
        three = [swap(one[:half], 2), swap(two[half:], 1)] if g else [swap(given, 3)]
        att.append([given, one, two] + three)
        dealts.append(dealt)
        lses.append(lse)
    att = [att[g][d] for d in range(3) for g in range(2)] + att[0][3:] + att[1][3:]

    feed = lambda blocks, diag, carried, after=(): ffn(
        me_arr, blocks, att, xs, cots, gain_f, w_wide, w_d, diag, carried, after
    )
    *carried, dn3a, dn3b, bo3a, bo3b = feed((3,), (), (), att[8:])
    diag = (swap(dn3a, 1), swap(dn3b, 2), swap(bo3a, 1), swap(bo3b, 2))
    *carried, dn0, bo0, middle = feed((0,), (), carried)
    *carried, dn1, dn2, bo1, bo2 = feed((1, 2), diag, carried)
    nf, hidden, d_gu, cot_all = carried
    dn = (dn0, swap(dn1, 1), swap(dn2, 2))
    scatter = lambda a: lax.psum_scatter(a, "shard", scatter_dimension=0, tiled=True)
    p_wd = weights_back(hidden, cot_all, 3)
    p_wgu = weights_back(nf, after(d_gu, p_wd), 4)
    p_wd, p_wgu = after((p_wd, p_wgu), dn)
    d_wd, d_wgu = scatter(p_wd), scatter(p_wgu)

    d_middle, branch, *d_att = middle_back(me_arr, dn, cot, middle, gain_f, w_wide, (p_wd, p_wgu, w_all))
    p_wo = out_weights(me_arr, att, branch)
    d_att = [d_att[0]] + [swap(d_att[d], d) for d in (1, 2, 3)]
    draw, head_gains = attend_back(
        seq_lengths, ocol, qx, k, v, kt, lses, dealts, d_att, rawq, rawk,
        cosine, sine_up, sine_down, q_gain, k_gain, head_dim, (),
    )
    bo1, bo2, *p_wo = after([bo1, bo2] + list(p_wo), d_att)
    bo = [bo0, swap(bo1, 1), swap(bo2, 2)]
    p_wo = [p_wo[0]] + [swap(p_wo[d], d) for d in (1, 2, 3)]
    *d_raw, p_last = rows_back(orow, draw, normed, p_wo, head_gains, shards, bo[1:3] + [d_wd])
    block_out = (middle + sum(b.astype(F32) for b in after(bo, p_last))).astype(BF16)
    d_raw = [d_raw[0]] + [swap(d_raw[d], d) for d in (1, 2, 3)]
    d_last = scatter(after(p_last, d_wgu))
    d_tokens = tokens_back(me_arr, d_raw, w_all, tokens[0], d_middle, gain_a, (p_last,))
    d_wgu, d_wd = after((d_wgu, d_wd), d_raw, p_last)

    def parts_of(part):
        return [part] + [swap(part, d) for d in (1, 2, 3)]

    d_wd = parts_of(d_wd)
    for a, b, which in ((0, 1, me % 2), (2, 3, me % 2), (0, 2, me // 2), (1, 3, me // 2)):
        d_wd[a], d_wd[b] = jnp.where(which == 1, d_wd[b], d_wd[a]), jnp.where(which == 1, d_wd[a], d_wd[b])
    d_wd = jnp.concatenate(d_wd, axis=0).astype(F32)
    d_wg, d_wu, ffn_dots = join_weights(me_arr, parts_of(d_wgu), w_gate, w_up, shards)
    d_wq, d_wk, d_wv, d_wo, attn_dots, head_gains = join_last(
        me_arr, parts_of(after(d_last, d_wgu)), w_query, w_key, w_value, w_out.shape[1]
    )
    d_attn_gain = attn_dots[:, 0] / attn_gain.astype(F32)
    d_ffn_gain = ffn_dots[:, 0] / ffn_gain.astype(F32)
    head_gains = head_gains[0:2, :head_dim] + head_gains[0:2, head_dim:]
    return (
        block_out[None], d_tokens[None], d_attn_gain, d_wq, d_wk, d_wv, head_gains[0], head_gains[1],
        d_wo, d_ffn_gain, d_wg, d_wu, d_wd,
    )


def solution(mesh):
    rows, flat, wide = P("shard", None), P("shard"), P("shard", "seq", None)
    in_specs = (
        wide, rows, rows, flat, rows, rows, rows, P(), P(), rows, flat, rows, rows, rows, wide,
    )
    out_specs = (wide, wide, flat, rows, rows, rows, P(), P(), rows, flat, rows, rows, rows)
    return jax.shard_map(body, mesh=mesh, in_specs=in_specs, out_specs=out_specs, check_vma=False)
```

```python
import functools

import jax
import jax.numpy as jnp
from jax import lax
from jax.experimental import pallas as pl
from jax.experimental.pallas import tpu as pltpu
from jax.sharding import PartitionSpec as P

EPSILON = 1e-05
ROPE_BASE = 1000000.0
LOG2E = 1.4426950408889634
ROWS = 256
LANES = 128
F32 = jnp.float32
BF16 = jnp.bfloat16
COST = pl.CostEstimate(flops=1 << 20, bytes_accessed=1 << 16, transcendentals=0)
VMEM_LIMIT = 58 * 1024 * 1024


def dot_nn(left, right):
    return jnp.dot(left, right, preferred_element_type=F32)


def dot_nt(left, right):
    return lax.dot_general(left, right, (((1,), (1,)), ((), ())), preferred_element_type=F32)


def dot_tn(left, right):
    return lax.dot_general(left, right, (((0,), (0,)), ((), ())), preferred_element_type=F32)


def vmem():
    return pl.BlockSpec(memory_space=pltpu.VMEM)


def smem():
    return pl.BlockSpec(memory_space=pltpu.SMEM)


def params():
    return pltpu.CompilerParams(vmem_limit_bytes=VMEM_LIMIT)


def lane_iota(rows, columns):
    return lax.broadcasted_iota(jnp.int32, (rows, columns), 1)


def row_iota(rows, columns):
    return lax.broadcasted_iota(jnp.int32, (rows, columns), 0)


def at_rows(block, rows=ROWS):
    return pl.ds(pl.multiple_of(block * rows, rows), rows)


def pair_ones(head_dim):
    return (
        row_iota(LANES, LANES) // head_dim == lane_iota(LANES, LANES) // head_dim
    ).astype(BF16)


def head_mean(values, ones, head_dim):
    high = values.astype(BF16)
    low = (values - high.astype(F32)).astype(BF16)
    return (dot_nn(high, ones) + dot_nn(low, ones)) * (1.0 / head_dim)


def turn(values, cosine, sine_up, sine_down, head_dim, sign=1.0):
    half = head_dim // 2
    up = pltpu.roll(values, LANES - half, 1) * sine_up
    down = pltpu.roll(values, half, 1) * sine_down
    return values * cosine + sign * (up + down)


def spread_heads(pair, group, head_dim, low_lanes):
    moved = pltpu.roll(pair, head_dim, 1)
    if group == 0:
        return jnp.where(low_lanes, pair, 0.0), jnp.where(low_lanes, moved, 0.0)
    return jnp.where(low_lanes, 0.0, moved), jnp.where(low_lanes, 0.0, pair)


def first_kernel(me_ref, q_ref, k_ref, v_ref, ga_ref, gf_ref, out_ref):
    at = 0
    for ref in (q_ref, k_ref, v_ref):
        size = ref.shape[1] // 4
        out_ref[:, at:at + size] = ref[:, pl.ds(pl.multiple_of(me_ref[0] * size, size), size)]
        at += size
    depth = out_ref.shape[0]
    row = row_iota(LANES, depth)
    gains = jnp.where(row == 0, ga_ref[...].astype(F32), jnp.where(row == 1, gf_ref[...].astype(F32), 0.0))
    out_ref[:, at:] = jnp.transpose(gains).astype(BF16)


def first_weights(me, w_query, w_key, w_value, attn_gain, ffn_gain):
    depth = w_query.shape[0]
    width = (w_query.shape[1] + w_key.shape[1] + w_value.shape[1]) // 4 + LANES
    return pl.pallas_call(
        first_kernel,
        out_shape=jax.ShapeDtypeStruct((depth, width), BF16),
        in_specs=[smem()] + [vmem()] * 5,
        out_specs=vmem(),
        compiler_params=params(),
        cost_estimate=COST,
        name="first_weights",
    )(me, w_query, w_key, w_value, attn_gain[None], ffn_gain[None])


def pack_rows(block, rows):
    rest = [block[rows:, c:c + LANES] for c in range(0, block.shape[1], LANES)]
    return jnp.concatenate([block[:rows], jnp.concatenate(rest, axis=0)], axis=1)


def unpack_rows(block, width):
    rows = block.shape[0]
    extra = rows * LANES // width
    rest = [block[extra * c:extra * (c + 1), width:] for c in range(width // LANES)]
    return jnp.concatenate([block[:, :width], jnp.concatenate(rest, axis=1)], axis=0)


def cut_kernel(shards, me_ref, gate_ref, up_ref, down_ref, wo_ref, out_ref):
    whole, units = gate_ref.shape[1], gate_ref.shape[1] // 4
    piece, span = units // shards, whole // shards
    for at, ref in ((0, gate_ref), (units, up_ref)):
        turned = pltpu.roll(ref[...].astype(F32), whole - piece * me_ref[0], 1)
        parts = [turned[:, span * k:span * k + piece] for k in range(shards)]
        out_ref[:, at:at + units] = jnp.concatenate(parts, axis=1).astype(BF16)
    out_ref[:, 2 * units:3 * units] = pack_rows(down_ref[...].astype(F32), out_ref.shape[0]).astype(BF16)
    width = wo_ref.shape[1]
    out_ref[:, 3 * units:3 * units + width] = wo_ref[...]
    out_ref[:, 3 * units + width:] = jnp.zeros((out_ref.shape[0], units - width), BF16)


def cut_weights(me, w_gate, w_up, w_down, w_out, shards):
    depth, whole = w_gate.shape
    return pl.pallas_call(
        functools.partial(cut_kernel, shards),
        out_shape=jax.ShapeDtypeStruct((depth, whole), BF16),
        in_specs=[smem()] + [vmem()] * 4,
        out_specs=vmem(),
        compiler_params=params(),
        cost_estimate=COST,
        name="cut_weights",
    )(me, w_gate, w_up, w_down, w_out)


def join_kernel(shards, me_ref, p0_ref, p1_ref, p2_ref, p3_ref, gate_ref, up_ref, dgate_ref, dup_ref, ddown_ref, dot_ref, st_ref):
    for d, ref in enumerate((p0_ref, p1_ref, p2_ref, p3_ref)):
        st_ref[d] = ref[...]
    units = p0_ref.shape[1] // 3
    piece = units // shards
    quarters = [st_ref[jnp.bitwise_xor(me_ref[0], q)] for q in range(4)]
    total = 0.0
    for at, w_ref, out_ref in ((0, gate_ref, dgate_ref), (units, up_ref, dup_ref)):
        parts = [q[:, at:at + units].astype(F32) for q in quarters]
        parts = [q[:, piece * k:piece * (k + 1)] for k in range(shards) for q in parts]
        joined = jnp.concatenate(parts, axis=1)
        out_ref[...] = joined
        total = total + jnp.sum(joined * w_ref[...].astype(F32), axis=1, keepdims=True)
    dot_ref[...] = total
    for q, quarter in enumerate(quarters):
        block = unpack_rows(quarter[:, 2 * units:].astype(F32), ddown_ref.shape[1])
        ddown_ref[q * piece:(q + 1) * piece, :] = block


def join_weights(me, parts, w_gate, w_up, down_shape, shards):
    depth, whole = w_gate.shape
    return pl.pallas_call(
        functools.partial(join_kernel, shards),
        out_shape=(jax.ShapeDtypeStruct((depth, whole), F32),) * 2
        + (jax.ShapeDtypeStruct(down_shape, F32), jax.ShapeDtypeStruct((depth, 1), F32)),
        in_specs=[smem()] + [vmem()] * 6,
        out_specs=(vmem(),) * 4,
        scratch_shapes=[pltpu.VMEM((4,) + parts[0].shape, BF16)],
        compiler_params=params(),
        cost_estimate=COST,
        name="join_weights",
    )(me, *parts, w_gate, w_up)


def join_last_kernel(me_ref, p0_ref, p1_ref, p2_ref, p3_ref, q_ref, k_ref, v_ref,
                     dq_ref, dk_ref, dv_ref, do_ref, dot_ref, gain_ref):
    at = 0
    parts = (p0_ref, p1_ref, p2_ref, p3_ref)
    total = jnp.zeros(dot_ref.shape, F32)
    for out_ref, w_ref in ((dq_ref, q_ref), (dk_ref, k_ref), (dv_ref, v_ref), (do_ref, None)):
        size = out_ref.shape[1] // 4
        for d, ref in enumerate(parts):
            there = pl.ds(pl.multiple_of(jnp.bitwise_xor(me_ref[0], d) * size, size), size)
            part = ref[:, at:at + size].astype(F32)
            out_ref[:, there] = part
            if w_ref is not None:
                total = total + jnp.sum(part * w_ref[:, there].astype(F32), axis=1, keepdims=True)
        at += size
    dot_ref[...] = total
    gains = jnp.zeros(gain_ref.shape, F32)
    for ref in parts:
        gains = gains + ref[0:16, at:].astype(F32)[:8]
    gain_ref[...] = gains


def join_last(me, parts, w_query, w_key, w_value, out_width):
    depth = w_query.shape[0]
    out = lambda c: jax.ShapeDtypeStruct((depth, c), F32)
    return pl.pallas_call(
        join_last_kernel,
        out_shape=(
            out(w_query.shape[1]), out(w_key.shape[1]), out(w_value.shape[1]), out(out_width), out(1),
            jax.ShapeDtypeStruct((8, LANES), F32),
        ),
        in_specs=[smem()] + [vmem()] * 7,
        out_specs=(vmem(),) * 6,
        compiler_params=params(),
        cost_estimate=COST,
        name="join_last",
    )(me, *parts, w_query, w_key, w_value)


def table_kernel(half, me_ref, lens_ref, order_ref, freq_ref, cos_ref, up_ref, down_ref, ocol_ref, orow_ref):
    all_rows = order_ref.shape[1]
    groups = LANES // half
    rows = all_rows // groups
    lane = lane_iota(rows, LANES)
    index = lane // half * rows + row_iota(rows, LANES)
    angles = (index - row_starts(lens_ref, index)).astype(F32) * freq_ref[...]
    cosine, sine = jnp.cos(angles), jnp.sin(angles)
    first = lane % (2 * half) < half
    for q in range(groups):

        def spread(table, q=q):
            one = jnp.where(lane < half, pltpu.roll(table, LANES - half * q, 1) if q else table, 0.0)
            return one + pltpu.roll(one, half, 1) + pltpu.roll(one, 2 * half, 1) + pltpu.roll(one, 3 * half, 1)

        here = slice(q * rows, (q + 1) * rows)
        cos_ref[here, :] = spread(cosine)
        wide = spread(sine)
        up_ref[here, :] = jnp.where(first, -wide, 0.0)
        down_ref[here, :] = jnp.where(first, 0.0, wide)
    relative = jnp.bitwise_xor(order_ref[...], me_ref[0] * (all_rows // 4))
    orow_ref[...] = relative
    for c in range(all_rows // LANES):
        here = slice(c * LANES, (c + 1) * LANES)
        across = jnp.broadcast_to(relative[:, here].astype(F32), (LANES, LANES))
        ocol_ref[here, :] = jnp.transpose(across).astype(jnp.int32)


def make_tables(me, lens, order, head_dim):
    all_rows = order.shape[1]
    half = head_dim // 2
    frequency = ROPE_BASE ** (-2.0 * jnp.arange(half, dtype=F32) / head_dim)
    out = lambda r, c, t: jax.ShapeDtypeStruct((r, c), t)
    return pl.pallas_call(
        functools.partial(table_kernel, half),
        out_shape=(out(all_rows, LANES, F32),) * 3 + (out(all_rows, LANES, jnp.int32), out(1, all_rows, jnp.int32)),
        in_specs=[smem(), smem(), vmem(), vmem()],
        out_specs=(vmem(),) * 5,
        compiler_params=params(),
        cost_estimate=COST,
        name="make_tables",
    )(me, lens, order, jnp.tile(frequency, LANES // half)[None, :])


def qkv_kernel(
    head_dim, x0_ref, x1_ref, x2_ref, x3a_ref, x3b_ref, w_ref, ocol_ref, cos_ref, su_ref, sd_ref,
    qg_ref, kg_ref, normed_ref, qx_ref, k_ref, v_ref, vx_ref, kt_ref, rawq_ref, rawk_ref, gain_ref, raw_ref,
):
    i = pl.program_id(0)
    tok = x0_ref.shape[0]
    all_rows, width = raw_ref.shape
    pairs = rawq_ref.shape[1] // LANES

    @pl.when(i == 0)
    def _():
        gain_ref[...] = jnp.transpose(w_ref[:, width:].astype(F32))[:8]

    def project(x, rows):
        x = x.astype(F32)
        r1 = lax.rsqrt(jnp.mean(x * x, axis=1, keepdims=True) + EPSILON)
        normed = (x * r1 * gain_ref[0:1, :]).astype(BF16)
        normed_ref[...] = normed
        raw_ref[rows, :] = dot_nn(normed, w_ref[:, :width]).astype(BF16)

    for d, refs in enumerate(((x0_ref,), (x1_ref,), (x2_ref,), (x3a_ref, x3b_ref))):

        @pl.when(i == d)
        def _(d=d, refs=refs):
            project(jnp.concatenate([ref[...] for ref in refs], axis=1), slice(d * tok, (d + 1) * tok))

    @pl.when(i >= 4)
    def _():
        ones = pair_ones(head_dim)
        low_lanes = lane_iota(tok, LANES) < head_dim
        pick = (ocol_ref[:, 0:1] == lane_iota(tok, all_rows)).astype(F32).astype(BF16)
        dealt = dot_nn(pick, raw_ref[...])
        cosine, su, sd = cos_ref[...], su_ref[...], sd_ref[...]
        for g in range(pairs):
            raw = dealt[:, g * LANES:(g + 1) * LANES]
            rawq_ref[:, g * LANES:(g + 1) * LANES] = raw.astype(BF16)
            rq = lax.rsqrt(head_mean(raw * raw, ones, head_dim) + EPSILON)
            pair = turn(raw * rq * qg_ref[...], cosine, su, sd, head_dim)
            for r, one in enumerate(spread_heads(pair, g, head_dim, low_lanes)):
                qx_ref[2 * g + r] = one.astype(BF16)
        raw = dealt[:, pairs * LANES:(pairs + 1) * LANES]
        rawk_ref[...] = raw.astype(BF16)
        rk = lax.rsqrt(head_mean(raw * raw, ones, head_dim) + EPSILON)
        keys = turn(raw * rk * kg_ref[...], cosine, su, sd, head_dim)
        k_ref[...] = keys.astype(BF16)
        kt_ref[...] = jnp.transpose(keys).astype(BF16)
        values = dealt[:, (pairs + 1) * LANES:]
        v_ref[...] = values.astype(BF16)
        vx_ref[0] = jnp.where(low_lanes, values, 1.0).astype(BF16)
        vx_ref[1] = jnp.where(low_lanes, 1.0, values).astype(BF16)


def fixed(array):
    return pl.BlockSpec(array.shape, lambda i: (0,) * array.ndim, pipeline_mode=pl.Buffered(1))


def qkv(xs, w, ocol, cosine, su, sd, qg, kg, head_dim):
    tok, width = xs[0].shape
    all_rows = 4 * tok
    out = lambda *dims: jax.ShapeDtypeStruct(dims, BF16)
    late = lambda c: pl.BlockSpec((tok, c), lambda i: (jnp.maximum(i - 4, 0), 0))
    heads = lambda n: pl.BlockSpec((n, tok, LANES), lambda i: (0, jnp.maximum(i - 4, 0), 0))
    return pl.pallas_call(
        functools.partial(qkv_kernel, head_dim),
        grid=(8,),
        out_shape=(
            out(all_rows, width), out(4, all_rows, LANES), out(all_rows, LANES), out(all_rows, LANES),
            out(2, all_rows, LANES), out(LANES, all_rows), out(all_rows, 2 * LANES), out(all_rows, LANES),
            jax.ShapeDtypeStruct((8, width), F32),
        ),
        in_specs=[fixed(x) for x in xs] + [fixed(w)] + [late(LANES)] * 4 + [fixed(qg), fixed(kg)],
        out_specs=(
            pl.BlockSpec((tok, width), lambda i: (jnp.minimum(i, 3), 0)),
            heads(4), late(LANES), late(LANES), heads(2),
            pl.BlockSpec((LANES, tok), lambda i: (0, jnp.maximum(i - 4, 0))), late(2 * LANES), late(LANES),
            pl.BlockSpec((8, width), lambda i: (0, 0)),
        ),
        scratch_shapes=[pltpu.VMEM((all_rows, 4 * LANES), BF16)],
        compiler_params=params(),
        cost_estimate=COST,
        name="qkv",
    )(*xs, w, ocol, cosine, su, sd, qg, kg)


def row_starts(lens_ref, index):
    start = jnp.zeros_like(index)
    end = lens_ref[0, 0]
    for s in range(1, lens_ref.shape[1]):
        start = jnp.where(index >= end, end, start)
        end = end + lens_ref[0, s]
    return start


def attend_kernel(head_dim, group, block, lens_ref, orow_ref, qx_ref, k_ref, vx_ref, *refs):
    given_ref, dealt_ref, lse_ref = refs[-3:]
    all_rows = k_ref.shape[0]
    scale = LOG2E * head_dim ** -0.5
    low_lanes = lane_iota(block, LANES) < head_dim
    mass_row = head_dim if group == 0 else 0

    def query_block(i, carry):
        rows = at_rows(i, block)
        q_index = i * block + row_iota(block, 1)
        start = row_starts(lens_ref, q_index)
        first = row_starts(lens_ref, i * block) // block
        clear = jnp.minimum((row_starts(lens_ref, i * block + block - 1) + block - 1) // block, i)
        queries = [qx_ref[r, rows, :] for r in range(2)]

        def step(j, state, masked):
            columns = at_rows(j, block)
            keys, values = k_ref[columns, :], vx_ref[0, columns, :]
            k_index = j * block + lane_iota(block, block)
            keep = (k_index <= q_index) & (k_index >= start)
            new = []
            for r in range(2):
                weights = jnp.exp2(dot_nt(queries[r], keys) * scale)
                if masked:
                    weights = jnp.where(keep, weights, 0.0)
                new.append(state[r] + dot_nn(weights.astype(BF16), values))
            return tuple(new)

        state = (jnp.zeros((block, LANES), F32),) * 2
        state = lax.fori_loop(first, clear, functools.partial(step, masked=True), state)
        state = lax.fori_loop(clear, i, functools.partial(step, masked=False), state)
        state = step(i, state, True)
        out = []
        for r in range(2):
            lse_ref[r:r + 1, rows] = jnp.log2(jnp.transpose(state[r])[mass_row:mass_row + 1, :])
            out.append(state[r] / pltpu.roll(state[r], head_dim, 1))
        if group == 0:
            pair = jnp.where(low_lanes, out[0], pltpu.roll(out[1], head_dim, 1))
        else:
            pair = jnp.where(low_lanes, pltpu.roll(out[0], head_dim, 1), out[1])
        dealt_ref[rows, :] = pair.astype(BF16)
        return carry

    lax.fori_loop(0, all_rows // block, query_block, 0)

    def undeal(i, carry):
        rows = at_rows(i, block)
        pick = (orow_ref[...] == i * block + row_iota(block, all_rows)).astype(F32).astype(BF16)
        given_ref[rows, :] = dot_nn(pick, dealt_ref[...]).astype(BF16)
        return carry

    lax.fori_loop(0, all_rows // block, undeal, 0)


def attend(group, lens, orow, qx, k, vx, head_dim, after):
    all_rows = k.shape[0]
    whole = lambda *dims: pl.BlockSpec(dims, lambda i: (0,) * len(dims))
    return pl.pallas_call(
        functools.partial(attend_kernel, head_dim, group, all_rows // 4),
        grid=(1,),
        out_shape=(
            jax.ShapeDtypeStruct((all_rows, LANES), BF16),
            jax.ShapeDtypeStruct((all_rows, LANES), BF16),
            jax.ShapeDtypeStruct((2, all_rows), F32),
        ),
        in_specs=[
            smem(), whole(1, all_rows),
            pl.BlockSpec((2, all_rows, LANES), lambda i: (group, 0, 0)),
            whole(all_rows, LANES),
            pl.BlockSpec((1, all_rows, LANES), lambda i: (group, 0, 0)),
        ] + anywhere(after),
        out_specs=(whole(all_rows, LANES), whole(all_rows, LANES), whole(2, all_rows)),
        compiler_params=params(),
        cost_estimate=COST,
        name="attend",
    )(lens, orow, qx, k, vx, *after)


def attend_back_kernel(head_dim, n_late, *refs):
    (lens_ref, ocol_ref, lse0_ref, lse1_ref, o0_ref, o1_ref, d0_ref, d1_ref, d2_ref, d3_ref, qg_ref, kg_ref) = refs[:12]
    late, refs = refs[12:12 + n_late], refs[-(2 + 5 + n_late + 1):]
    draw_ref, gain_ref, dgiven_ref, dx_ref, delta_ref, dk_ref, dv_ref = refs[:7]
    here, sems = refs[7:7 + n_late], refs[7 + n_late]
    qx_ref, k_ref, v_ref, kt_ref, rawq_ref, rawk_ref, cos_ref, su_ref, sd_ref = here
    copies = [pltpu.make_async_copy(late[n], here[n], sems.at[n]) for n in range(n_late)]
    for copy in copies:
        copy.start()
    all_rows = k_ref.shape[0]
    blocks = all_rows // ROWS
    exponent = LOG2E * head_dim ** -0.5
    scale = head_dim ** -0.5
    tok = d0_ref.shape[0]
    for d, ref in enumerate((d0_ref, d1_ref, d2_ref, d3_ref)):
        dgiven_ref[d * tok:(d + 1) * tok, :] = ref[...]
    dk_ref[...] = jnp.zeros_like(dk_ref)
    dv_ref[...] = jnp.zeros_like(dv_ref)
    gain_ref[...] = jnp.zeros_like(gain_ref)

    def deal(i, carry):
        rows = at_rows(i, tok)
        low_lanes = lane_iota(tok, LANES) < head_dim
        pick = (ocol_ref[rows, 0:1] == lane_iota(tok, all_rows)).astype(F32).astype(BF16)
        dealt = dot_nn(pick, dgiven_ref[...])
        for g, o_ref in enumerate((o0_ref, o1_ref)):
            pair = dealt[:, g * LANES:(g + 1) * LANES]
            for r, one in enumerate(spread_heads(pair, g, head_dim, low_lanes)):
                dx_ref[2 * g + r, rows, :] = one.astype(BF16)
            across = jnp.transpose(pair * o_ref[rows, :].astype(F32))
            for r in range(2):
                delta_ref[2 * g + r:2 * g + r + 1, rows] = jnp.sum(
                    across[r * head_dim:(r + 1) * head_dim], axis=0, keepdims=True
                )
        return carry

    lax.fori_loop(0, all_rows // tok, deal, 0)
    for copy in copies:
        copy.wait()
    ones = pair_ones(head_dim)

    def query_block(i, carry):
        rows = at_rows(i)
        q_index = i * ROWS + lane_iota(1, ROWS)
        start = row_starts(lens_ref, q_index)
        first = row_starts(lens_ref, i * ROWS) // ROWS
        count = (i + 2 - first) // 2
        base = jnp.maximum(i + 1 - 2 * count, 0)

        def step(n, state):
            at = base + 2 * n
            columns = pl.ds(pl.multiple_of(at * ROWS, ROWS), 2 * ROWS)
            k_index = at * ROWS + row_iota(2 * ROWS, ROWS)
            keep = (k_index <= q_index) & (k_index >= start)
            keys = k_ref[columns, :]
            values = v_ref[columns, :]
            new = []
            dk, dv = dk_ref[columns, :], dv_ref[columns, :]
            for h in range(4):
                g = h // 2
                queries = qx_ref[h, rows, :]
                grads = dx_ref[h, rows, :]
                lse = (lse0_ref, lse1_ref)[g][h % 2:h % 2 + 1, rows]
                weights = jnp.where(keep, jnp.exp2(dot_nt(keys, queries) * exponent - lse), 0.0)
                d_weights = dot_nt(values, grads)
                d_scores = (weights * (d_weights - delta_ref[h:h + 1, rows])).astype(BF16)
                dv = dv + dot_nn(weights.astype(BF16), grads)
                dk = dk + dot_nn(d_scores, queries)
                new.append(state[h] + dot_nn(kt_ref[g * head_dim:(g + 1) * head_dim, columns], d_scores))
            dk_ref[columns, :] = dk
            dv_ref[columns, :] = dv
            return tuple(new)

        state = lax.fori_loop(0, count, step, (jnp.zeros((head_dim, ROWS), F32),) * 4)
        cosine, su, sd = cos_ref[rows, :], su_ref[rows, :], sd_ref[rows, :]
        for g in range(2):
            pair = jnp.transpose(jnp.concatenate(state[2 * g:2 * g + 2], axis=0)) * scale
            lanes = slice(g * LANES, (g + 1) * LANES)
            draw, gain = norm_back(
                pair, rawq_ref[rows, lanes].astype(F32), qg_ref[...], cosine, su, sd, ones, head_dim
            )
            draw_ref[rows, lanes] = draw
            gain_ref[0:1, :] += gain
        return carry

    lax.fori_loop(0, blocks, query_block, 0)

    def key_block(i, carry):
        rows = at_rows(i, tok)
        cosine, su, sd = cos_ref[rows, :], su_ref[rows, :], sd_ref[rows, :]
        draw, gain = norm_back(
            dk_ref[rows, :] * scale, rawk_ref[rows, :].astype(F32), kg_ref[...], cosine, su, sd, ones, head_dim
        )
        draw_ref[rows, 2 * LANES:3 * LANES] = draw
        draw_ref[rows, 3 * LANES:] = dv_ref[rows, :].astype(BF16)
        gain_ref[1:2, :] += gain
        return carry

    lax.fori_loop(0, all_rows // tok, key_block, 0)


def rows_back_kernel(period, orow_ref, draw_ref, normed_ref, o0_ref, o1_ref, o2_ref, o3_ref, gain_ref, *refs):
    d_refs, out_ref, grad_ref = refs[-6:-2], refs[-2], refs[-1]
    i = pl.program_id(0)
    all_rows, width = draw_ref.shape
    rows = all_rows // 4
    for d, ref in enumerate(d_refs):

        @pl.when(i == d)
        def _(d=d, ref=ref):
            pick = (orow_ref[...] == d * rows + row_iota(rows, all_rows)).astype(F32).astype(BF16)
            grads = dot_nn(pick, draw_ref[...]).astype(BF16)
            grad_ref[d * rows:(d + 1) * rows, :] = grads
            ref[...] = grads

    @pl.when(i >= 4)
    def _():
        extra = o0_ref.shape[1]
        out_ref[:, :width] = dot_tn(normed_ref[...], grad_ref[...]).astype(BF16)
        total = o0_ref[...].astype(F32)
        for ref in (o1_ref, o2_ref, o3_ref):
            total = total + ref[...].astype(F32)
        out_ref[:, width:width + extra] = total.astype(BF16)
        place = row_iota(out_ref.shape[0], LANES) % period
        gains = jnp.where(place == 0, gain_ref[0:1, :], jnp.where(place == 1, gain_ref[1:2, :], 0.0))
        out_ref[:, width + extra:] = gains.astype(BF16)


def norm_back(pair, raw, gain, cosine, su, sd, ones, head_dim):
    pair = pair.astype(BF16).astype(F32)
    u = turn(pair, cosine, su, sd, head_dim, -1.0)
    r = lax.rsqrt(head_mean(raw * raw, ones, head_dim) + EPSILON)
    unit = raw * r
    scaled = u * gain
    draw = r * (scaled - unit * head_mean(scaled * unit, ones, head_dim))
    return draw.astype(BF16), jnp.sum(u * unit, axis=0, keepdims=True)


def anywhere(arrays):
    return [pl.BlockSpec(memory_space=pl.ANY)] * len(arrays)


def attend_back(lens, ocol, qx, k, v, kt, lses, dealts, grads, rawq, rawk, cosine, su, sd, qg, kg, head_dim):
    all_rows = k.shape[0]
    late = (qx, k, v, kt, rawq, rawk, cosine, su, sd)
    return pl.pallas_call(
        functools.partial(attend_back_kernel, head_dim, len(late)),
        out_shape=(
            jax.ShapeDtypeStruct((all_rows, 4 * LANES), BF16),
            jax.ShapeDtypeStruct((2, LANES), F32),
        ),
        in_specs=[smem()] + [vmem()] * 11 + anywhere(late),
        out_specs=(vmem(),) * 2,
        scratch_shapes=[
            pltpu.VMEM((all_rows, 2 * LANES), BF16),
            pltpu.VMEM((4, all_rows, LANES), BF16),
            pltpu.VMEM((4, all_rows), F32),
            pltpu.VMEM((all_rows, LANES), F32),
            pltpu.VMEM((all_rows, LANES), F32),
        ] + [pltpu.VMEM(a.shape, a.dtype) for a in late] + [pltpu.SemaphoreType.DMA((len(late),))],
        compiler_params=params(),
        cost_estimate=COST,
        name="attend_back",
    )(lens, ocol, *lses, *dealts, *grads, qg, kg, *late)


def rows_back(orow, draw, normed, parts, gains, shards, after):
    all_rows, width = draw.shape
    depth, extra = normed.shape[1], parts[0].shape[1]
    tok = all_rows // 4
    late = lambda c: pl.BlockSpec((depth // 4, c), lambda i: (jnp.maximum(i - 4, 0), 0))
    wide = width + extra + LANES
    return pl.pallas_call(
        functools.partial(rows_back_kernel, depth // shards),
        grid=(8,),
        out_shape=(jax.ShapeDtypeStruct((tok, width), BF16),) * 4 + (jax.ShapeDtypeStruct((depth, wide), BF16),),
        in_specs=[fixed(orow), fixed(draw), pl.BlockSpec((all_rows, depth // 4), lambda i: (0, jnp.maximum(i - 4, 0)))]
        + [late(extra)] * 4 + [fixed(gains)] + anywhere(after),
        out_specs=(pl.BlockSpec((tok, width), lambda i: (0, 0)),) * 4 + (late(wide),),
        scratch_shapes=[pltpu.VMEM((all_rows, width), BF16)],
        compiler_params=params(),
        cost_estimate=COST,
        name="rows_back",
    )(orow, draw, normed, *parts, gains, *after)


def tokens_kernel(me_ref, g0_ref, g1_ref, g2_ref, g3_ref, w_ref, x_ref, mid_ref, gain_ref, *refs):
    out_ref = refs[-1]
    me = me_ref[0]
    d_normed = jnp.zeros(x_ref.shape, F32)
    span, width = 2 * LANES, 8 * LANES
    for d, ref in enumerate((g0_ref, g1_ref, g2_ref, g3_ref)):
        other = jnp.bitwise_xor(me, d)
        take = lambda at, size: w_ref[:, pl.ds(pl.multiple_of(at + other * size, size), size)]
        weights = jnp.concatenate([take(0, span), take(width, LANES), take(width + 4 * LANES, LANES)], axis=1)
        d_normed = d_normed + dot_nt(ref[...], weights)
    x = x_ref[...].astype(F32)
    r1 = lax.rsqrt(jnp.mean(x * x, axis=1, keepdims=True) + EPSILON)
    scaled = d_normed * gain_ref[...]
    pull = jnp.mean(scaled * x, axis=1, keepdims=True)
    out_ref[...] = (mid_ref[...] + r1 * scaled - x * (r1 * r1 * r1 * pull)).astype(BF16)


def tokens_back(me, grads, w, x, d_middle, gain, after):
    tok, width = x.shape
    rows = lambda c: pl.BlockSpec((ROWS, c), lambda i: (i, 0))
    return pl.pallas_call(
        tokens_kernel,
        grid=(tok // ROWS,),
        out_shape=jax.ShapeDtypeStruct((tok, width), BF16),
        in_specs=[smem()] + [rows(grads[0].shape[1])] * 4 + [fixed(w), rows(width), rows(width), fixed(gain)] + anywhere(after),
        out_specs=rows(width),
        compiler_params=params(),
        cost_estimate=COST,
        name="tokens_back",
    )(me, *grads, w, x, d_middle, gain, *after)


def ffn_kernel(per, shards, blocks, n_carried, *refs):
    refs = list(refs)
    take = lambda n: [refs.pop(0) for _ in range(n)]
    me_ref = take(1)[0]
    att = [take(2 if d < 3 else 2 * len(blocks)) for d in range(4)]
    xs = [take(2 if d == 3 else 1) for d in blocks]
    cots = [take(2 if d == 3 else 1) for d in blocks]
    wo_ref, gain_ref, wg_ref, wu_ref, wd_ref = take(5)
    diag = take(4) if blocks == (1, 2) else None
    take(n_carried)
    nf_ref, hid_ref, dgu_ref, cot_ref = take(4)
    packed_ref, wd_ref = wd_ref, refs.pop()
    i = pl.program_id(0)
    me = me_ref[0]
    hidden_units = hid_ref.shape[1]
    which = i // per

    @pl.when(i == 0)
    def _():
        rows, piece = packed_ref.shape[0] // shards, wd_ref.shape[0] // shards
        for k in range(shards):
            block = packed_ref[k * rows:(k + 1) * rows, :]
            if piece % 16:
                block = block.astype(F32)
            wd_ref[k * piece:(k + 1) * piece, :] = unpack_rows(block, wd_ref.shape[1]).astype(BF16)

    def read(lists):
        parts = [jnp.concatenate([ref[...] for ref in one], axis=1) for one in lists]
        return parts[0] if len(parts) == 1 else jnp.where(which == 0, parts[0], parts[1])

    middle = read(xs).astype(F32)
    for d in range(4):
        block = read([att[d][2 * n:2 * n + 2] for n in range(len(att[d]) // 2)])
        middle = middle + dot_nn(block, wo_ref[at_rows(jnp.bitwise_xor(me, d), 2 * LANES), :middle.shape[1]])
    r2 = lax.rsqrt(jnp.mean(middle * middle, axis=1, keepdims=True) + EPSILON)
    nf = (middle * r2 * gain_ref[...]).astype(BF16)
    nf_ref[...] = nf
    cot = read(cots)
    cot_ref[...] = cot
    wg, wu = wg_ref[...], wu_ref[...]
    gate = dot_nn(nf, wg)
    up = dot_nn(nf, wu)
    s = jax.nn.sigmoid(gate)
    silu = gate * s
    hidden = (silu * up).astype(BF16)
    hid_ref[...] = hidden
    d_hidden = dot_nt(cot, wd_ref[...])
    d_gate = (d_hidden * up * s * (1.0 + gate * (1.0 - s))).astype(BF16)
    d_up = (d_hidden * silu).astype(BF16)
    dgu_ref[:, :hidden_units] = d_gate
    dgu_ref[:, hidden_units:] = d_up
    dn = dot_nt(d_gate, wg) + dot_nt(d_up, wu)
    bo = dot_nn(hidden, wd_ref[...])
    half = dn.shape[1] // 2
    if blocks == (3,):
        for ref, value in zip(take(4), (dn[:, :half], dn[:, half:], bo[:, :half], bo[:, half:])):
            ref[...] = value.astype(BF16)
    elif blocks == (0,):
        dn_ref, bo_ref, mid_ref = take(3)
        dn_ref[...] = dn.astype(BF16)
        bo_ref[...] = bo.astype(BF16)
        mid_ref[...] = middle
    else:
        dn1_ref, dn2_ref, bo1_ref, bo2_ref = take(4)

        @pl.when(which == 0)
        def _():
            for ref, value, extra in ((dn1_ref, dn, diag[1]), (bo1_ref, bo, diag[3])):
                ref[:, :half] = value[:, :half].astype(BF16)
                ref[:, half:] = (value[:, half:] + extra[...].astype(F32)).astype(BF16)

        @pl.when(which == 1)
        def _():
            for ref, value, extra in ((dn2_ref, dn, diag[0]), (bo2_ref, bo, diag[2])):
                ref[:, :half] = (value[:, :half] + extra[...].astype(F32)).astype(BF16)
                ref[:, half:] = value[:, half:].astype(BF16)


def ffn(me, blocks, att, xs, cots, gain, wide, shards, diag, carried, after):
    all_rows = att[0].shape[0]
    units, width = wide.shape[1] // 4, wide.shape[0]
    tok = all_rows // 4
    per = tok // ROWS
    block_of = lambda i: blocks[0] + (i // per) * (blocks[-1] - blocks[0])
    everywhere = lambda c: pl.BlockSpec((ROWS, c), lambda i: (block_of(i) * per + i % per, 0))
    crossed = lambda d: pl.BlockSpec(
        (ROWS, LANES), lambda i: (jnp.bitwise_xor(block_of(i), d) * per + i % per, 0)
    )
    held = lambda n, c: pl.BlockSpec((ROWS, c), lambda i: (jnp.clip(i - n * per, 0, per - 1), 0))
    halves = {0: 1, 1: 1, 2: 0, 3: 0}
    last = []
    for n, d in enumerate(blocks):
        local = lambda i, n=n, d=d: ((3 - d) % 2 * per + jnp.clip(i - n * per, 0, per - 1), 0)
        last += [(att[6], crossed(3)), (att[7 + halves[d]], pl.BlockSpec((ROWS, LANES), local))]
    weight = lambda n: pl.BlockSpec((wide.shape[0], units), lambda i: (0, n), pipeline_mode=pl.Buffered(1))
    out = lambda r, c, t=BF16: jax.ShapeDtypeStruct((r, c), t)
    pieces = lambda arrays: [held(n, a.shape[1]) for n, d in enumerate(blocks) for a in arrays[d]]
    shapes = [out(all_rows, width), out(all_rows, units), out(all_rows, 2 * units), out(all_rows, width)]
    specs = [everywhere(width), everywhere(units), everywhere(2 * units), everywhere(width)]
    if blocks == (3,):
        shapes += [out(tok, width // 2)] * 4
        specs += [held(0, width // 2)] * 4
    elif blocks == (0,):
        shapes += [out(tok, width)] * 2 + [out(tok, width, F32)]
        specs += [held(0, width)] * 3
    else:
        shapes += [out(tok, width)] * 4
        specs += [held(0, width), held(1, width)] * 2
    diag_specs = [held(1, width // 2), held(0, width // 2)] * 2 if diag else []
    operands = (
        [me] + list(att[:6]) + [a for a, _ in last] + [a for d in blocks for a in xs[d]] + [a for d in blocks for a in cots[d]]
        + [wide, gain, wide, wide, wide] + list(diag) + list(carried) + list(after)
    )
    first = len(operands) - len(carried) - len(after)
    return pl.pallas_call(
        functools.partial(ffn_kernel, per, shards, blocks, len(carried) + len(after)),
        grid=(len(blocks) * per,),
        out_shape=tuple(shapes),
        in_specs=[smem()] + [crossed(d) for d in range(3) for _ in range(2)] + [spec for _, spec in last]
        + pieces(xs) + pieces(cots) + [weight(3), fixed(gain), weight(0), weight(1), weight(2)] + diag_specs + anywhere(carried) + anywhere(after),
        out_specs=tuple(specs),
        input_output_aliases={first + n: n for n in range(len(carried))},
        scratch_shapes=[pltpu.VMEM((units, width), BF16)],
        compiler_params=params(),
        cost_estimate=COST,
        name="ffn",
    )(*operands)


def weights_kernel(shards, nf_ref, dgu_ref, hid_ref, cot_ref, out_ref, down_ref):
    i = pl.program_id(0)

    @pl.when(i == 0)
    def _():
        down_ref[...] = dot_tn(hid_ref[...], cot_ref[...])

    @pl.when(i > 0)
    def _():
        out_ref[:, :dgu_ref.shape[1]] = dot_tn(nf_ref[...], dgu_ref[...]).astype(BF16)

    per, piece = shards // 4, down_ref.shape[0] // shards
    rows = out_ref.shape[0] // per
    for k in range(shards):

        @pl.when(i == 1 + k // per)
        def _(k=k):
            block = pack_rows(down_ref[k * piece:(k + 1) * piece, :], rows)
            at = k % per * rows
            out_ref[at:at + rows, dgu_ref.shape[1]:] = block.astype(BF16)


def weights_back(nf, d_gu, hidden, cot, shards):
    rows, depth = nf.shape
    late = lambda i: jnp.maximum(i - 1, 0)
    wide = d_gu.shape[1] + hidden.shape[1]
    return pl.pallas_call(
        functools.partial(weights_kernel, shards),
        grid=(5,),
        out_shape=jax.ShapeDtypeStruct((depth, wide), BF16),
        in_specs=[pl.BlockSpec((rows, depth // 4), lambda i: (0, late(i))), fixed(d_gu), fixed(hidden), fixed(cot)],
        out_specs=pl.BlockSpec((depth // 4, wide), lambda i: (late(i), 0)),
        scratch_shapes=[pltpu.VMEM((hidden.shape[1], cot.shape[1]), F32)],
        compiler_params=params(),
        cost_estimate=COST,
        name="weights_back",
    )(nf, d_gu, hidden, cot)


def middle_kernel(*refs):
    me_ref, dn_refs = refs[0], refs[1:4]
    cot_ref, mid_ref, gain_ref, wo_ref = refs[4:8]
    dmid_ref, branch_ref, da_refs = refs[-6], refs[-5], refs[-4:]
    me = me_ref[0]
    tok = mid_ref.shape[0]

    def rows_of(i, carry):
        rows = at_rows(i)
        middle = mid_ref[rows, :]
        d_normed = dn_refs[0][rows, :].astype(F32)
        for ref in dn_refs[1:]:
            d_normed = d_normed + ref[rows, :].astype(F32)
        r2 = lax.rsqrt(jnp.mean(middle * middle, axis=1, keepdims=True) + EPSILON)
        scaled = d_normed * gain_ref[...]
        pull = jnp.mean(scaled * middle, axis=1, keepdims=True)
        d_middle = cot_ref[rows, :].astype(F32) + r2 * scaled - middle * (r2 * r2 * r2 * pull)
        dmid_ref[rows, :] = d_middle
        branch_ref[rows, :] = d_middle.astype(BF16)
        return carry

    lax.fori_loop(0, tok // ROWS, rows_of, 0)
    span = 2 * LANES
    for d in range(4):
        there = pl.ds(pl.multiple_of(jnp.bitwise_xor(me, d) * span, span), span)
        da_refs[d][...] = dot_nt(branch_ref[...], wo_ref[there, :branch_ref.shape[1]]).astype(BF16)


def out_kernel(me_ref, *refs):
    att_refs, branch_ref, outs = refs[:8], refs[8], refs[9:]
    span = 2 * LANES
    for d in range(4):
        there = pl.ds(pl.multiple_of(jnp.bitwise_xor(me_ref[0], d) * span, span), span)
        rows = jnp.concatenate([att_refs[2 * d][...], att_refs[2 * d + 1][...]], axis=1)
        for e in range(4):
            columns = pl.ds(pl.multiple_of(jnp.bitwise_xor(me_ref[0], e) * span, span), span)
            outs[e][there, :] = dot_tn(rows, branch_ref[:, columns]).astype(BF16)


def out_weights(me, att, branch):
    tok, width = branch.shape
    whole = lambda r, c: pl.BlockSpec((r, c), lambda i: (0, 0))
    own = lambda d: pl.BlockSpec((tok, LANES), lambda i: (d, 0))
    return pl.pallas_call(
        out_kernel,
        grid=(1,),
        out_shape=(jax.ShapeDtypeStruct((width, width // 4), BF16),) * 4,
        in_specs=[smem()] + [own(d) for d in (0, 0, 1, 1, 2, 2, 3, 1)] + [whole(tok, width)],
        out_specs=(whole(width, width // 4),) * 4,
        compiler_params=params(),
        cost_estimate=COST,
        name="out_weights",
    )(me, *att[:7], att[8], branch)


def middle_back(me, parts, cot, middle, gain, wide, after):
    tok, width = middle.shape
    wo = pl.BlockSpec((wide.shape[0], wide.shape[1] // 4), lambda i: (0, 3))
    whole = lambda r, c: pl.BlockSpec((r, c), lambda i: (0, 0))
    out = lambda r, c, t=BF16: jax.ShapeDtypeStruct((r, c), t)
    return pl.pallas_call(
        middle_kernel,
        grid=(1,),
        out_shape=(out(tok, width, F32), out(tok, width)) + (out(tok, 2 * LANES),) * 4,
        in_specs=[smem()] + [whole(tok, width)] * 5 + [whole(1, width), wo] + anywhere(after),
        out_specs=(whole(tok, width),) * 2 + (whole(tok, 2 * LANES),) * 4,
        compiler_params=params(),
        cost_estimate=COST,
        name="middle_back",
    )(me, *parts, cot, middle, gain, wide, *after)


def swap(array, distance):
    return lax.ppermute(array, "seq", [(s, s ^ distance) for s in range(4)])


def gather_rows(block, meanwhile):
    half = block.shape[1] // 2
    one, two = swap(block, 1), swap(block, 2)
    one, two, meanwhile = lax.optimization_barrier((one, two, meanwhile))
    return [meanwhile, [one], [two], [swap(one[:, :half], 2), swap(two[:, half:], 1)]]


def after(value, *others):
    return lax.optimization_barrier((value, others))[0]


def body(
    tokens, order, seq_lengths, attn_gain, w_query, w_key, w_value, query_gain, key_gain,
    w_out, ffn_gain, w_gate, w_up, w_down, cotangent,
):
    tok = tokens.shape[1]
    ways = lax.axis_size("seq")
    shards = lax.axis_size("shard")
    all_rows = tok * ways
    head_dim = query_gain.shape[0]
    me = lax.axis_index("seq")
    me_arr = me.astype(jnp.int32)[None]
    own = lambda a, axis: lax.dynamic_slice_in_dim(a, me * (a.shape[axis] // ways), a.shape[axis] // ways, axis)
    depth = w_gate.shape[0]
    units = w_gate.shape[1] // ways
    piece = units // shards

    cosine, sine_up, sine_down, ocol, orow = make_tables(me_arr, seq_lengths, order, head_dim)
    q_gain = jnp.tile(query_gain.astype(F32), LANES // head_dim)[None, :]
    k_gain = jnp.tile(key_gain.astype(F32), LANES // head_dim)[None, :]

    tables = (cosine, sine_up, sine_down, ocol, orow, q_gain, k_gain)

    xs = gather_rows(tokens[0], tables)
    w_first = first_weights(me_arr, w_query, w_key, w_value, attn_gain, ffn_gain)
    w_qkv = lax.all_gather(w_first, "shard", axis=0, tiled=True)
    w_cut = cut_weights(me_arr, w_gate, w_up, own(w_down, 0), w_out, shards)
    w_wide = lax.all_gather(after(w_cut, xs[1]), "shard", axis=0, tiled=True)

    cosine, sine_up, sine_down, ocol, orow, q_gain, k_gain = xs[0]
    xs = [[tokens[0]]] + xs[1:]
    normed, qx, k, v, vx, kt, rawq, rawk, gains = qkv(
        [x for one in xs for x in one], w_qkv, ocol, cosine, sine_up, sine_down, q_gain, k_gain, head_dim
    )
    cot = cotangent[0]
    cots = gather_rows(after(cot, xs[3]), gains)
    gains, cots = cots[0], [[cot]] + cots[1:]
    gain_a, gain_f = gains[0:1], gains[1:2]
    w_rows = jnp.concatenate(after([w_query, w_key, w_value], xs[3]), axis=1)
    w_all = lax.all_gather(w_rows, "shard", axis=0, tiled=True)

    att, dealts, lses = [], [], []
    for g in range(2):
        given, dealt, lse = attend(g, seq_lengths, orow, qx, k, vx, head_dim, [])
        one, two = swap(given, 1), swap(given, 2)
        half = given.shape[0] // 2
        three = [swap(one[:half], 2), swap(two[half:], 1)] if g else [swap(given, 3)]
        att.append([given, one, two] + three)
        dealts.append(dealt)
        lses.append(lse)
    att = [att[g][d] for d in range(3) for g in range(2)] + att[0][3:] + att[1][3:]

    feed = lambda blocks, diag, carried, after=(): ffn(
        me_arr, blocks, att, xs, cots, gain_f, w_wide, shards, diag, carried, after
    )
    *carried, dn3a, dn3b, bo3a, bo3b = feed((3,), (), (), att[8:])
    diag = (swap(dn3a, 1), swap(dn3b, 2), swap(bo3a, 1), swap(bo3b, 2))
    *carried, dn0, bo0, middle = feed((0,), (), carried)
    *carried, dn1, dn2, bo1, bo2 = feed((1, 2), diag, carried)
    nf, hidden, d_gu, cot_all = carried
    dn = (dn0, swap(dn1, 1), swap(dn2, 2))
    scatter = lambda a: lax.psum_scatter(a, "shard", scatter_dimension=0, tiled=True)
    p_ffn = weights_back(nf, d_gu, hidden, cot_all, shards)
    d_ffn = scatter(after(p_ffn, dn))

    d_middle, branch, *d_att = middle_back(me_arr, dn, cot, middle, gain_f, w_wide, (p_ffn, w_all))
    p_wo = out_weights(me_arr, att, branch)
    d_att = [d_att[0]] + [swap(d_att[d], d) for d in (1, 2, 3)]
    draw, head_gains = attend_back(
        seq_lengths, ocol, qx, k, v, kt, lses, dealts, d_att, rawq, rawk,
        cosine, sine_up, sine_down, q_gain, k_gain, head_dim,
    )
    bo1, bo2, *p_wo = after([bo1, bo2] + list(p_wo), d_att)
    bo = [bo0, swap(bo1, 1), swap(bo2, 2)]
    p_wo = [p_wo[0]] + [swap(p_wo[d], d) for d in (1, 2, 3)]
    *d_raw, p_last = rows_back(orow, draw, normed, p_wo, head_gains, shards, bo[1:3])
    block_out = (middle + sum(b.astype(F32) for b in after(bo, p_last))).astype(BF16)
    d_raw = [d_raw[0]] + [swap(d_raw[d], d) for d in (1, 2, 3)]
    d_last = scatter(after(p_last, d_ffn))
    d_tokens = tokens_back(me_arr, d_raw, w_all, tokens[0], d_middle, gain_a, (p_last,))
    d_ffn = after(d_ffn, d_raw, p_last)

    def parts_of(part):
        return [part] + [swap(part, d) for d in (1, 2, 3)]

    d_wg, d_wu, d_wd, ffn_dots = join_weights(me_arr, parts_of(d_ffn), w_gate, w_up, w_down.shape, shards)
    d_wq, d_wk, d_wv, d_wo, attn_dots, head_gains = join_last(
        me_arr, parts_of(after(d_last, d_ffn, d_tokens, block_out)), w_query, w_key, w_value, w_out.shape[1]
    )
    d_attn_gain = attn_dots[:, 0] / attn_gain.astype(F32)
    d_ffn_gain = ffn_dots[:, 0] / ffn_gain.astype(F32)
    head_gains = head_gains[0:2, :head_dim] + head_gains[0:2, head_dim:]
    return (
        block_out[None], d_tokens[None], d_attn_gain, d_wq, d_wk, d_wv, head_gains[0], head_gains[1],
        d_wo, d_ffn_gain, d_wg, d_wu, d_wd,
    )


def solution(mesh):
    rows, flat, wide = P("shard", None), P("shard"), P("shard", "seq", None)
    in_specs = (
        wide, rows, rows, flat, rows, rows, rows, P(), P(), rows, flat, rows, rows, rows, wide,
    )
    out_specs = (wide, wide, flat, rows, rows, rows, P(), P(), rows, flat, rows, rows, rows)
    return jax.shard_map(body, mesh=mesh, in_specs=in_specs, out_specs=out_specs, check_vma=False)
```

```python
import functools

import jax
import jax.numpy as jnp
from jax import lax
from jax.experimental import pallas as pl
from jax.experimental.pallas import tpu as pltpu
from jax.sharding import PartitionSpec as P

EPSILON = 1e-05
ROPE_BASE = 1000000.0
LOG2E = 1.4426950408889634
ROWS = 256
LANES = 128
F32 = jnp.float32
BF16 = jnp.bfloat16
COST = pl.CostEstimate(flops=1 << 20, bytes_accessed=1 << 16, transcendentals=0)
VMEM_LIMIT = 58 * 1024 * 1024


def dot_nn(left, right):
    return jnp.dot(left, right, preferred_element_type=F32)


def dot_nt(left, right):
    return lax.dot_general(left, right, (((1,), (1,)), ((), ())), preferred_element_type=F32)


def dot_tn(left, right):
    return lax.dot_general(left, right, (((0,), (0,)), ((), ())), preferred_element_type=F32)


def vmem():
    return pl.BlockSpec(memory_space=pltpu.VMEM)


def smem():
    return pl.BlockSpec(memory_space=pltpu.SMEM)


def params():
    return pltpu.CompilerParams(vmem_limit_bytes=VMEM_LIMIT)


def lane_iota(rows, columns):
    return lax.broadcasted_iota(jnp.int32, (rows, columns), 1)


def row_iota(rows, columns):
    return lax.broadcasted_iota(jnp.int32, (rows, columns), 0)


def at_rows(block, rows=ROWS):
    return pl.ds(pl.multiple_of(block * rows, rows), rows)


def pair_ones(head_dim):
    return (
        row_iota(LANES, LANES) // head_dim == lane_iota(LANES, LANES) // head_dim
    ).astype(BF16)


def head_mean(values, ones, head_dim):
    high = values.astype(BF16)
    low = (values - high.astype(F32)).astype(BF16)
    return (dot_nn(high, ones) + dot_nn(low, ones)) * (1.0 / head_dim)


def turn(values, cosine, sine_up, sine_down, head_dim, sign=1.0):
    half = head_dim // 2
    up = pltpu.roll(values, LANES - half, 1) * sine_up
    down = pltpu.roll(values, half, 1) * sine_down
    return values * cosine + sign * (up + down)


def spread_heads(pair, group, head_dim, low_lanes):
    moved = pltpu.roll(pair, head_dim, 1)
    if group == 0:
        return jnp.where(low_lanes, pair, 0.0), jnp.where(low_lanes, moved, 0.0)
    return jnp.where(low_lanes, 0.0, moved), jnp.where(low_lanes, 0.0, pair)


def first_kernel(me_ref, q_ref, k_ref, v_ref, ga_ref, gf_ref, out_ref):
    at = 0
    for ref in (q_ref, k_ref, v_ref):
        size = ref.shape[1] // 4
        out_ref[:, at:at + size] = ref[:, pl.ds(pl.multiple_of(me_ref[0] * size, size), size)]
        at += size
    depth = out_ref.shape[0]
    row = row_iota(LANES, depth)
    gains = jnp.where(row == 0, ga_ref[...].astype(F32), jnp.where(row == 1, gf_ref[...].astype(F32), 0.0))
    out_ref[:, at:] = jnp.transpose(gains).astype(BF16)


def first_weights(me, w_query, w_key, w_value, attn_gain, ffn_gain):
    depth = w_query.shape[0]
    width = (w_query.shape[1] + w_key.shape[1] + w_value.shape[1]) // 4 + LANES
    return pl.pallas_call(
        first_kernel,
        out_shape=jax.ShapeDtypeStruct((depth, width), BF16),
        in_specs=[smem()] + [vmem()] * 5,
        out_specs=vmem(),
        compiler_params=params(),
        cost_estimate=COST,
        name="first_weights",
    )(me, w_query, w_key, w_value, attn_gain[None], ffn_gain[None])


def pack_rows(block, rows):
    rest = [block[rows:, c:c + LANES] for c in range(0, block.shape[1], LANES)]
    return jnp.concatenate([block[:rows], jnp.concatenate(rest, axis=0)], axis=1)


def unpack_rows(block, width):
    rows = block.shape[0]
    extra = rows * LANES // width
    rest = [block[extra * c:extra * (c + 1), width:] for c in range(width // LANES)]
    return jnp.concatenate([block[:, :width], jnp.concatenate(rest, axis=1)], axis=0)


def cut_kernel(shards, me_ref, gate_ref, up_ref, down_ref, wo_ref, out_ref):
    whole, units = gate_ref.shape[1], gate_ref.shape[1] // 4
    piece, span = units // shards, whole // shards
    for at, ref in ((0, gate_ref), (units, up_ref)):
        turned = pltpu.roll(ref[...].astype(F32), whole - piece * me_ref[0], 1)
        parts = [turned[:, span * k:span * k + piece] for k in range(shards)]
        out_ref[:, at:at + units] = jnp.concatenate(parts, axis=1).astype(BF16)
    out_ref[:, 2 * units:3 * units] = pack_rows(down_ref[...].astype(F32), out_ref.shape[0]).astype(BF16)
    width = wo_ref.shape[1]
    out_ref[:, 3 * units:3 * units + width] = wo_ref[...]
    out_ref[:, 3 * units + width:] = jnp.zeros((out_ref.shape[0], units - width), BF16)


def cut_weights(me, w_gate, w_up, w_down, w_out, shards):
    depth, whole = w_gate.shape
    return pl.pallas_call(
        functools.partial(cut_kernel, shards),
        out_shape=jax.ShapeDtypeStruct((depth, whole), BF16),
        in_specs=[smem()] + [vmem()] * 4,
        out_specs=vmem(),
        compiler_params=params(),
        cost_estimate=COST,
        name="cut_weights",
    )(me, w_gate, w_up, w_down, w_out)


def divided_row(column, gain_ref):
    across = jnp.transpose(jnp.broadcast_to(column, (column.shape[0], LANES)))
    return across[0:1, :] / gain_ref[...].astype(F32)


def join_kernel(shards, me_ref, p0_ref, p1_ref, p2_ref, p3_ref, gate_ref, up_ref, gain_ref, dgate_ref, dup_ref, ddown_ref, dot_ref, st_ref):
    for d, ref in enumerate((p0_ref, p1_ref, p2_ref, p3_ref)):
        st_ref[d] = ref[...]
    units = p0_ref.shape[1] // 3
    piece = units // shards
    quarters = [st_ref[jnp.bitwise_xor(me_ref[0], q)] for q in range(4)]
    total = 0.0
    for at, w_ref, out_ref in ((0, gate_ref, dgate_ref), (units, up_ref, dup_ref)):
        parts = [q[:, at:at + units].astype(F32) for q in quarters]
        parts = [q[:, piece * k:piece * (k + 1)] for k in range(shards) for q in parts]
        joined = jnp.concatenate(parts, axis=1)
        out_ref[...] = joined
        total = total + jnp.sum(joined * w_ref[...].astype(F32), axis=1, keepdims=True)
    dot_ref[...] = divided_row(total, gain_ref)
    for q, quarter in enumerate(quarters):
        block = unpack_rows(quarter[:, 2 * units:].astype(F32), ddown_ref.shape[1])
        ddown_ref[q * piece:(q + 1) * piece, :] = block


def join_weights(me, parts, w_gate, w_up, gain, down_shape, shards):
    depth, whole = w_gate.shape
    return pl.pallas_call(
        functools.partial(join_kernel, shards),
        out_shape=(jax.ShapeDtypeStruct((depth, whole), F32),) * 2
        + (jax.ShapeDtypeStruct(down_shape, F32), jax.ShapeDtypeStruct((1, depth), F32)),
        in_specs=[smem()] + [vmem()] * 7,
        out_specs=(vmem(),) * 4,
        scratch_shapes=[pltpu.VMEM((4,) + parts[0].shape, BF16)],
        compiler_params=params(),
        cost_estimate=COST,
        name="join_weights",
    )(me, *parts, w_gate, w_up, gain[None])


def join_last_kernel(me_ref, p0_ref, p1_ref, p2_ref, p3_ref, q_ref, k_ref, v_ref, gain_ref,
                     dq_ref, dk_ref, dv_ref, do_ref, dot_ref, qgain_ref, kgain_ref):
    at = 0
    parts = (p0_ref, p1_ref, p2_ref, p3_ref)
    total = jnp.zeros((dq_ref.shape[0], 1), F32)
    for out_ref, w_ref in ((dq_ref, q_ref), (dk_ref, k_ref), (dv_ref, v_ref), (do_ref, None)):
        size = out_ref.shape[1] // 4
        for d, ref in enumerate(parts):
            there = pl.ds(pl.multiple_of(jnp.bitwise_xor(me_ref[0], d) * size, size), size)
            part = ref[:, at:at + size].astype(F32)
            out_ref[:, there] = part
            if w_ref is not None:
                total = total + jnp.sum(part * w_ref[:, there].astype(F32), axis=1, keepdims=True)
        at += size
    dot_ref[...] = divided_row(total, gain_ref)
    gains = jnp.zeros((8, LANES), F32)
    for ref in parts:
        gains = gains + ref[0:16, at:].astype(F32)[:8]
    head_dim = qgain_ref.shape[1]
    gains = gains[:, :head_dim] + gains[:, head_dim:]
    qgain_ref[...] = gains[0:1]
    kgain_ref[...] = gains[1:2]


def join_last(me, parts, w_query, w_key, w_value, gain, out_width, head_dim):
    depth = w_query.shape[0]
    out = lambda c: jax.ShapeDtypeStruct((depth, c), F32)
    return pl.pallas_call(
        join_last_kernel,
        out_shape=(
            out(w_query.shape[1]), out(w_key.shape[1]), out(w_value.shape[1]), out(out_width),
            jax.ShapeDtypeStruct((1, depth), F32),
        ) + (jax.ShapeDtypeStruct((1, head_dim), F32),) * 2,
        in_specs=[smem()] + [vmem()] * 8,
        out_specs=(vmem(),) * 7,
        compiler_params=params(),
        cost_estimate=COST,
        name="join_last",
    )(me, *parts, w_query, w_key, w_value, gain[None])


def table_kernel(half, me_ref, lens_ref, order_ref, freq_ref, cos_ref, up_ref, down_ref, ocol_ref, orow_ref):
    all_rows = order_ref.shape[1]
    groups = LANES // half
    rows = all_rows // groups
    lane = lane_iota(rows, LANES)
    index = lane // half * rows + row_iota(rows, LANES)
    angles = (index - row_starts(lens_ref, index)).astype(F32) * freq_ref[...]
    cosine, sine = jnp.cos(angles), jnp.sin(angles)
    first = lane % (2 * half) < half
    for q in range(groups):

        def spread(table, q=q):
            one = jnp.where(lane < half, pltpu.roll(table, LANES - half * q, 1) if q else table, 0.0)
            return one + pltpu.roll(one, half, 1) + pltpu.roll(one, 2 * half, 1) + pltpu.roll(one, 3 * half, 1)

        here = slice(q * rows, (q + 1) * rows)
        cos_ref[here, :] = spread(cosine)
        wide = spread(sine)
        up_ref[here, :] = jnp.where(first, -wide, 0.0)
        down_ref[here, :] = jnp.where(first, 0.0, wide)
    relative = jnp.bitwise_xor(order_ref[...], me_ref[0] * (all_rows // 4))
    orow_ref[...] = relative
    for c in range(all_rows // LANES):
        here = slice(c * LANES, (c + 1) * LANES)
        across = jnp.broadcast_to(relative[:, here].astype(F32), (LANES, LANES))
        ocol_ref[here, :] = jnp.transpose(across).astype(jnp.int32)


def make_tables(me, lens, order, head_dim):
    all_rows = order.shape[1]
    half = head_dim // 2
    frequency = ROPE_BASE ** (-2.0 * jnp.arange(half, dtype=F32) / head_dim)
    out = lambda r, c, t: jax.ShapeDtypeStruct((r, c), t)
    return pl.pallas_call(
        functools.partial(table_kernel, half),
        out_shape=(out(all_rows, LANES, F32),) * 3 + (out(all_rows, LANES, jnp.int32), out(1, all_rows, jnp.int32)),
        in_specs=[smem(), smem(), vmem(), vmem()],
        out_specs=(vmem(),) * 5,
        compiler_params=params(),
        cost_estimate=COST,
        name="make_tables",
    )(me, lens, order, jnp.tile(frequency, LANES // half)[None, :])


def qkv_kernel(
    head_dim, x0_ref, x1_ref, x2_ref, x3a_ref, x3b_ref, w_ref, ocol_ref, cos_ref, su_ref, sd_ref,
    qg_ref, kg_ref, normed_ref, qx_ref, k_ref, v_ref, vx_ref, kt_ref, rawq_ref, rawk_ref, gain_ref, raw_ref,
):
    i = pl.program_id(0)
    tok = x0_ref.shape[0]
    all_rows, width = raw_ref.shape
    pairs = rawq_ref.shape[1] // LANES

    @pl.when(i == 0)
    def _():
        gain_ref[...] = jnp.transpose(w_ref[:, width:].astype(F32))[:8]

    def project(x, rows):
        x = x.astype(F32)
        r1 = lax.rsqrt(jnp.mean(x * x, axis=1, keepdims=True) + EPSILON)
        normed = (x * r1 * gain_ref[0:1, :]).astype(BF16)
        normed_ref[...] = normed
        raw_ref[rows, :] = dot_nn(normed, w_ref[:, :width]).astype(BF16)

    for d, refs in enumerate(((x0_ref,), (x1_ref,), (x2_ref,), (x3a_ref, x3b_ref))):

        @pl.when(i == d)
        def _(d=d, refs=refs):
            project(jnp.concatenate([ref[...] for ref in refs], axis=1), slice(d * tok, (d + 1) * tok))

    @pl.when(i >= 4)
    def _():
        ones = pair_ones(head_dim)
        low_lanes = lane_iota(tok, LANES) < head_dim
        pick = (ocol_ref[:, 0:1] == lane_iota(tok, all_rows)).astype(F32).astype(BF16)
        dealt = dot_nn(pick, raw_ref[...])
        cosine, su, sd = cos_ref[...], su_ref[...], sd_ref[...]
        for g in range(pairs):
            raw = dealt[:, g * LANES:(g + 1) * LANES]
            rawq_ref[:, g * LANES:(g + 1) * LANES] = raw.astype(BF16)
            rq = lax.rsqrt(head_mean(raw * raw, ones, head_dim) + EPSILON)
            pair = turn(raw * rq * qg_ref[...], cosine, su, sd, head_dim)
            for r, one in enumerate(spread_heads(pair, g, head_dim, low_lanes)):
                qx_ref[2 * g + r] = one.astype(BF16)
        raw = dealt[:, pairs * LANES:(pairs + 1) * LANES]
        rawk_ref[...] = raw.astype(BF16)
        rk = lax.rsqrt(head_mean(raw * raw, ones, head_dim) + EPSILON)
        keys = turn(raw * rk * kg_ref[...], cosine, su, sd, head_dim)
        k_ref[...] = keys.astype(BF16)
        kt_ref[...] = jnp.transpose(keys).astype(BF16)
        values = dealt[:, (pairs + 1) * LANES:]
        v_ref[...] = values.astype(BF16)
        vx_ref[0] = jnp.where(low_lanes, values, 1.0).astype(BF16)
        vx_ref[1] = jnp.where(low_lanes, 1.0, values).astype(BF16)


def fixed(array):
    return pl.BlockSpec(array.shape, lambda i: (0,) * array.ndim, pipeline_mode=pl.Buffered(1))


def qkv(xs, w, ocol, cosine, su, sd, qg, kg, head_dim):
    tok, width = xs[0].shape
    all_rows = 4 * tok
    out = lambda *dims: jax.ShapeDtypeStruct(dims, BF16)
    late = lambda c: pl.BlockSpec((tok, c), lambda i: (jnp.maximum(i - 4, 0), 0))
    heads = lambda n: pl.BlockSpec((n, tok, LANES), lambda i: (0, jnp.maximum(i - 4, 0), 0))
    return pl.pallas_call(
        functools.partial(qkv_kernel, head_dim),
        grid=(8,),
        out_shape=(
            out(all_rows, width), out(4, all_rows, LANES), out(all_rows, LANES), out(all_rows, LANES),
            out(2, all_rows, LANES), out(LANES, all_rows), out(all_rows, 2 * LANES), out(all_rows, LANES),
            jax.ShapeDtypeStruct((8, width), F32),
        ),
        in_specs=[fixed(x) for x in xs] + [fixed(w)] + [late(LANES)] * 4 + [fixed(qg), fixed(kg)],
        out_specs=(
            pl.BlockSpec((tok, width), lambda i: (jnp.minimum(i, 3), 0)),
            heads(4), late(LANES), late(LANES), heads(2),
            pl.BlockSpec((LANES, tok), lambda i: (0, jnp.maximum(i - 4, 0))), late(2 * LANES), late(LANES),
            pl.BlockSpec((8, width), lambda i: (0, 0)),
        ),
        scratch_shapes=[pltpu.VMEM((all_rows, 4 * LANES), BF16)],
        compiler_params=params(),
        cost_estimate=COST,
        name="qkv",
    )(*xs, w, ocol, cosine, su, sd, qg, kg)


def row_starts(lens_ref, index):
    start = jnp.zeros_like(index)
    end = lens_ref[0, 0]
    for s in range(1, lens_ref.shape[1]):
        start = jnp.where(index >= end, end, start)
        end = end + lens_ref[0, s]
    return start


def attend_kernel(head_dim, group, block, lens_ref, orow_ref, qx_ref, k_ref, vx_ref, *refs):
    given_ref, dealt_ref, lse_ref = refs[-3:]
    all_rows = k_ref.shape[0]
    scale = LOG2E * head_dim ** -0.5
    low_lanes = lane_iota(block, LANES) < head_dim
    mass_row = head_dim if group == 0 else 0

    def query_block(i, carry):
        rows = at_rows(i, block)
        q_index = i * block + row_iota(block, 1)
        start = row_starts(lens_ref, q_index)
        first = row_starts(lens_ref, i * block) // block
        clear = jnp.minimum((row_starts(lens_ref, i * block + block - 1) + block - 1) // block, i)
        queries = [qx_ref[r, rows, :] for r in range(2)]

        def step(j, state, masked):
            columns = at_rows(j, block)
            keys, values = k_ref[columns, :], vx_ref[0, columns, :]
            k_index = j * block + lane_iota(block, block)
            keep = (k_index <= q_index) & (k_index >= start)
            new = []
            for r in range(2):
                weights = jnp.exp2(dot_nt(queries[r], keys) * scale)
                if masked:
                    weights = jnp.where(keep, weights, 0.0)
                new.append(state[r] + dot_nn(weights.astype(BF16), values))
            return tuple(new)

        state = (jnp.zeros((block, LANES), F32),) * 2
        state = lax.fori_loop(first, clear, functools.partial(step, masked=True), state)
        state = lax.fori_loop(clear, i, functools.partial(step, masked=False), state)
        state = step(i, state, True)
        out = []
        for r in range(2):
            lse_ref[r:r + 1, rows] = jnp.log2(jnp.transpose(state[r])[mass_row:mass_row + 1, :])
            out.append(state[r] / pltpu.roll(state[r], head_dim, 1))
        if group == 0:
            pair = jnp.where(low_lanes, out[0], pltpu.roll(out[1], head_dim, 1))
        else:
            pair = jnp.where(low_lanes, pltpu.roll(out[0], head_dim, 1), out[1])
        dealt_ref[rows, :] = pair.astype(BF16)
        return carry

    lax.fori_loop(0, all_rows // block, query_block, 0)

    def undeal(i, carry):
        rows = at_rows(i, block)
        pick = (orow_ref[...] == i * block + row_iota(block, all_rows)).astype(F32).astype(BF16)
        given_ref[rows, :] = dot_nn(pick, dealt_ref[...]).astype(BF16)
        return carry

    lax.fori_loop(0, all_rows // block, undeal, 0)


def attend(group, lens, orow, qx, k, vx, head_dim, after):
    all_rows = k.shape[0]
    whole = lambda *dims: pl.BlockSpec(dims, lambda i: (0,) * len(dims))
    return pl.pallas_call(
        functools.partial(attend_kernel, head_dim, group, all_rows // 4),
        grid=(1,),
        out_shape=(
            jax.ShapeDtypeStruct((all_rows, LANES), BF16),
            jax.ShapeDtypeStruct((all_rows, LANES), BF16),
            jax.ShapeDtypeStruct((2, all_rows), F32),
        ),
        in_specs=[
            smem(), whole(1, all_rows),
            pl.BlockSpec((2, all_rows, LANES), lambda i: (group, 0, 0)),
            whole(all_rows, LANES),
            pl.BlockSpec((1, all_rows, LANES), lambda i: (group, 0, 0)),
        ] + anywhere(after),
        out_specs=(whole(all_rows, LANES), whole(all_rows, LANES), whole(2, all_rows)),
        compiler_params=params(),
        cost_estimate=COST,
        name="attend",
    )(lens, orow, qx, k, vx, *after)


def attend_back_kernel(head_dim, n_late, *refs):
    (lens_ref, ocol_ref, lse0_ref, lse1_ref, o0_ref, o1_ref, d0_ref, d1_ref, d2_ref, d3_ref, qg_ref, kg_ref) = refs[:12]
    late, refs = refs[12:12 + n_late], refs[-(2 + 5 + n_late + 1):]
    draw_ref, gain_ref, dgiven_ref, dx_ref, delta_ref, dk_ref, dv_ref = refs[:7]
    here, sems = refs[7:7 + n_late], refs[7 + n_late]
    qx_ref, k_ref, v_ref, kt_ref, rawq_ref, rawk_ref, cos_ref, su_ref, sd_ref = here
    copies = [pltpu.make_async_copy(late[n], here[n], sems.at[n]) for n in range(n_late)]
    for copy in copies:
        copy.start()
    all_rows = k_ref.shape[0]
    blocks = all_rows // ROWS
    exponent = LOG2E * head_dim ** -0.5
    scale = head_dim ** -0.5
    tok = d0_ref.shape[0]
    for d, ref in enumerate((d0_ref, d1_ref, d2_ref, d3_ref)):
        dgiven_ref[d * tok:(d + 1) * tok, :] = ref[...]
    dk_ref[...] = jnp.zeros_like(dk_ref)
    dv_ref[...] = jnp.zeros_like(dv_ref)
    gain_ref[...] = jnp.zeros_like(gain_ref)

    def deal(i, carry):
        rows = at_rows(i, tok)
        low_lanes = lane_iota(tok, LANES) < head_dim
        pick = (ocol_ref[rows, 0:1] == lane_iota(tok, all_rows)).astype(F32).astype(BF16)
        dealt = dot_nn(pick, dgiven_ref[...])
        for g, o_ref in enumerate((o0_ref, o1_ref)):
            pair = dealt[:, g * LANES:(g + 1) * LANES]
            for r, one in enumerate(spread_heads(pair, g, head_dim, low_lanes)):
                dx_ref[2 * g + r, rows, :] = one.astype(BF16)
            across = jnp.transpose(pair * o_ref[rows, :].astype(F32))
            for r in range(2):
                delta_ref[2 * g + r:2 * g + r + 1, rows] = jnp.sum(
                    across[r * head_dim:(r + 1) * head_dim], axis=0, keepdims=True
                )
        return carry

    lax.fori_loop(0, all_rows // tok, deal, 0)
    for copy in copies:
        copy.wait()
    ones = pair_ones(head_dim)

    def query_block(i, carry):
        rows = at_rows(i)
        q_index = i * ROWS + lane_iota(1, ROWS)
        start = row_starts(lens_ref, q_index)
        first = row_starts(lens_ref, i * ROWS) // ROWS
        count = (i + 2 - first) // 2
        base = jnp.maximum(i + 1 - 2 * count, 0)

        def step(n, state):
            at = base + 2 * n
            columns = pl.ds(pl.multiple_of(at * ROWS, ROWS), 2 * ROWS)
            k_index = at * ROWS + row_iota(2 * ROWS, ROWS)
            keep = (k_index <= q_index) & (k_index >= start)
            keys = k_ref[columns, :]
            values = v_ref[columns, :]
            new = []
            dk, dv = dk_ref[columns, :], dv_ref[columns, :]
            for h in range(4):
                g = h // 2
                queries = qx_ref[h, rows, :]
                grads = dx_ref[h, rows, :]
                lse = (lse0_ref, lse1_ref)[g][h % 2:h % 2 + 1, rows]
                weights = jnp.where(keep, jnp.exp2(dot_nt(keys, queries) * exponent - lse), 0.0)
                d_weights = dot_nt(values, grads)
                d_scores = (weights * (d_weights - delta_ref[h:h + 1, rows])).astype(BF16)
                dv = dv + dot_nn(weights.astype(BF16), grads)
                dk = dk + dot_nn(d_scores, queries)
                new.append(state[h] + dot_nn(kt_ref[g * head_dim:(g + 1) * head_dim, columns], d_scores))
            dk_ref[columns, :] = dk
            dv_ref[columns, :] = dv
            return tuple(new)

        state = lax.fori_loop(0, count, step, (jnp.zeros((head_dim, ROWS), F32),) * 4)
        cosine, su, sd = cos_ref[rows, :], su_ref[rows, :], sd_ref[rows, :]
        for g in range(2):
            pair = jnp.transpose(jnp.concatenate(state[2 * g:2 * g + 2], axis=0)) * scale
            lanes = slice(g * LANES, (g + 1) * LANES)
            draw, gain = norm_back(
                pair, rawq_ref[rows, lanes].astype(F32), qg_ref[...], cosine, su, sd, ones, head_dim
            )
            draw_ref[rows, lanes] = draw
            gain_ref[0:1, :] += gain
        return carry

    lax.fori_loop(0, blocks, query_block, 0)

    def key_block(i, carry):
        rows = at_rows(i, tok)
        cosine, su, sd = cos_ref[rows, :], su_ref[rows, :], sd_ref[rows, :]
        draw, gain = norm_back(
            dk_ref[rows, :] * scale, rawk_ref[rows, :].astype(F32), kg_ref[...], cosine, su, sd, ones, head_dim
        )
        draw_ref[rows, 2 * LANES:3 * LANES] = draw
        draw_ref[rows, 3 * LANES:] = dv_ref[rows, :].astype(BF16)
        gain_ref[1:2, :] += gain
        return carry

    lax.fori_loop(0, all_rows // tok, key_block, 0)


def rows_back_kernel(orow_ref, draw_ref, *refs):
    grad_ref, d_refs = refs[-5], refs[-4:]
    i = pl.program_id(0)
    all_rows = draw_ref.shape[0]
    rows = grad_ref.shape[0]
    pick = (orow_ref[...] == i * rows + row_iota(rows, all_rows)).astype(F32).astype(BF16)
    grads = dot_nn(pick, draw_ref[...]).astype(BF16)
    grad_ref[...] = grads
    for d, ref in enumerate(d_refs):

        @pl.when(i == d)
        def _(ref=ref):
            ref[...] = grads


def last_kernel(period, normed_ref, grads_ref, o0_ref, o1_ref, o2_ref, o3_ref, gain_ref, out_ref):
    width, extra = grads_ref.shape[1], o0_ref.shape[1]
    out_ref[:, :width] = dot_tn(normed_ref[...], grads_ref[...]).astype(BF16)
    total = o0_ref[...].astype(F32)
    for ref in (o1_ref, o2_ref, o3_ref):
        total = total + ref[...].astype(F32)
    out_ref[:, width:width + extra] = total.astype(BF16)
    place = row_iota(out_ref.shape[0], LANES) % period
    gains = jnp.where(place == 0, gain_ref[0:1, :], jnp.where(place == 1, gain_ref[1:2, :], 0.0))
    out_ref[:, width + extra:] = gains.astype(BF16)


def norm_back(pair, raw, gain, cosine, su, sd, ones, head_dim):
    pair = pair.astype(BF16).astype(F32)
    u = turn(pair, cosine, su, sd, head_dim, -1.0)
    r = lax.rsqrt(head_mean(raw * raw, ones, head_dim) + EPSILON)
    unit = raw * r
    scaled = u * gain
    draw = r * (scaled - unit * head_mean(scaled * unit, ones, head_dim))
    return draw.astype(BF16), jnp.sum(u * unit, axis=0, keepdims=True)


def anywhere(arrays):
    return [pl.BlockSpec(memory_space=pl.ANY)] * len(arrays)


def attend_back(lens, ocol, qx, k, v, kt, lses, dealts, grads, rawq, rawk, cosine, su, sd, qg, kg, head_dim):
    all_rows = k.shape[0]
    late = (qx, k, v, kt, rawq, rawk, cosine, su, sd)
    return pl.pallas_call(
        functools.partial(attend_back_kernel, head_dim, len(late)),
        out_shape=(
            jax.ShapeDtypeStruct((all_rows, 4 * LANES), BF16),
            jax.ShapeDtypeStruct((2, LANES), F32),
        ),
        in_specs=[smem()] + [vmem()] * 11 + anywhere(late),
        out_specs=(vmem(),) * 2,
        scratch_shapes=[
            pltpu.VMEM((all_rows, 2 * LANES), BF16),
            pltpu.VMEM((4, all_rows, LANES), BF16),
            pltpu.VMEM((4, all_rows), F32),
            pltpu.VMEM((all_rows, LANES), F32),
            pltpu.VMEM((all_rows, LANES), F32),
        ] + [pltpu.VMEM(a.shape, a.dtype) for a in late] + [pltpu.SemaphoreType.DMA((len(late),))],
        compiler_params=params(),
        cost_estimate=COST,
        name="attend_back",
    )(lens, ocol, *lses, *dealts, *grads, qg, kg, *late)


def rows_back(orow, draw, after):
    all_rows, width = draw.shape
    tok = all_rows // 4
    return pl.pallas_call(
        rows_back_kernel,
        grid=(4,),
        out_shape=(jax.ShapeDtypeStruct((all_rows, width), BF16),) + (jax.ShapeDtypeStruct((tok, width), BF16),) * 4,
        in_specs=[fixed(orow), fixed(draw)] + anywhere(after),
        out_specs=(pl.BlockSpec((tok, width), lambda i: (i, 0)),)
        + (pl.BlockSpec((tok, width), lambda i: (0, 0)),) * 4,
        compiler_params=params(),
        cost_estimate=COST,
        name="rows_back",
    )(orow, draw, *after)


def last_weights(normed, grads, parts, gains, shards):
    all_rows, width = grads.shape
    depth, extra = normed.shape[1], parts[0].shape[1]
    wide = width + extra + LANES
    block = lambda c: pl.BlockSpec((depth // 4, c), lambda i: (i, 0))
    return pl.pallas_call(
        functools.partial(last_kernel, depth // shards),
        grid=(4,),
        out_shape=jax.ShapeDtypeStruct((depth, wide), BF16),
        in_specs=[pl.BlockSpec((all_rows, depth // 4), lambda i: (0, i)), fixed(grads)]
        + [block(extra)] * 4 + [fixed(gains)],
        out_specs=block(wide),
        compiler_params=params(),
        cost_estimate=COST,
        name="last_weights",
    )(normed, grads, *parts, gains)


def tokens_kernel(me_ref, g0_ref, g1_ref, g2_ref, g3_ref, w_ref, x_ref, mid_ref, gain_ref, *refs):
    out_ref = refs[-1]
    me = me_ref[0]
    d_normed = jnp.zeros(x_ref.shape, F32)
    span, width = 2 * LANES, 8 * LANES
    for d, ref in enumerate((g0_ref, g1_ref, g2_ref, g3_ref)):
        other = jnp.bitwise_xor(me, d)
        take = lambda at, size: w_ref[:, pl.ds(pl.multiple_of(at + other * size, size), size)]
        weights = jnp.concatenate([take(0, span), take(width, LANES), take(width + 4 * LANES, LANES)], axis=1)
        d_normed = d_normed + dot_nt(ref[...], weights)
    x = x_ref[...].astype(F32)
    r1 = lax.rsqrt(jnp.mean(x * x, axis=1, keepdims=True) + EPSILON)
    scaled = d_normed * gain_ref[...]
    pull = jnp.mean(scaled * x, axis=1, keepdims=True)
    out_ref[...] = (mid_ref[...] + r1 * scaled - x * (r1 * r1 * r1 * pull)).astype(BF16)


def tokens_back(me, grads, w, x, d_middle, gain, after):
    tok, width = x.shape
    rows = lambda c: pl.BlockSpec((ROWS, c), lambda i: (i, 0))
    return pl.pallas_call(
        tokens_kernel,
        grid=(tok // ROWS,),
        out_shape=jax.ShapeDtypeStruct((tok, width), BF16),
        in_specs=[smem()] + [rows(grads[0].shape[1])] * 4 + [fixed(w), rows(width), rows(width), fixed(gain)] + anywhere(after),
        out_specs=rows(width),
        compiler_params=params(),
        cost_estimate=COST,
        name="tokens_back",
    )(me, *grads, w, x, d_middle, gain, *after)


def ffn_kernel(per, shards, blocks, n_carried, *refs):
    refs = list(refs)
    take = lambda n: [refs.pop(0) for _ in range(n)]
    me_ref = take(1)[0]
    att = [take(2 if d < 3 else 2 * len(blocks)) for d in range(4)]
    xs = [take(2 if d == 3 else 1) for d in blocks]
    cots = [take(2 if d == 3 else 1) for d in blocks]
    wo_ref, gain_ref, wg_ref, wu_ref, wd_ref = take(5)
    diag = take(4) if blocks == (1, 2) else None
    take(n_carried)
    nf_ref, hid_ref, dgu_ref, cot_ref = take(4)
    packed_ref, wd_ref = wd_ref, refs.pop()
    i = pl.program_id(0)
    me = me_ref[0]
    hidden_units = hid_ref.shape[1]
    which = i // per

    @pl.when(i == 0)
    def _():
        rows, piece = packed_ref.shape[0] // shards, wd_ref.shape[0] // shards
        for k in range(shards):
            block = packed_ref[k * rows:(k + 1) * rows, :]
            if piece % 16:
                block = block.astype(F32)
            wd_ref[k * piece:(k + 1) * piece, :] = unpack_rows(block, wd_ref.shape[1]).astype(BF16)

    def read(lists):
        parts = [jnp.concatenate([ref[...] for ref in one], axis=1) for one in lists]
        return parts[0] if len(parts) == 1 else jnp.where(which == 0, parts[0], parts[1])

    middle = read(xs).astype(F32)
    for d in range(4):
        block = read([att[d][2 * n:2 * n + 2] for n in range(len(att[d]) // 2)])
        middle = middle + dot_nn(block, wo_ref[at_rows(jnp.bitwise_xor(me, d), 2 * LANES), :middle.shape[1]])
    r2 = lax.rsqrt(jnp.mean(middle * middle, axis=1, keepdims=True) + EPSILON)
    nf = (middle * r2 * gain_ref[...]).astype(BF16)
    nf_ref[...] = nf
    cot = read(cots)
    cot_ref[...] = cot
    wg, wu = wg_ref[...], wu_ref[...]
    gate = dot_nn(nf, wg)
    up = dot_nn(nf, wu)
    s = jax.nn.sigmoid(gate)
    silu = gate * s
    hidden = (silu * up).astype(BF16)
    hid_ref[...] = hidden
    d_hidden = dot_nt(cot, wd_ref[...])
    d_gate = (d_hidden * up * s * (1.0 + gate * (1.0 - s))).astype(BF16)
    d_up = (d_hidden * silu).astype(BF16)
    dgu_ref[:, :hidden_units] = d_gate
    dgu_ref[:, hidden_units:] = d_up
    dn = dot_nt(d_gate, wg) + dot_nt(d_up, wu)
    bo = dot_nn(hidden, wd_ref[...])
    half = dn.shape[1] // 2
    if blocks == (3,):
        for ref, value in zip(take(4), (dn[:, :half], dn[:, half:], bo[:, :half], bo[:, half:])):
            ref[...] = value.astype(BF16)
    elif blocks == (0,):
        dn_ref, bo_ref, mid_ref = take(3)
        dn_ref[...] = dn.astype(BF16)
        bo_ref[...] = bo.astype(BF16)
        mid_ref[...] = middle
    else:
        dn1_ref, dn2_ref, bo1_ref, bo2_ref = take(4)

        @pl.when(which == 0)
        def _():
            for ref, value, extra in ((dn1_ref, dn, diag[1]), (bo1_ref, bo, diag[3])):
                ref[:, :half] = value[:, :half].astype(BF16)
                ref[:, half:] = (value[:, half:] + extra[...].astype(F32)).astype(BF16)

        @pl.when(which == 1)
        def _():
            for ref, value, extra in ((dn2_ref, dn, diag[0]), (bo2_ref, bo, diag[2])):
                ref[:, :half] = (value[:, :half] + extra[...].astype(F32)).astype(BF16)
                ref[:, half:] = value[:, half:].astype(BF16)


def ffn(me, blocks, att, xs, cots, gain, wide, shards, diag, carried, after):
    all_rows = att[0].shape[0]
    units, width = wide.shape[1] // 4, wide.shape[0]
    tok = all_rows // 4
    per = tok // ROWS
    block_of = lambda i: blocks[0] + (i // per) * (blocks[-1] - blocks[0])
    everywhere = lambda c: pl.BlockSpec((ROWS, c), lambda i: (block_of(i) * per + i % per, 0))
    crossed = lambda d: pl.BlockSpec(
        (ROWS, LANES), lambda i: (jnp.bitwise_xor(block_of(i), d) * per + i % per, 0)
    )
    held = lambda n, c: pl.BlockSpec((ROWS, c), lambda i: (jnp.clip(i - n * per, 0, per - 1), 0))
    halves = {0: 1, 1: 1, 2: 0, 3: 0}
    last = []
    for n, d in enumerate(blocks):
        local = lambda i, n=n, d=d: ((3 - d) % 2 * per + jnp.clip(i - n * per, 0, per - 1), 0)
        last += [(att[6], crossed(3)), (att[7 + halves[d]], pl.BlockSpec((ROWS, LANES), local))]
    weight = lambda n: pl.BlockSpec((wide.shape[0], units), lambda i: (0, n), pipeline_mode=pl.Buffered(1))
    out = lambda r, c, t=BF16: jax.ShapeDtypeStruct((r, c), t)
    pieces = lambda arrays: [held(n, a.shape[1]) for n, d in enumerate(blocks) for a in arrays[d]]
    shapes = [out(all_rows, width), out(all_rows, units), out(all_rows, 2 * units), out(all_rows, width)]
    specs = [everywhere(width), everywhere(units), everywhere(2 * units), everywhere(width)]
    if blocks == (3,):
        shapes += [out(tok, width // 2)] * 4
        specs += [held(0, width // 2)] * 4
    elif blocks == (0,):
        shapes += [out(tok, width)] * 2 + [out(tok, width, F32)]
        specs += [held(0, width)] * 3
    else:
        shapes += [out(tok, width)] * 4
        specs += [held(0, width), held(1, width)] * 2
    diag_specs = [held(1, width // 2), held(0, width // 2)] * 2 if diag else []
    operands = (
        [me] + list(att[:6]) + [a for a, _ in last] + [a for d in blocks for a in xs[d]] + [a for d in blocks for a in cots[d]]
        + [wide, gain, wide, wide, wide] + list(diag) + list(carried) + list(after)
    )
    first = len(operands) - len(carried) - len(after)
    return pl.pallas_call(
        functools.partial(ffn_kernel, per, shards, blocks, len(carried) + len(after)),
        grid=(len(blocks) * per,),
        out_shape=tuple(shapes),
        in_specs=[smem()] + [crossed(d) for d in range(3) for _ in range(2)] + [spec for _, spec in last]
        + pieces(xs) + pieces(cots) + [weight(3), fixed(gain), weight(0), weight(1), weight(2)] + diag_specs + anywhere(carried) + anywhere(after),
        out_specs=tuple(specs),
        input_output_aliases={first + n: n for n in range(len(carried))},
        scratch_shapes=[pltpu.VMEM((units, width), BF16)],
        compiler_params=params(),
        cost_estimate=COST,
        name="ffn",
    )(*operands)


DOWN_STEPS = 3


def weights_kernel(shards, nf_ref, dgu_from, hid_ref, cot_ref, out_ref, down_ref, dgu_ref, sem):
    i = pl.program_id(0)
    copy = pltpu.make_async_copy(dgu_from, dgu_ref, sem)

    @pl.when(i == 0)
    def _():
        copy.start()

    @pl.when(i < DOWN_STEPS)
    def _():
        down_ref[at_rows(i, hid_ref.shape[1]), :] = dot_tn(hid_ref[...], cot_ref[...])

    @pl.when(i == DOWN_STEPS)
    def _():
        copy.wait()

    @pl.when(i >= DOWN_STEPS)
    def _():
        out_ref[:, :dgu_ref.shape[1]] = dot_tn(nf_ref[...], dgu_ref[...]).astype(BF16)

    per, piece = shards // 4, down_ref.shape[0] // shards
    rows = out_ref.shape[0] // per
    for k in range(shards):

        @pl.when(i == DOWN_STEPS + k // per)
        def _(k=k):
            block = pack_rows(down_ref[k * piece:(k + 1) * piece, :], rows)
            at = k % per * rows
            out_ref[at:at + rows, dgu_ref.shape[1]:] = block.astype(BF16)


def weights_back(nf, d_gu, hidden, cot, shards):
    rows, depth = nf.shape
    late = lambda i: jnp.maximum(i - DOWN_STEPS, 0)
    units = hidden.shape[1]
    wide = d_gu.shape[1] + units
    return pl.pallas_call(
        functools.partial(weights_kernel, shards),
        grid=(DOWN_STEPS + 4,),
        out_shape=jax.ShapeDtypeStruct((depth, wide), BF16),
        in_specs=[
            pl.BlockSpec((rows, depth // 4), lambda i: (0, late(i))), pl.BlockSpec(memory_space=pl.ANY),
            pl.BlockSpec((rows, units // DOWN_STEPS), lambda i: (0, jnp.minimum(i, DOWN_STEPS - 1))), fixed(cot),
        ],
        out_specs=pl.BlockSpec((depth // 4, wide), lambda i: (late(i), 0)),
        scratch_shapes=[
            pltpu.VMEM((units, cot.shape[1]), F32), pltpu.VMEM(d_gu.shape, BF16), pltpu.SemaphoreType.DMA,
        ],
        compiler_params=params(),
        cost_estimate=COST,
        name="weights_back",
    )(nf, d_gu, hidden, cot)


def middle_kernel(*refs):
    me_ref, dn_refs = refs[0], refs[1:4]
    cot_ref, mid_ref, gain_ref, wide_ref = refs[4:8]
    dmid_ref, branch_ref, da_refs, wo_ref, sem = refs[-8], refs[-7], refs[-6:-2], refs[-2], refs[-1]
    at = wide_ref.shape[1] // 4 * 3
    copy = pltpu.make_async_copy(wide_ref.at[:, at:at + wo_ref.shape[1]], wo_ref, sem)
    copy.start()
    me = me_ref[0]
    tok = mid_ref.shape[0]

    def rows_of(i, carry):
        rows = at_rows(i)
        middle = mid_ref[rows, :]
        d_normed = dn_refs[0][rows, :].astype(F32)
        for ref in dn_refs[1:]:
            d_normed = d_normed + ref[rows, :].astype(F32)
        r2 = lax.rsqrt(jnp.mean(middle * middle, axis=1, keepdims=True) + EPSILON)
        scaled = d_normed * gain_ref[...]
        pull = jnp.mean(scaled * middle, axis=1, keepdims=True)
        d_middle = cot_ref[rows, :].astype(F32) + r2 * scaled - middle * (r2 * r2 * r2 * pull)
        dmid_ref[rows, :] = d_middle
        branch_ref[rows, :] = d_middle.astype(BF16)
        return carry

    lax.fori_loop(0, tok // ROWS, rows_of, 0)
    copy.wait()
    span = 2 * LANES
    for d in range(4):
        there = pl.ds(pl.multiple_of(jnp.bitwise_xor(me, d) * span, span), span)
        da_refs[d][...] = dot_nt(branch_ref[...], wo_ref[there, :branch_ref.shape[1]]).astype(BF16)


def out_kernel(me_ref, *refs):
    att_refs, branch_ref, outs = refs[:8], refs[8], refs[9:]
    span = 2 * LANES
    for d in range(4):
        there = pl.ds(pl.multiple_of(jnp.bitwise_xor(me_ref[0], d) * span, span), span)
        rows = jnp.concatenate([att_refs[2 * d][...], att_refs[2 * d + 1][...]], axis=1)
        for e in range(4):
            columns = pl.ds(pl.multiple_of(jnp.bitwise_xor(me_ref[0], e) * span, span), span)
            outs[e][there, :] = dot_tn(rows, branch_ref[:, columns]).astype(BF16)


def out_weights(me, att, branch):
    tok, width = branch.shape
    whole = lambda r, c: pl.BlockSpec((r, c), lambda i: (0, 0))
    own = lambda d: pl.BlockSpec((tok, LANES), lambda i: (d, 0))
    return pl.pallas_call(
        out_kernel,
        grid=(1,),
        out_shape=(jax.ShapeDtypeStruct((width, width // 4), BF16),) * 4,
        in_specs=[smem()] + [own(d) for d in (0, 0, 1, 1, 2, 2, 3, 1)] + [whole(tok, width)],
        out_specs=(whole(width, width // 4),) * 4,
        compiler_params=params(),
        cost_estimate=COST,
        name="out_weights",
    )(me, *att[:7], att[8], branch)


def middle_back(me, parts, cot, middle, gain, wide, after):
    tok, width = middle.shape
    whole = lambda r, c: pl.BlockSpec((r, c), lambda i: (0, 0))
    out = lambda r, c, t=BF16: jax.ShapeDtypeStruct((r, c), t)
    return pl.pallas_call(
        middle_kernel,
        grid=(1,),
        out_shape=(out(tok, width, F32), out(tok, width)) + (out(tok, 2 * LANES),) * 4,
        in_specs=[smem()] + [whole(tok, width)] * 5 + [whole(1, width)] + anywhere((wide,) + tuple(after)),
        out_specs=(whole(tok, width),) * 2 + (whole(tok, 2 * LANES),) * 4,
        scratch_shapes=[pltpu.VMEM((wide.shape[0], width), BF16), pltpu.SemaphoreType.DMA],
        compiler_params=params(),
        cost_estimate=COST,
        name="middle_back",
    )(me, *parts, cot, middle, gain, wide, *after)


def swap(array, distance):
    return lax.ppermute(array, "seq", [(s, s ^ distance) for s in range(4)])


def gather_rows(block, meanwhile):
    half = block.shape[1] // 2
    one, two = swap(block, 1), swap(block, 2)
    one, two, meanwhile = lax.optimization_barrier((one, two, meanwhile))
    return [meanwhile, [one], [two], [swap(one[:, :half], 2), swap(two[:, half:], 1)]]


def after(value, *others):
    return lax.optimization_barrier((value, others))[0]


def body(
    tokens, order, seq_lengths, attn_gain, w_query, w_key, w_value, query_gain, key_gain,
    w_out, ffn_gain, w_gate, w_up, w_down, cotangent,
):
    tok = tokens.shape[1]
    ways = lax.axis_size("seq")
    shards = lax.axis_size("shard")
    all_rows = tok * ways
    head_dim = query_gain.shape[0]
    me = lax.axis_index("seq")
    me_arr = me.astype(jnp.int32)[None]
    own = lambda a, axis: lax.dynamic_slice_in_dim(a, me * (a.shape[axis] // ways), a.shape[axis] // ways, axis)
    depth = w_gate.shape[0]
    units = w_gate.shape[1] // ways
    piece = units // shards

    cosine, sine_up, sine_down, ocol, orow = make_tables(me_arr, seq_lengths, order, head_dim)
    q_gain = jnp.tile(query_gain.astype(F32), LANES // head_dim)[None, :]
    k_gain = jnp.tile(key_gain.astype(F32), LANES // head_dim)[None, :]

    tables = (cosine, sine_up, sine_down, ocol, orow, q_gain, k_gain)

    xs = gather_rows(tokens[0], tables)
    w_first = first_weights(me_arr, w_query, w_key, w_value, attn_gain, ffn_gain)
    w_qkv = lax.all_gather(w_first, "shard", axis=0, tiled=True)
    w_cut = cut_weights(me_arr, w_gate, w_up, own(w_down, 0), w_out, shards)
    w_wide = lax.all_gather(after(w_cut, xs[1]), "shard", axis=0, tiled=True)

    cosine, sine_up, sine_down, ocol, orow, q_gain, k_gain = xs[0]
    xs = [[tokens[0]]] + xs[1:]
    normed, qx, k, v, vx, kt, rawq, rawk, gains = qkv(
        [x for one in xs for x in one], w_qkv, ocol, cosine, sine_up, sine_down, q_gain, k_gain, head_dim
    )
    cot = cotangent[0]
    cots = gather_rows(after(cot, xs[3]), gains)
    gains, cots = cots[0], [[cot]] + cots[1:]
    gain_a, gain_f = gains[0:1], gains[1:2]
    w_rows = jnp.concatenate(after([w_query, w_key, w_value], xs[3]), axis=1)
    w_all = lax.all_gather(w_rows, "shard", axis=0, tiled=True)

    att, dealts, lses = [], [], []
    for g in range(2):
        given, dealt, lse = attend(g, seq_lengths, orow, qx, k, vx, head_dim, [])
        one, two = swap(given, 1), swap(given, 2)
        half = given.shape[0] // 2
        three = [swap(one[:half], 2), swap(two[half:], 1)] if g else [swap(given, 3)]
        att.append([given, one, two] + three)
        dealts.append(dealt)
        lses.append(lse)
    att = [att[g][d] for d in range(3) for g in range(2)] + att[0][3:] + att[1][3:]

    feed = lambda blocks, diag, carried, after=(): ffn(
        me_arr, blocks, att, xs, cots, gain_f, w_wide, shards, diag, carried, after
    )
    *carried, dn3a, dn3b, bo3a, bo3b = feed((3,), (), (), att[8:])
    diag = (swap(dn3a, 1), swap(dn3b, 2), swap(bo3a, 1), swap(bo3b, 2))
    *carried, dn0, bo0, middle = feed((0,), (), carried)
    *carried, dn1, dn2, bo1, bo2 = feed((1, 2), diag, carried)
    nf, hidden, d_gu, cot_all = carried
    dn = (dn0, swap(dn1, 1), swap(dn2, 2))
    scatter = lambda a: lax.psum_scatter(a, "shard", scatter_dimension=0, tiled=True)
    p_ffn = weights_back(nf, d_gu, hidden, cot_all, shards)
    d_ffn = scatter(after(p_ffn, dn))

    d_middle, branch, *d_att = middle_back(me_arr, dn, cot, middle, gain_f, w_wide, (p_ffn, w_all))
    p_wo = out_weights(me_arr, att, branch)
    d_att = [d_att[0]] + [swap(d_att[d], d) for d in (1, 2, 3)]
    draw, head_gains = attend_back(
        seq_lengths, ocol, qx, k, v, kt, lses, dealts, d_att, rawq, rawk,
        cosine, sine_up, sine_down, q_gain, k_gain, head_dim,
    )
    bo1, bo2, *p_wo = after([bo1, bo2] + list(p_wo), d_att)
    bo = [bo0, swap(bo1, 1), swap(bo2, 2)]
    p_wo = [p_wo[0]] + [swap(p_wo[d], d) for d in (1, 2, 3)]
    grads, *d_raw = rows_back(orow, draw, bo[1:3])
    d_raw = [d_raw[0]] + [swap(d_raw[d], d) for d in (1, 2, 3)]
    p_last = last_weights(normed, grads, p_wo, head_gains, shards)
    block_out = (middle + sum(b.astype(F32) for b in after(bo, p_last))).astype(BF16)
    d_last = scatter(after(p_last, d_ffn, d_raw))
    d_tokens = tokens_back(me_arr, d_raw, w_all, tokens[0], d_middle, gain_a, (p_last,))
    d_ffn = after(d_ffn, d_raw, p_last)

    def parts_of(part):
        return [part] + [swap(part, d) for d in (1, 2, 3)]

    d_wg, d_wu, d_wd, d_ffn_gain = join_weights(me_arr, parts_of(d_ffn), w_gate, w_up, ffn_gain, w_down.shape, shards)
    d_wq, d_wk, d_wv, d_wo, d_attn_gain, d_query_gain, d_key_gain = join_last(
        me_arr, parts_of(after(d_last, d_ffn, d_tokens, block_out)), w_query, w_key, w_value, attn_gain,
        w_out.shape[1], head_dim,
    )
    return (
        block_out[None], d_tokens[None], d_attn_gain[0], d_wq, d_wk, d_wv, d_query_gain[0], d_key_gain[0],
        d_wo, d_ffn_gain[0], d_wg, d_wu, d_wd,
    )


def solution(mesh):
    rows, flat, wide = P("shard", None), P("shard"), P("shard", "seq", None)
    in_specs = (
        wide, rows, rows, flat, rows, rows, rows, P(), P(), rows, flat, rows, rows, rows, wide,
    )
    out_specs = (wide, wide, flat, rows, rows, rows, P(), P(), rows, flat, rows, rows, rows)
    return jax.shard_map(body, mesh=mesh, in_specs=in_specs, out_specs=out_specs, check_vma=False)
```

```python
import functools

import jax
import jax.numpy as jnp
from jax import lax
from jax.experimental import pallas as pl
from jax.experimental.pallas import tpu as pltpu
from jax.sharding import PartitionSpec as P

EPSILON = 1e-05
ROPE_BASE = 1000000.0
LOG2E = 1.4426950408889634
ROWS = 256
LANES = 128
F32 = jnp.float32
BF16 = jnp.bfloat16
COST = pl.CostEstimate(flops=1 << 20, bytes_accessed=1 << 16, transcendentals=0)
VMEM_LIMIT = 58 * 1024 * 1024


def dot_nn(left, right):
    return jnp.dot(left, right, preferred_element_type=F32)


def dot_nt(left, right):
    return lax.dot_general(left, right, (((1,), (1,)), ((), ())), preferred_element_type=F32)


def dot_tn(left, right):
    return lax.dot_general(left, right, (((0,), (0,)), ((), ())), preferred_element_type=F32)


def vmem():
    return pl.BlockSpec(memory_space=pltpu.VMEM)


def smem():
    return pl.BlockSpec(memory_space=pltpu.SMEM)


def params():
    return pltpu.CompilerParams(vmem_limit_bytes=VMEM_LIMIT)


def lane_iota(rows, columns):
    return lax.broadcasted_iota(jnp.int32, (rows, columns), 1)


def row_iota(rows, columns):
    return lax.broadcasted_iota(jnp.int32, (rows, columns), 0)


def at_rows(block, rows=ROWS):
    return pl.ds(pl.multiple_of(block * rows, rows), rows)


def pair_ones(head_dim):
    return (
        row_iota(LANES, LANES) // head_dim == lane_iota(LANES, LANES) // head_dim
    ).astype(BF16)


def head_mean(values, ones, head_dim):
    high = values.astype(BF16)
    low = (values - high.astype(F32)).astype(BF16)
    return (dot_nn(high, ones) + dot_nn(low, ones)) * (1.0 / head_dim)


def turn(values, cosine, sine_up, sine_down, head_dim, sign=1.0):
    half = head_dim // 2
    up = pltpu.roll(values, LANES - half, 1) * sine_up
    down = pltpu.roll(values, half, 1) * sine_down
    return values * cosine + sign * (up + down)


def spread_heads(pair, group, head_dim, low_lanes):
    moved = pltpu.roll(pair, head_dim, 1)
    if group == 0:
        return jnp.where(low_lanes, pair, 0.0), jnp.where(low_lanes, moved, 0.0)
    return jnp.where(low_lanes, 0.0, moved), jnp.where(low_lanes, 0.0, pair)


def first_kernel(me_ref, q_ref, k_ref, v_ref, ga_ref, gf_ref, out_ref):
    at = 0
    for ref in (q_ref, k_ref, v_ref):
        size = ref.shape[1] // 4
        out_ref[:, at:at + size] = ref[:, pl.ds(pl.multiple_of(me_ref[0] * size, size), size)]
        at += size
    depth = out_ref.shape[0]
    row = row_iota(LANES, depth)
    gains = jnp.where(row == 0, ga_ref[...].astype(F32), jnp.where(row == 1, gf_ref[...].astype(F32), 0.0))
    out_ref[:, at:] = jnp.transpose(gains).astype(BF16)


def first_weights(me, w_query, w_key, w_value, attn_gain, ffn_gain):
    depth = w_query.shape[0]
    width = (w_query.shape[1] + w_key.shape[1] + w_value.shape[1]) // 4 + LANES
    return pl.pallas_call(
        first_kernel,
        out_shape=jax.ShapeDtypeStruct((depth, width), BF16),
        in_specs=[smem()] + [vmem()] * 5,
        out_specs=vmem(),
        compiler_params=params(),
        cost_estimate=COST,
        name="first_weights",
    )(me, w_query, w_key, w_value, attn_gain[None], ffn_gain[None])


def pack_rows(block, rows):
    rest = [block[rows:, c:c + LANES] for c in range(0, block.shape[1], LANES)]
    return jnp.concatenate([block[:rows], jnp.concatenate(rest, axis=0)], axis=1)


def unpack_rows(block, width):
    rows = block.shape[0]
    extra = rows * LANES // width
    rest = [block[extra * c:extra * (c + 1), width:] for c in range(width // LANES)]
    return jnp.concatenate([block[:, :width], jnp.concatenate(rest, axis=1)], axis=0)


def cut_kernel(shards, me_ref, gate_ref, up_ref, down_ref, wo_ref, out_ref):
    whole, units = gate_ref.shape[1], gate_ref.shape[1] // 4
    piece, span = units // shards, whole // shards
    for at, ref in ((0, gate_ref), (units, up_ref)):
        turned = pltpu.roll(ref[...].astype(F32), whole - piece * me_ref[0], 1)
        parts = [turned[:, span * k:span * k + piece] for k in range(shards)]
        out_ref[:, at:at + units] = jnp.concatenate(parts, axis=1).astype(BF16)
    out_ref[:, 2 * units:3 * units] = pack_rows(down_ref[...].astype(F32), out_ref.shape[0]).astype(BF16)
    width = wo_ref.shape[1]
    out_ref[:, 3 * units:3 * units + width] = wo_ref[...]
    out_ref[:, 3 * units + width:] = jnp.zeros((out_ref.shape[0], units - width), BF16)


def cut_weights(me, w_gate, w_up, w_down, w_out, shards):
    depth, whole = w_gate.shape
    return pl.pallas_call(
        functools.partial(cut_kernel, shards),
        out_shape=jax.ShapeDtypeStruct((depth, whole), BF16),
        in_specs=[smem()] + [vmem()] * 4,
        out_specs=vmem(),
        compiler_params=params(),
        cost_estimate=COST,
        name="cut_weights",
    )(me, w_gate, w_up, w_down, w_out)


def divided_row(column, gain_ref):
    across = jnp.transpose(jnp.broadcast_to(column, (column.shape[0], LANES)))
    return across[0:1, :] / gain_ref[...].astype(F32)


def join_kernel(shards, me_ref, p0_ref, p1_ref, p2_ref, p3a_ref, p3b_ref, gate_ref, up_ref, gain_ref, dgate_ref, dup_ref, ddown_ref, dot_ref, st_ref):
    for d, ref in enumerate((p0_ref, p1_ref, p2_ref)):
        st_ref[d] = ref[...]
    st_ref[3] = jnp.concatenate([p3a_ref[...], p3b_ref[...]], axis=1)
    units = p0_ref.shape[1] // 3
    piece = units // shards
    quarters = [st_ref[jnp.bitwise_xor(me_ref[0], q)] for q in range(4)]
    total = 0.0
    for at, w_ref, out_ref in ((0, gate_ref, dgate_ref), (units, up_ref, dup_ref)):
        parts = [q[:, at:at + units].astype(F32) for q in quarters]
        parts = [q[:, piece * k:piece * (k + 1)] for k in range(shards) for q in parts]
        joined = jnp.concatenate(parts, axis=1)
        out_ref[...] = joined
        total = total + jnp.sum(joined * w_ref[...].astype(F32), axis=1, keepdims=True)
    dot_ref[...] = divided_row(total, gain_ref)
    for q, quarter in enumerate(quarters):
        block = unpack_rows(quarter[:, 2 * units:].astype(F32), ddown_ref.shape[1])
        ddown_ref[q * piece:(q + 1) * piece, :] = block


def join_weights(me, parts, w_gate, w_up, gain, down_shape, shards):
    depth, whole = w_gate.shape
    return pl.pallas_call(
        functools.partial(join_kernel, shards),
        out_shape=(jax.ShapeDtypeStruct((depth, whole), F32),) * 2
        + (jax.ShapeDtypeStruct(down_shape, F32), jax.ShapeDtypeStruct((1, depth), F32)),
        in_specs=[smem()] + [vmem()] * 8,
        out_specs=(vmem(),) * 4,
        scratch_shapes=[pltpu.VMEM((4,) + parts[0].shape, BF16)],
        compiler_params=params(),
        cost_estimate=COST,
        name="join_weights",
    )(me, *parts, w_gate, w_up, gain[None])


def join_last_kernel(me_ref, p0_ref, p1_ref, p2_ref, p3_ref, q_ref, k_ref, v_ref, gain_ref,
                     dq_ref, dk_ref, dv_ref, do_ref, dot_ref, qgain_ref, kgain_ref):
    at = 0
    parts = (p0_ref, p1_ref, p2_ref, p3_ref)
    total = jnp.zeros((dq_ref.shape[0], 1), F32)
    for out_ref, w_ref in ((dq_ref, q_ref), (dk_ref, k_ref), (dv_ref, v_ref), (do_ref, None)):
        size = out_ref.shape[1] // 4
        for d, ref in enumerate(parts):
            there = pl.ds(pl.multiple_of(jnp.bitwise_xor(me_ref[0], d) * size, size), size)
            part = ref[:, at:at + size].astype(F32)
            out_ref[:, there] = part
            if w_ref is not None:
                total = total + jnp.sum(part * w_ref[:, there].astype(F32), axis=1, keepdims=True)
        at += size
    dot_ref[...] = divided_row(total, gain_ref)
    gains = jnp.zeros((8, LANES), F32)
    for ref in parts:
        gains = gains + ref[0:16, at:].astype(F32)[:8]
    head_dim = qgain_ref.shape[1]
    gains = gains[:, :head_dim] + gains[:, head_dim:]
    qgain_ref[...] = gains[0:1]
    kgain_ref[...] = gains[1:2]


def join_last(me, parts, w_query, w_key, w_value, gain, out_width, head_dim):
    depth = w_query.shape[0]
    out = lambda c: jax.ShapeDtypeStruct((depth, c), F32)
    return pl.pallas_call(
        join_last_kernel,
        out_shape=(
            out(w_query.shape[1]), out(w_key.shape[1]), out(w_value.shape[1]), out(out_width),
            jax.ShapeDtypeStruct((1, depth), F32),
        ) + (jax.ShapeDtypeStruct((1, head_dim), F32),) * 2,
        in_specs=[smem()] + [vmem()] * 8,
        out_specs=(vmem(),) * 7,
        compiler_params=params(),
        cost_estimate=COST,
        name="join_last",
    )(me, *parts, w_query, w_key, w_value, gain[None])


def table_kernel(half, me_ref, lens_ref, order_ref, freq_ref, cos_ref, up_ref, down_ref, ocol_ref, orow_ref):
    all_rows = order_ref.shape[1]
    groups = LANES // half
    rows = all_rows // groups
    lane = lane_iota(rows, LANES)
    index = lane // half * rows + row_iota(rows, LANES)
    angles = (index - row_starts(lens_ref, index)).astype(F32) * freq_ref[...]
    cosine, sine = jnp.cos(angles), jnp.sin(angles)
    first = lane % (2 * half) < half
    for q in range(groups):

        def spread(table, q=q):
            one = jnp.where(lane < half, pltpu.roll(table, LANES - half * q, 1) if q else table, 0.0)
            return one + pltpu.roll(one, half, 1) + pltpu.roll(one, 2 * half, 1) + pltpu.roll(one, 3 * half, 1)

        here = slice(q * rows, (q + 1) * rows)
        cos_ref[here, :] = spread(cosine)
        wide = spread(sine)
        up_ref[here, :] = jnp.where(first, -wide, 0.0)
        down_ref[here, :] = jnp.where(first, 0.0, wide)
    relative = jnp.bitwise_xor(order_ref[...], me_ref[0] * (all_rows // 4))
    orow_ref[...] = relative
    for c in range(all_rows // LANES):
        here = slice(c * LANES, (c + 1) * LANES)
        across = jnp.broadcast_to(relative[:, here].astype(F32), (LANES, LANES))
        ocol_ref[here, :] = jnp.transpose(across).astype(jnp.int32)


def make_tables(me, lens, order, head_dim):
    all_rows = order.shape[1]
    half = head_dim // 2
    frequency = ROPE_BASE ** (-2.0 * jnp.arange(half, dtype=F32) / head_dim)
    out = lambda r, c, t: jax.ShapeDtypeStruct((r, c), t)
    return pl.pallas_call(
        functools.partial(table_kernel, half),
        out_shape=(out(all_rows, LANES, F32),) * 3 + (out(all_rows, LANES, jnp.int32), out(1, all_rows, jnp.int32)),
        in_specs=[smem(), smem(), vmem(), vmem()],
        out_specs=(vmem(),) * 5,
        compiler_params=params(),
        cost_estimate=COST,
        name="make_tables",
    )(me, lens, order, jnp.tile(frequency, LANES // half)[None, :])


def qkv_kernel(
    head_dim, x0_ref, x1_ref, x2_ref, x3a_ref, x3b_ref, w_ref, ocol_ref, cos_ref, su_ref, sd_ref,
    qg_ref, kg_ref, normed_ref, qx_ref, k_ref, v_ref, vx_ref, kt_ref, rawq_ref, rawk_ref, gain_ref, raw_ref,
):
    i = pl.program_id(0)
    tok = x0_ref.shape[0]
    all_rows, width = raw_ref.shape
    pairs = rawq_ref.shape[1] // LANES

    @pl.when(i == 0)
    def _():
        gain_ref[...] = jnp.transpose(w_ref[:, width:].astype(F32))[:8]

    def project(x, rows):
        x = x.astype(F32)
        r1 = lax.rsqrt(jnp.mean(x * x, axis=1, keepdims=True) + EPSILON)
        normed = (x * r1 * gain_ref[0:1, :]).astype(BF16)
        normed_ref[...] = normed
        raw_ref[rows, :] = dot_nn(normed, w_ref[:, :width]).astype(BF16)

    for d, refs in enumerate(((x0_ref,), (x1_ref,), (x2_ref,), (x3a_ref, x3b_ref))):

        @pl.when(i == d)
        def _(d=d, refs=refs):
            project(jnp.concatenate([ref[...] for ref in refs], axis=1), slice(d * tok, (d + 1) * tok))

    @pl.when(i >= 4)
    def _():
        ones = pair_ones(head_dim)
        low_lanes = lane_iota(tok, LANES) < head_dim
        pick = (ocol_ref[:, 0:1] == lane_iota(tok, all_rows)).astype(F32).astype(BF16)
        dealt = dot_nn(pick, raw_ref[...])
        cosine, su, sd = cos_ref[...], su_ref[...], sd_ref[...]
        for g in range(pairs):
            raw = dealt[:, g * LANES:(g + 1) * LANES]
            rawq_ref[:, g * LANES:(g + 1) * LANES] = raw.astype(BF16)
            rq = lax.rsqrt(head_mean(raw * raw, ones, head_dim) + EPSILON)
            pair = turn(raw * rq * qg_ref[...], cosine, su, sd, head_dim)
            for r, one in enumerate(spread_heads(pair, g, head_dim, low_lanes)):
                qx_ref[2 * g + r] = one.astype(BF16)
        raw = dealt[:, pairs * LANES:(pairs + 1) * LANES]
        rawk_ref[...] = raw.astype(BF16)
        rk = lax.rsqrt(head_mean(raw * raw, ones, head_dim) + EPSILON)
        keys = turn(raw * rk * kg_ref[...], cosine, su, sd, head_dim)
        k_ref[...] = keys.astype(BF16)
        kt_ref[...] = jnp.transpose(keys).astype(BF16)
        values = dealt[:, (pairs + 1) * LANES:]
        v_ref[...] = values.astype(BF16)
        vx_ref[0] = jnp.where(low_lanes, values, 1.0).astype(BF16)
        vx_ref[1] = jnp.where(low_lanes, 1.0, values).astype(BF16)


def fixed(array):
    return pl.BlockSpec(array.shape, lambda i: (0,) * array.ndim, pipeline_mode=pl.Buffered(1))


def qkv(xs, w, ocol, cosine, su, sd, qg, kg, head_dim):
    tok, width = xs[0].shape
    all_rows = 4 * tok
    out = lambda *dims: jax.ShapeDtypeStruct(dims, BF16)
    late = lambda c: pl.BlockSpec((tok, c), lambda i: (jnp.maximum(i - 4, 0), 0))
    heads = lambda n: pl.BlockSpec((n, tok, LANES), lambda i: (0, jnp.maximum(i - 4, 0), 0))
    return pl.pallas_call(
        functools.partial(qkv_kernel, head_dim),
        grid=(8,),
        out_shape=(
            out(all_rows, width), out(4, all_rows, LANES), out(all_rows, LANES), out(all_rows, LANES),
            out(2, all_rows, LANES), out(LANES, all_rows), out(all_rows, 2 * LANES), out(all_rows, LANES),
            jax.ShapeDtypeStruct((8, width), F32),
        ),
        in_specs=[fixed(x) for x in xs] + [fixed(w)] + [late(LANES)] * 4 + [fixed(qg), fixed(kg)],
        out_specs=(
            pl.BlockSpec((tok, width), lambda i: (jnp.minimum(i, 3), 0)),
            heads(4), late(LANES), late(LANES), heads(2),
            pl.BlockSpec((LANES, tok), lambda i: (0, jnp.maximum(i - 4, 0))), late(2 * LANES), late(LANES),
            pl.BlockSpec((8, width), lambda i: (0, 0)),
        ),
        scratch_shapes=[pltpu.VMEM((all_rows, 4 * LANES), BF16)],
        compiler_params=params(),
        cost_estimate=COST,
        name="qkv",
    )(*xs, w, ocol, cosine, su, sd, qg, kg)


def row_starts(lens_ref, index):
    start = jnp.zeros_like(index)
    end = lens_ref[0, 0]
    for s in range(1, lens_ref.shape[1]):
        start = jnp.where(index >= end, end, start)
        end = end + lens_ref[0, s]
    return start


def attend_kernel(head_dim, group, block, lens_ref, orow_ref, qx_ref, k_ref, vx_ref, *refs):
    given_ref, dealt_ref, lse_ref = refs[-3:]
    all_rows = k_ref.shape[0]
    scale = LOG2E * head_dim ** -0.5
    low_lanes = lane_iota(block, LANES) < head_dim
    mass_row = head_dim if group == 0 else 0

    def query_block(i, carry):
        rows = at_rows(i, block)
        q_index = i * block + row_iota(block, 1)
        start = row_starts(lens_ref, q_index)
        first = row_starts(lens_ref, i * block) // block
        clear = jnp.minimum((row_starts(lens_ref, i * block + block - 1) + block - 1) // block, i)
        queries = [qx_ref[r, rows, :] for r in range(2)]

        def step(j, state, masked):
            columns = at_rows(j, block)
            keys, values = k_ref[columns, :], vx_ref[0, columns, :]
            k_index = j * block + lane_iota(block, block)
            keep = (k_index <= q_index) & (k_index >= start)
            new = []
            for r in range(2):
                weights = jnp.exp2(dot_nt(queries[r], keys) * scale)
                if masked:
                    weights = jnp.where(keep, weights, 0.0)
                new.append(state[r] + dot_nn(weights.astype(BF16), values))
            return tuple(new)

        state = (jnp.zeros((block, LANES), F32),) * 2
        state = lax.fori_loop(first, clear, functools.partial(step, masked=True), state)
        state = lax.fori_loop(clear, i, functools.partial(step, masked=False), state)
        state = step(i, state, True)
        out = []
        for r in range(2):
            lse_ref[r:r + 1, rows] = jnp.log2(jnp.transpose(state[r])[mass_row:mass_row + 1, :])
            out.append(state[r] / pltpu.roll(state[r], head_dim, 1))
        if group == 0:
            pair = jnp.where(low_lanes, out[0], pltpu.roll(out[1], head_dim, 1))
        else:
            pair = jnp.where(low_lanes, pltpu.roll(out[0], head_dim, 1), out[1])
        dealt_ref[rows, :] = pair.astype(BF16)
        return carry

    lax.fori_loop(0, all_rows // block, query_block, 0)

    def undeal(i, carry):
        rows = at_rows(i, block)
        pick = (orow_ref[...] == i * block + row_iota(block, all_rows)).astype(F32).astype(BF16)
        given_ref[rows, :] = dot_nn(pick, dealt_ref[...]).astype(BF16)
        return carry

    lax.fori_loop(0, all_rows // block, undeal, 0)


def attend(group, lens, orow, qx, k, vx, head_dim, after):
    all_rows = k.shape[0]
    whole = lambda *dims: pl.BlockSpec(dims, lambda i: (0,) * len(dims))
    return pl.pallas_call(
        functools.partial(attend_kernel, head_dim, group, all_rows // 4),
        grid=(1,),
        out_shape=(
            jax.ShapeDtypeStruct((all_rows, LANES), BF16),
            jax.ShapeDtypeStruct((all_rows, LANES), BF16),
            jax.ShapeDtypeStruct((2, all_rows), F32),
        ),
        in_specs=[
            smem(), whole(1, all_rows),
            pl.BlockSpec((2, all_rows, LANES), lambda i: (group, 0, 0)),
            whole(all_rows, LANES),
            pl.BlockSpec((1, all_rows, LANES), lambda i: (group, 0, 0)),
        ] + anywhere(after),
        out_specs=(whole(all_rows, LANES), whole(all_rows, LANES), whole(2, all_rows)),
        compiler_params=params(),
        cost_estimate=COST,
        name="attend",
    )(lens, orow, qx, k, vx, *after)


def attend_back_kernel(head_dim, n_late, *refs):
    (lens_ref, ocol_ref, lse0_ref, lse1_ref, o0_ref, o1_ref, d0_ref, d1_ref, d2_ref, d3_ref, qg_ref, kg_ref) = refs[:12]
    late, refs = refs[12:12 + n_late], refs[-(2 + 5 + n_late + 1):]
    draw_ref, gain_ref, dgiven_ref, dx_ref, delta_ref, dk_ref, dv_ref = refs[:7]
    here, sems = refs[7:7 + n_late], refs[7 + n_late]
    qx_ref, k_ref, v_ref, kt_ref, rawq_ref, rawk_ref, cos_ref, su_ref, sd_ref = here
    copies = [pltpu.make_async_copy(late[n], here[n], sems.at[n]) for n in range(n_late)]
    for copy in copies:
        copy.start()
    all_rows = k_ref.shape[0]
    blocks = all_rows // ROWS
    exponent = LOG2E * head_dim ** -0.5
    scale = head_dim ** -0.5
    tok = d0_ref.shape[0]
    for d, ref in enumerate((d0_ref, d1_ref, d2_ref, d3_ref)):
        dgiven_ref[d * tok:(d + 1) * tok, :] = ref[...]
    dk_ref[...] = jnp.zeros_like(dk_ref)
    dv_ref[...] = jnp.zeros_like(dv_ref)
    gain_ref[...] = jnp.zeros_like(gain_ref)

    def deal(i, carry):
        rows = at_rows(i, tok)
        low_lanes = lane_iota(tok, LANES) < head_dim
        pick = (ocol_ref[rows, 0:1] == lane_iota(tok, all_rows)).astype(F32).astype(BF16)
        dealt = dot_nn(pick, dgiven_ref[...])
        for g, o_ref in enumerate((o0_ref, o1_ref)):
            pair = dealt[:, g * LANES:(g + 1) * LANES]
            for r, one in enumerate(spread_heads(pair, g, head_dim, low_lanes)):
                dx_ref[2 * g + r, rows, :] = one.astype(BF16)
            across = jnp.transpose(pair * o_ref[rows, :].astype(F32))
            for r in range(2):
                delta_ref[2 * g + r:2 * g + r + 1, rows] = jnp.sum(
                    across[r * head_dim:(r + 1) * head_dim], axis=0, keepdims=True
                )
        return carry

    lax.fori_loop(0, all_rows // tok, deal, 0)
    for copy in copies:
        copy.wait()
    ones = pair_ones(head_dim)

    def query_block(i, carry):
        rows = at_rows(i)
        q_index = i * ROWS + lane_iota(1, ROWS)
        start = row_starts(lens_ref, q_index)
        first = row_starts(lens_ref, i * ROWS) // ROWS
        count = (i + 2 - first) // 2
        base = jnp.maximum(i + 1 - 2 * count, 0)

        def step(n, state):
            at = base + 2 * n
            columns = pl.ds(pl.multiple_of(at * ROWS, ROWS), 2 * ROWS)
            k_index = at * ROWS + row_iota(2 * ROWS, ROWS)
            keep = (k_index <= q_index) & (k_index >= start)
            keys = k_ref[columns, :]
            values = v_ref[columns, :]
            new = []
            dk, dv = dk_ref[columns, :], dv_ref[columns, :]
            for h in range(4):
                g = h // 2
                queries = qx_ref[h, rows, :]
                grads = dx_ref[h, rows, :]
                lse = (lse0_ref, lse1_ref)[g][h % 2:h % 2 + 1, rows]
                weights = jnp.where(keep, jnp.exp2(dot_nt(keys, queries) * exponent - lse), 0.0)
                d_weights = dot_nt(values, grads)
                d_scores = (weights * (d_weights - delta_ref[h:h + 1, rows])).astype(BF16)
                dv = dv + dot_nn(weights.astype(BF16), grads)
                dk = dk + dot_nn(d_scores, queries)
                new.append(state[h] + dot_nn(kt_ref[g * head_dim:(g + 1) * head_dim, columns], d_scores))
            dk_ref[columns, :] = dk
            dv_ref[columns, :] = dv
            return tuple(new)

        state = lax.fori_loop(0, count, step, (jnp.zeros((head_dim, ROWS), F32),) * 4)
        cosine, su, sd = cos_ref[rows, :], su_ref[rows, :], sd_ref[rows, :]
        for g in range(2):
            pair = jnp.transpose(jnp.concatenate(state[2 * g:2 * g + 2], axis=0)) * scale
            lanes = slice(g * LANES, (g + 1) * LANES)
            draw, gain = norm_back(
                pair, rawq_ref[rows, lanes].astype(F32), qg_ref[...], cosine, su, sd, ones, head_dim
            )
            draw_ref[rows, lanes] = draw
            gain_ref[0:1, :] += gain
        return carry

    lax.fori_loop(0, blocks, query_block, 0)

    def key_block(i, carry):
        rows = at_rows(i, tok)
        cosine, su, sd = cos_ref[rows, :], su_ref[rows, :], sd_ref[rows, :]
        draw, gain = norm_back(
            dk_ref[rows, :] * scale, rawk_ref[rows, :].astype(F32), kg_ref[...], cosine, su, sd, ones, head_dim
        )
        draw_ref[rows, 2 * LANES:3 * LANES] = draw
        draw_ref[rows, 3 * LANES:] = dv_ref[rows, :].astype(BF16)
        gain_ref[1:2, :] += gain
        return carry

    lax.fori_loop(0, all_rows // tok, key_block, 0)


def rows_back_kernel(orow_ref, draw_ref, *refs):
    grad_ref, d_refs = refs[-5], refs[-4:]
    i = pl.program_id(0)
    all_rows = draw_ref.shape[0]
    rows = grad_ref.shape[0]
    pick = (orow_ref[...] == i * rows + row_iota(rows, all_rows)).astype(F32).astype(BF16)
    grads = dot_nn(pick, draw_ref[...]).astype(BF16)
    grad_ref[...] = grads
    for d, ref in enumerate(d_refs):

        @pl.when(i == d)
        def _(ref=ref):
            ref[...] = grads


def last_kernel(period, normed_ref, grads_ref, o0_ref, o1_ref, o2_ref, o3_ref, gain_ref, out_ref):
    width, extra = grads_ref.shape[1], o0_ref.shape[1]
    out_ref[:, :width] = dot_tn(normed_ref[...], grads_ref[...]).astype(BF16)
    total = o0_ref[...].astype(F32)
    for ref in (o1_ref, o2_ref, o3_ref):
        total = total + ref[...].astype(F32)
    out_ref[:, width:width + extra] = total.astype(BF16)
    place = row_iota(out_ref.shape[0], LANES) % period
    gains = jnp.where(place == 0, gain_ref[0:1, :], jnp.where(place == 1, gain_ref[1:2, :], 0.0))
    out_ref[:, width + extra:] = gains.astype(BF16)


def norm_back(pair, raw, gain, cosine, su, sd, ones, head_dim):
    pair = pair.astype(BF16).astype(F32)
    u = turn(pair, cosine, su, sd, head_dim, -1.0)
    r = lax.rsqrt(head_mean(raw * raw, ones, head_dim) + EPSILON)
    unit = raw * r
    scaled = u * gain
    draw = r * (scaled - unit * head_mean(scaled * unit, ones, head_dim))
    return draw.astype(BF16), jnp.sum(u * unit, axis=0, keepdims=True)


def anywhere(arrays):
    return [pl.BlockSpec(memory_space=pl.ANY)] * len(arrays)


def attend_back(lens, ocol, qx, k, v, kt, lses, dealts, grads, rawq, rawk, cosine, su, sd, qg, kg, head_dim):
    all_rows = k.shape[0]
    late = (qx, k, v, kt, rawq, rawk, cosine, su, sd)
    return pl.pallas_call(
        functools.partial(attend_back_kernel, head_dim, len(late)),
        out_shape=(
            jax.ShapeDtypeStruct((all_rows, 4 * LANES), BF16),
            jax.ShapeDtypeStruct((2, LANES), F32),
        ),
        in_specs=[smem()] + [vmem()] * 11 + anywhere(late),
        out_specs=(vmem(),) * 2,
        scratch_shapes=[
            pltpu.VMEM((all_rows, 2 * LANES), BF16),
            pltpu.VMEM((4, all_rows, LANES), BF16),
            pltpu.VMEM((4, all_rows), F32),
            pltpu.VMEM((all_rows, LANES), F32),
            pltpu.VMEM((all_rows, LANES), F32),
        ] + [pltpu.VMEM(a.shape, a.dtype) for a in late] + [pltpu.SemaphoreType.DMA((len(late),))],
        compiler_params=params(),
        cost_estimate=COST,
        name="attend_back",
    )(lens, ocol, *lses, *dealts, *grads, qg, kg, *late)


def rows_back(orow, draw, after):
    all_rows, width = draw.shape
    tok = all_rows // 4
    return pl.pallas_call(
        rows_back_kernel,
        grid=(4,),
        out_shape=(jax.ShapeDtypeStruct((all_rows, width), BF16),) + (jax.ShapeDtypeStruct((tok, width), BF16),) * 4,
        in_specs=[fixed(orow), fixed(draw)] + anywhere(after),
        out_specs=(pl.BlockSpec((tok, width), lambda i: (i, 0)),)
        + (pl.BlockSpec((tok, width), lambda i: (0, 0)),) * 4,
        compiler_params=params(),
        cost_estimate=COST,
        name="rows_back",
    )(orow, draw, *after)


def last_weights(normed, grads, parts, gains, shards):
    all_rows, width = grads.shape
    depth, extra = normed.shape[1], parts[0].shape[1]
    wide = width + extra + LANES
    block = lambda c: pl.BlockSpec((depth // 4, c), lambda i: (i, 0))
    return pl.pallas_call(
        functools.partial(last_kernel, depth // shards),
        grid=(4,),
        out_shape=jax.ShapeDtypeStruct((depth, wide), BF16),
        in_specs=[pl.BlockSpec((all_rows, depth // 4), lambda i: (0, i)), fixed(grads)]
        + [block(extra)] * 4 + [fixed(gains)],
        out_specs=block(wide),
        compiler_params=params(),
        cost_estimate=COST,
        name="last_weights",
    )(normed, grads, *parts, gains)


def tokens_kernel(me_ref, g0_ref, g1_ref, g2_ref, g3_ref, w_ref, x_ref, mid_ref, gain_ref, *refs):
    out_ref = refs[-1]
    me = me_ref[0]
    d_normed = jnp.zeros(x_ref.shape, F32)
    span, width = 2 * LANES, 8 * LANES
    for d, ref in enumerate((g0_ref, g1_ref, g2_ref, g3_ref)):
        other = jnp.bitwise_xor(me, d)
        take = lambda at, size: w_ref[:, pl.ds(pl.multiple_of(at + other * size, size), size)]
        weights = jnp.concatenate([take(0, span), take(width, LANES), take(width + 4 * LANES, LANES)], axis=1)
        d_normed = d_normed + dot_nt(ref[...], weights)
    x = x_ref[...].astype(F32)
    r1 = lax.rsqrt(jnp.mean(x * x, axis=1, keepdims=True) + EPSILON)
    scaled = d_normed * gain_ref[...]
    pull = jnp.mean(scaled * x, axis=1, keepdims=True)
    out_ref[...] = (mid_ref[...] + r1 * scaled - x * (r1 * r1 * r1 * pull)).astype(BF16)


def tokens_back(me, grads, w, x, d_middle, gain, after):
    tok, width = x.shape
    rows = lambda c: pl.BlockSpec((ROWS, c), lambda i: (i, 0))
    return pl.pallas_call(
        tokens_kernel,
        grid=(tok // ROWS,),
        out_shape=jax.ShapeDtypeStruct((tok, width), BF16),
        in_specs=[smem()] + [rows(grads[0].shape[1])] * 4 + [fixed(w), rows(width), rows(width), fixed(gain)] + anywhere(after),
        out_specs=rows(width),
        compiler_params=params(),
        cost_estimate=COST,
        name="tokens_back",
    )(me, *grads, w, x, d_middle, gain, *after)


def ffn_kernel(per, shards, blocks, n_carried, *refs):
    refs = list(refs)
    take = lambda n: [refs.pop(0) for _ in range(n)]
    me_ref = take(1)[0]
    att = [take(2 if d < 3 else 2 * len(blocks)) for d in range(4)]
    xs = [take(2 if d == 3 else 1) for d in blocks]
    cots = [take(2 if d == 3 else 1) for d in blocks]
    wo_ref, gain_ref, wg_ref, wu_ref, wd_ref = take(5)
    diag = take(4) if blocks == (1, 2) else None
    take(n_carried)
    nf_ref, hid_ref, dgu_ref, cot_ref = take(4)
    packed_ref, wd_ref = wd_ref, refs.pop()
    i = pl.program_id(0)
    me = me_ref[0]
    hidden_units = hid_ref.shape[1]
    which = i // per

    @pl.when(i == 0)
    def _():
        rows, piece = packed_ref.shape[0] // shards, wd_ref.shape[0] // shards
        for k in range(shards):
            block = packed_ref[k * rows:(k + 1) * rows, :]
            if piece % 16:
                block = block.astype(F32)
            wd_ref[k * piece:(k + 1) * piece, :] = unpack_rows(block, wd_ref.shape[1]).astype(BF16)

    def read(lists):
        parts = [jnp.concatenate([ref[...] for ref in one], axis=1) for one in lists]
        return parts[0] if len(parts) == 1 else jnp.where(which == 0, parts[0], parts[1])

    middle = read(xs).astype(F32)
    for d in range(4):
        block = read([att[d][2 * n:2 * n + 2] for n in range(len(att[d]) // 2)])
        middle = middle + dot_nn(block, wo_ref[at_rows(jnp.bitwise_xor(me, d), 2 * LANES), :middle.shape[1]])
    r2 = lax.rsqrt(jnp.mean(middle * middle, axis=1, keepdims=True) + EPSILON)
    nf = (middle * r2 * gain_ref[...]).astype(BF16)
    nf_ref[...] = nf
    cot = read(cots)
    cot_ref[...] = cot
    wg, wu = wg_ref[...], wu_ref[...]
    gate = dot_nn(nf, wg)
    up = dot_nn(nf, wu)
    s = jax.nn.sigmoid(gate)
    silu = gate * s
    hidden = (silu * up).astype(BF16)
    hid_ref[...] = hidden
    d_hidden = dot_nt(cot, wd_ref[...])
    d_gate = (d_hidden * up * s * (1.0 + gate * (1.0 - s))).astype(BF16)
    d_up = (d_hidden * silu).astype(BF16)
    dgu_ref[:, :hidden_units] = d_gate
    dgu_ref[:, hidden_units:] = d_up
    dn = dot_nt(d_gate, wg) + dot_nt(d_up, wu)
    bo = dot_nn(hidden, wd_ref[...])
    half = dn.shape[1] // 2
    if blocks == (3,):
        for ref, value in zip(take(4), (dn[:, :half], dn[:, half:], bo[:, :half], bo[:, half:])):
            ref[...] = value.astype(BF16)
    elif blocks == (0,):
        dn_ref, bo_ref, mid_ref = take(3)
        dn_ref[...] = dn.astype(BF16)
        bo_ref[...] = bo.astype(BF16)
        mid_ref[...] = middle
    else:
        dn1_ref, dn2_ref, bo1_ref, bo2_ref = take(4)

        @pl.when(which == 0)
        def _():
            for ref, value, extra in ((dn1_ref, dn, diag[1]), (bo1_ref, bo, diag[3])):
                ref[:, :half] = value[:, :half].astype(BF16)
                ref[:, half:] = (value[:, half:] + extra[...].astype(F32)).astype(BF16)

        @pl.when(which == 1)
        def _():
            for ref, value, extra in ((dn2_ref, dn, diag[0]), (bo2_ref, bo, diag[2])):
                ref[:, :half] = (value[:, :half] + extra[...].astype(F32)).astype(BF16)
                ref[:, half:] = value[:, half:].astype(BF16)


def ffn(me, blocks, att, xs, cots, gain, wide, shards, diag, carried, after):
    all_rows = att[0].shape[0]
    units, width = wide.shape[1] // 4, wide.shape[0]
    tok = all_rows // 4
    per = tok // ROWS
    block_of = lambda i: blocks[0] + (i // per) * (blocks[-1] - blocks[0])
    everywhere = lambda c: pl.BlockSpec((ROWS, c), lambda i: (block_of(i) * per + i % per, 0))
    crossed = lambda d: pl.BlockSpec(
        (ROWS, LANES), lambda i: (jnp.bitwise_xor(block_of(i), d) * per + i % per, 0)
    )
    held = lambda n, c: pl.BlockSpec((ROWS, c), lambda i: (jnp.clip(i - n * per, 0, per - 1), 0))
    halves = {0: 1, 1: 1, 2: 0, 3: 0}
    last = []
    for n, d in enumerate(blocks):
        local = lambda i, n=n, d=d: ((3 - d) % 2 * per + jnp.clip(i - n * per, 0, per - 1), 0)
        last += [(att[6], crossed(3)), (att[7 + halves[d]], pl.BlockSpec((ROWS, LANES), local))]
    weight = lambda n: pl.BlockSpec((wide.shape[0], units), lambda i: (0, n), pipeline_mode=pl.Buffered(1))
    out = lambda r, c, t=BF16: jax.ShapeDtypeStruct((r, c), t)
    pieces = lambda arrays: [held(n, a.shape[1]) for n, d in enumerate(blocks) for a in arrays[d]]
    shapes = [out(all_rows, width), out(all_rows, units), out(all_rows, 2 * units), out(all_rows, width)]
    specs = [everywhere(width), everywhere(units), everywhere(2 * units), everywhere(width)]
    if blocks == (3,):
        shapes += [out(tok, width // 2)] * 4
        specs += [held(0, width // 2)] * 4
    elif blocks == (0,):
        shapes += [out(tok, width)] * 2 + [out(tok, width, F32)]
        specs += [held(0, width)] * 3
    else:
        shapes += [out(tok, width)] * 4
        specs += [held(0, width), held(1, width)] * 2
    diag_specs = [held(1, width // 2), held(0, width // 2)] * 2 if diag else []
    operands = (
        [me] + list(att[:6]) + [a for a, _ in last] + [a for d in blocks for a in xs[d]] + [a for d in blocks for a in cots[d]]
        + [wide, gain, wide, wide, wide] + list(diag) + list(carried) + list(after)
    )
    first = len(operands) - len(carried) - len(after)
    return pl.pallas_call(
        functools.partial(ffn_kernel, per, shards, blocks, len(carried) + len(after)),
        grid=(len(blocks) * per,),
        out_shape=tuple(shapes),
        in_specs=[smem()] + [crossed(d) for d in range(3) for _ in range(2)] + [spec for _, spec in last]
        + pieces(xs) + pieces(cots) + [weight(3), fixed(gain), weight(0), weight(1), weight(2)] + diag_specs + anywhere(carried) + anywhere(after),
        out_specs=tuple(specs),
        input_output_aliases={first + n: n for n in range(len(carried))},
        scratch_shapes=[pltpu.VMEM((units, width), BF16)],
        compiler_params=params(),
        cost_estimate=COST,
        name="ffn",
    )(*operands)


DOWN_STEPS = 3


def weights_kernel(shards, nf_ref, dgu_from, hid_ref, cot_ref, out_ref, down_ref, dgu_ref, sem):
    i = pl.program_id(0)
    copy = pltpu.make_async_copy(dgu_from, dgu_ref, sem)

    @pl.when(i == 0)
    def _():
        copy.start()

    @pl.when(i < DOWN_STEPS)
    def _():
        down_ref[at_rows(i, hid_ref.shape[1]), :] = dot_tn(hid_ref[...], cot_ref[...])

    @pl.when(i == DOWN_STEPS)
    def _():
        copy.wait()

    @pl.when(i >= DOWN_STEPS)
    def _():
        out_ref[:, :dgu_ref.shape[1]] = dot_tn(nf_ref[...], dgu_ref[...]).astype(BF16)

    per, piece = shards // 4, down_ref.shape[0] // shards
    rows = out_ref.shape[0] // per
    for k in range(shards):

        @pl.when(i == DOWN_STEPS + k // per)
        def _(k=k):
            block = pack_rows(down_ref[k * piece:(k + 1) * piece, :], rows)
            at = k % per * rows
            out_ref[at:at + rows, dgu_ref.shape[1]:] = block.astype(BF16)


def weights_back(nf, d_gu, hidden, cot, shards):
    rows, depth = nf.shape
    late = lambda i: jnp.maximum(i - DOWN_STEPS, 0)
    units = hidden.shape[1]
    wide = d_gu.shape[1] + units
    return pl.pallas_call(
        functools.partial(weights_kernel, shards),
        grid=(DOWN_STEPS + 4,),
        out_shape=jax.ShapeDtypeStruct((depth, wide), BF16),
        in_specs=[
            pl.BlockSpec((rows, depth // 4), lambda i: (0, late(i))), pl.BlockSpec(memory_space=pl.ANY),
            pl.BlockSpec((rows, units // DOWN_STEPS), lambda i: (0, jnp.minimum(i, DOWN_STEPS - 1))), fixed(cot),
        ],
        out_specs=pl.BlockSpec((depth // 4, wide), lambda i: (late(i), 0)),
        scratch_shapes=[
            pltpu.VMEM((units, cot.shape[1]), F32), pltpu.VMEM(d_gu.shape, BF16), pltpu.SemaphoreType.DMA,
        ],
        compiler_params=params(),
        cost_estimate=COST,
        name="weights_back",
    )(nf, d_gu, hidden, cot)


def middle_kernel(*refs):
    me_ref, dn_refs = refs[0], refs[1:4]
    cot_ref, mid_ref, gain_ref, wide_ref = refs[4:8]
    dmid_ref, branch_ref, da_refs, wo_ref, sem = refs[-8], refs[-7], refs[-6:-2], refs[-2], refs[-1]
    at = wide_ref.shape[1] // 4 * 3
    copy = pltpu.make_async_copy(wide_ref.at[:, at:at + wo_ref.shape[1]], wo_ref, sem)
    copy.start()
    me = me_ref[0]
    tok = mid_ref.shape[0]

    def rows_of(i, carry):
        rows = at_rows(i)
        middle = mid_ref[rows, :]
        d_normed = dn_refs[0][rows, :].astype(F32)
        for ref in dn_refs[1:]:
            d_normed = d_normed + ref[rows, :].astype(F32)
        r2 = lax.rsqrt(jnp.mean(middle * middle, axis=1, keepdims=True) + EPSILON)
        scaled = d_normed * gain_ref[...]
        pull = jnp.mean(scaled * middle, axis=1, keepdims=True)
        d_middle = cot_ref[rows, :].astype(F32) + r2 * scaled - middle * (r2 * r2 * r2 * pull)
        dmid_ref[rows, :] = d_middle
        branch_ref[rows, :] = d_middle.astype(BF16)
        return carry

    lax.fori_loop(0, tok // ROWS, rows_of, 0)
    copy.wait()
    span = 2 * LANES
    for d in range(4):
        there = pl.ds(pl.multiple_of(jnp.bitwise_xor(me, d) * span, span), span)
        da_refs[d][...] = dot_nt(branch_ref[...], wo_ref[there, :branch_ref.shape[1]]).astype(BF16)


def out_kernel(me_ref, *refs):
    att_refs, branch_ref, outs = refs[:8], refs[8], refs[9:]
    span = 2 * LANES
    for d in range(4):
        there = pl.ds(pl.multiple_of(jnp.bitwise_xor(me_ref[0], d) * span, span), span)
        rows = jnp.concatenate([att_refs[2 * d][...], att_refs[2 * d + 1][...]], axis=1)
        for e in range(4):
            columns = pl.ds(pl.multiple_of(jnp.bitwise_xor(me_ref[0], e) * span, span), span)
            outs[e][there, :] = dot_tn(rows, branch_ref[:, columns]).astype(BF16)


def out_weights(me, att, branch):
    tok, width = branch.shape
    whole = lambda r, c: pl.BlockSpec((r, c), lambda i: (0, 0))
    own = lambda d: pl.BlockSpec((tok, LANES), lambda i: (d, 0))
    return pl.pallas_call(
        out_kernel,
        grid=(1,),
        out_shape=(jax.ShapeDtypeStruct((width, width // 4), BF16),) * 4,
        in_specs=[smem()] + [own(d) for d in (0, 0, 1, 1, 2, 2, 3, 1)] + [whole(tok, width)],
        out_specs=(whole(width, width // 4),) * 4,
        compiler_params=params(),
        cost_estimate=COST,
        name="out_weights",
    )(me, *att[:7], att[8], branch)


def middle_back(me, parts, cot, middle, gain, wide, after):
    tok, width = middle.shape
    whole = lambda r, c: pl.BlockSpec((r, c), lambda i: (0, 0))
    out = lambda r, c, t=BF16: jax.ShapeDtypeStruct((r, c), t)
    return pl.pallas_call(
        middle_kernel,
        grid=(1,),
        out_shape=(out(tok, width, F32), out(tok, width)) + (out(tok, 2 * LANES),) * 4,
        in_specs=[smem()] + [whole(tok, width)] * 5 + [whole(1, width)] + anywhere((wide,) + tuple(after)),
        out_specs=(whole(tok, width),) * 2 + (whole(tok, 2 * LANES),) * 4,
        scratch_shapes=[pltpu.VMEM((wide.shape[0], width), BF16), pltpu.SemaphoreType.DMA],
        compiler_params=params(),
        cost_estimate=COST,
        name="middle_back",
    )(me, *parts, cot, middle, gain, wide, *after)


def swap(array, distance):
    return lax.ppermute(array, "seq", [(s, s ^ distance) for s in range(4)])


def gather_rows(block, meanwhile):
    half = block.shape[1] // 2
    one, two = swap(block, 1), swap(block, 2)
    one, two, meanwhile = lax.optimization_barrier((one, two, meanwhile))
    return [meanwhile, [one], [two], [swap(one[:, :half], 2), swap(two[:, half:], 1)]]


def after(value, *others):
    return lax.optimization_barrier((value, others))[0]


def body(
    tokens, order, seq_lengths, attn_gain, w_query, w_key, w_value, query_gain, key_gain,
    w_out, ffn_gain, w_gate, w_up, w_down, cotangent,
):
    tok = tokens.shape[1]
    ways = lax.axis_size("seq")
    shards = lax.axis_size("shard")
    all_rows = tok * ways
    head_dim = query_gain.shape[0]
    me = lax.axis_index("seq")
    me_arr = me.astype(jnp.int32)[None]
    own = lambda a, axis: lax.dynamic_slice_in_dim(a, me * (a.shape[axis] // ways), a.shape[axis] // ways, axis)
    depth = w_gate.shape[0]
    units = w_gate.shape[1] // ways
    piece = units // shards

    cosine, sine_up, sine_down, ocol, orow = make_tables(me_arr, seq_lengths, order, head_dim)
    q_gain = jnp.tile(query_gain.astype(F32), LANES // head_dim)[None, :]
    k_gain = jnp.tile(key_gain.astype(F32), LANES // head_dim)[None, :]

    tables = (cosine, sine_up, sine_down, ocol, orow, q_gain, k_gain)

    xs = gather_rows(tokens[0], tables)
    w_first = first_weights(me_arr, w_query, w_key, w_value, attn_gain, ffn_gain)
    w_qkv = lax.all_gather(w_first, "shard", axis=0, tiled=True)
    w_cut = cut_weights(me_arr, w_gate, w_up, own(w_down, 0), w_out, shards)
    w_wide = lax.all_gather(after(w_cut, xs[1]), "shard", axis=0, tiled=True)

    cosine, sine_up, sine_down, ocol, orow, q_gain, k_gain = xs[0]
    xs = [[tokens[0]]] + xs[1:]
    normed, qx, k, v, vx, kt, rawq, rawk, gains = qkv(
        [x for one in xs for x in one], w_qkv, ocol, cosine, sine_up, sine_down, q_gain, k_gain, head_dim
    )
    cot = cotangent[0]
    cots = gather_rows(after(cot, xs[3]), gains)
    gains, cots = cots[0], [[cot]] + cots[1:]
    gain_a, gain_f = gains[0:1], gains[1:2]
    w_rows = jnp.concatenate(after([w_query, w_key, w_value], xs[3]), axis=1)
    w_all = lax.all_gather(w_rows, "shard", axis=0, tiled=True)

    att, dealts, lses = [], [], []
    for g in range(2):
        given, dealt, lse = attend(g, seq_lengths, orow, qx, k, vx, head_dim, [])
        one, two = swap(given, 1), swap(given, 2)
        half = given.shape[0] // 2
        three = [swap(one[:half], 2), swap(two[half:], 1)] if g else [swap(given, 3)]
        att.append([given, one, two] + three)
        dealts.append(dealt)
        lses.append(lse)
    att = [att[g][d] for d in range(3) for g in range(2)] + att[0][3:] + att[1][3:]

    feed = lambda blocks, diag, carried, after=(): ffn(
        me_arr, blocks, att, xs, cots, gain_f, w_wide, shards, diag, carried, after
    )
    *carried, dn3a, dn3b, bo3a, bo3b = feed((3,), (), (), att[8:])
    diag = (swap(dn3a, 1), swap(dn3b, 2), swap(bo3a, 1), swap(bo3b, 2))
    *carried, dn0, bo0, middle = feed((0,), (), carried)
    *carried, dn1, dn2, bo1, bo2 = feed((1, 2), diag, carried)
    nf, hidden, d_gu, cot_all = carried
    dn = (dn0, swap(dn1, 1), swap(dn2, 2))
    scatter = lambda a: lax.psum_scatter(a, "shard", scatter_dimension=0, tiled=True)
    p_ffn = weights_back(nf, d_gu, hidden, cot_all, shards)
    d_ffn = scatter(after(p_ffn, dn))

    d_middle, branch, *d_att = middle_back(me_arr, dn, cot, middle, gain_f, w_wide, (p_ffn, w_all))
    p_wo = out_weights(me_arr, att, branch)
    d_att = [d_att[0]] + [swap(d_att[d], d) for d in (1, 2, 3)]
    draw, head_gains = attend_back(
        seq_lengths, ocol, qx, k, v, kt, lses, dealts, d_att, rawq, rawk,
        cosine, sine_up, sine_down, q_gain, k_gain, head_dim,
    )
    bo1, bo2, *p_wo = after([bo1, bo2] + list(p_wo), d_att)
    bo = [bo0, swap(bo1, 1), swap(bo2, 2)]
    p_wo = [p_wo[0]] + [swap(p_wo[d], d) for d in (1, 2, 3)]
    grads, *d_raw = rows_back(orow, draw, bo[1:3])
    d_raw = [d_raw[0]] + [swap(d_raw[d], d) for d in (1, 2, 3)]
    p_last = last_weights(normed, grads, p_wo, head_gains, shards)
    block_out = (middle + sum(b.astype(F32) for b in after(bo, p_last))).astype(BF16)
    d_last = scatter(after(p_last, d_ffn, d_raw))
    d_tokens = tokens_back(me_arr, d_raw, w_all, tokens[0], d_middle, gain_a, (p_last,))
    d_ffn = after(d_ffn, d_raw, p_last)

    def two_stages(part):
        half = part.shape[1] // 2 // LANES * LANES
        one, two = swap(part, 1), swap(part, 2)
        return [part, one, two, swap(one[:, :half], 2), swap(two[:, half:], 1)]

    def parts_of(part):
        return [part] + [swap(part, d) for d in (1, 2, 3)]

    d_wg, d_wu, d_wd, d_ffn_gain = join_weights(me_arr, two_stages(d_ffn), w_gate, w_up, ffn_gain, w_down.shape, shards)
    d_wq, d_wk, d_wv, d_wo, d_attn_gain, d_query_gain, d_key_gain = join_last(
        me_arr, parts_of(after(d_last, d_ffn, d_tokens, block_out)), w_query, w_key, w_value, attn_gain,
        w_out.shape[1], head_dim,
    )
    return (
        block_out[None], d_tokens[None], d_attn_gain[0], d_wq, d_wk, d_wv, d_query_gain[0], d_key_gain[0],
        d_wo, d_ffn_gain[0], d_wg, d_wu, d_wd,
    )


def solution(mesh):
    rows, flat, wide = P("shard", None), P("shard"), P("shard", "seq", None)
    in_specs = (
        wide, rows, rows, flat, rows, rows, rows, P(), P(), rows, flat, rows, rows, rows, wide,
    )
    out_specs = (wide, wide, flat, rows, rows, rows, P(), P(), rows, flat, rows, rows, rows)
    return jax.shard_map(body, mesh=mesh, in_specs=in_specs, out_specs=out_specs, check_vma=False)
```

```python
import functools

import jax
import jax.numpy as jnp
from jax import lax
from jax.experimental import pallas as pl
from jax.experimental.pallas import tpu as pltpu
from jax.sharding import PartitionSpec as P

EPSILON = 1e-05
ROPE_BASE = 1000000.0
LOG2E = 1.4426950408889634
ROWS = 256
LANES = 128
F32 = jnp.float32
BF16 = jnp.bfloat16
COST = pl.CostEstimate(flops=1 << 20, bytes_accessed=1 << 16, transcendentals=0)
VMEM_LIMIT = 58 * 1024 * 1024


def dot_nn(left, right):
    return jnp.dot(left, right, preferred_element_type=F32)


def dot_nt(left, right):
    return lax.dot_general(left, right, (((1,), (1,)), ((), ())), preferred_element_type=F32)


def dot_tn(left, right):
    return lax.dot_general(left, right, (((0,), (0,)), ((), ())), preferred_element_type=F32)


def vmem():
    return pl.BlockSpec(memory_space=pltpu.VMEM)


def smem():
    return pl.BlockSpec(memory_space=pltpu.SMEM)


def params():
    return pltpu.CompilerParams(vmem_limit_bytes=VMEM_LIMIT)


def lane_iota(rows, columns):
    return lax.broadcasted_iota(jnp.int32, (rows, columns), 1)


def row_iota(rows, columns):
    return lax.broadcasted_iota(jnp.int32, (rows, columns), 0)


def at_rows(block, rows=ROWS):
    return pl.ds(pl.multiple_of(block * rows, rows), rows)


def pair_ones(head_dim):
    return (
        row_iota(LANES, LANES) // head_dim == lane_iota(LANES, LANES) // head_dim
    ).astype(BF16)


def head_mean(values, ones, head_dim):
    high = values.astype(BF16)
    low = (values - high.astype(F32)).astype(BF16)
    return (dot_nn(high, ones) + dot_nn(low, ones)) * (1.0 / head_dim)


def turn(values, cosine, sine_up, sine_down, head_dim, sign=1.0):
    half = head_dim // 2
    up = pltpu.roll(values, LANES - half, 1) * sine_up
    down = pltpu.roll(values, half, 1) * sine_down
    return values * cosine + sign * (up + down)


def spread_heads(pair, group, head_dim, low_lanes):
    moved = pltpu.roll(pair, head_dim, 1)
    if group == 0:
        return jnp.where(low_lanes, pair, 0.0), jnp.where(low_lanes, moved, 0.0)
    return jnp.where(low_lanes, 0.0, moved), jnp.where(low_lanes, 0.0, pair)


def first_kernel(me_ref, q_ref, k_ref, v_ref, ga_ref, gf_ref, out_ref):
    at = 0
    for ref in (q_ref, k_ref, v_ref):
        size = ref.shape[1] // 4
        out_ref[:, at:at + size] = ref[:, pl.ds(pl.multiple_of(me_ref[0] * size, size), size)]
        at += size
    depth = out_ref.shape[0]
    row = row_iota(LANES, depth)
    gains = jnp.where(row == 0, ga_ref[...].astype(F32), jnp.where(row == 1, gf_ref[...].astype(F32), 0.0))
    out_ref[:, at:] = jnp.transpose(gains).astype(BF16)


def first_weights(me, w_query, w_key, w_value, attn_gain, ffn_gain):
    depth = w_query.shape[0]
    width = (w_query.shape[1] + w_key.shape[1] + w_value.shape[1]) // 4 + LANES
    return pl.pallas_call(
        first_kernel,
        out_shape=jax.ShapeDtypeStruct((depth, width), BF16),
        in_specs=[smem()] + [vmem()] * 5,
        out_specs=vmem(),
        compiler_params=params(),
        cost_estimate=COST,
        name="first_weights",
    )(me, w_query, w_key, w_value, attn_gain[None], ffn_gain[None])


def pack_rows(block, rows):
    rest = [block[rows:, c:c + LANES] for c in range(0, block.shape[1], LANES)]
    return jnp.concatenate([block[:rows], jnp.concatenate(rest, axis=0)], axis=1)


def unpack_rows(block, width):
    rows = block.shape[0]
    extra = rows * LANES // width
    rest = [block[extra * c:extra * (c + 1), width:] for c in range(width // LANES)]
    return jnp.concatenate([block[:, :width], jnp.concatenate(rest, axis=1)], axis=0)


def cut_kernel(shards, me_ref, gate_ref, up_ref, down_ref, wo_ref, out_ref):
    whole, units = gate_ref.shape[1], gate_ref.shape[1] // 4
    piece, span = units // shards, whole // shards
    for at, ref in ((0, gate_ref), (units, up_ref)):
        turned = pltpu.roll(ref[...].astype(F32), whole - piece * me_ref[0], 1)
        parts = [turned[:, span * k:span * k + piece] for k in range(shards)]
        out_ref[:, at:at + units] = jnp.concatenate(parts, axis=1).astype(BF16)
    out_ref[:, 2 * units:3 * units] = pack_rows(down_ref[...].astype(F32), out_ref.shape[0]).astype(BF16)
    width = wo_ref.shape[1]
    out_ref[:, 3 * units:3 * units + width] = wo_ref[...]
    out_ref[:, 3 * units + width:] = jnp.zeros((out_ref.shape[0], units - width), BF16)


def cut_weights(me, w_gate, w_up, w_down, w_out, shards):
    depth, whole = w_gate.shape
    return pl.pallas_call(
        functools.partial(cut_kernel, shards),
        out_shape=jax.ShapeDtypeStruct((depth, whole), BF16),
        in_specs=[smem()] + [vmem()] * 4,
        out_specs=vmem(),
        compiler_params=params(),
        cost_estimate=COST,
        name="cut_weights",
    )(me, w_gate, w_up, w_down, w_out)


def divided_row(column, gain_ref):
    across = jnp.transpose(jnp.broadcast_to(column, (column.shape[0], LANES)))
    return across[0:1, :] / gain_ref[...].astype(F32)


def join_kernel(shards, me_ref, p0_ref, p1_ref, p2_ref, p3a_ref, p3b_ref, gate_ref, up_ref, gain_ref, dgate_ref, dup_ref, ddown_ref, dot_ref, st_ref):
    for d, ref in enumerate((p0_ref, p1_ref, p2_ref)):
        st_ref[d] = ref[...]
    st_ref[3] = jnp.concatenate([p3a_ref[...], p3b_ref[...]], axis=1)
    units = p0_ref.shape[1] // 3
    piece = units // shards
    quarters = [st_ref[jnp.bitwise_xor(me_ref[0], q)] for q in range(4)]
    total = 0.0
    for at, w_ref, out_ref in ((0, gate_ref, dgate_ref), (units, up_ref, dup_ref)):
        parts = [q[:, at:at + units].astype(F32) for q in quarters]
        parts = [q[:, piece * k:piece * (k + 1)] for k in range(shards) for q in parts]
        joined = jnp.concatenate(parts, axis=1)
        out_ref[...] = joined
        total = total + jnp.sum(joined * w_ref[...].astype(F32), axis=1, keepdims=True)
    dot_ref[...] = divided_row(total, gain_ref)
    for q, quarter in enumerate(quarters):
        block = unpack_rows(quarter[:, 2 * units:].astype(F32), ddown_ref.shape[1])
        ddown_ref[q * piece:(q + 1) * piece, :] = block


def join_weights(me, parts, w_gate, w_up, gain, down_shape, shards):
    depth, whole = w_gate.shape
    return pl.pallas_call(
        functools.partial(join_kernel, shards),
        out_shape=(jax.ShapeDtypeStruct((depth, whole), F32),) * 2
        + (jax.ShapeDtypeStruct(down_shape, F32), jax.ShapeDtypeStruct((1, depth), F32)),
        in_specs=[smem()] + [vmem()] * 8,
        out_specs=(vmem(),) * 4,
        scratch_shapes=[pltpu.VMEM((4,) + parts[0].shape, BF16)],
        compiler_params=params(),
        cost_estimate=COST,
        name="join_weights",
    )(me, *parts, w_gate, w_up, gain[None])


def join_last_kernel(me_ref, p0_ref, p1_ref, p2_ref, p3_ref, q_ref, k_ref, v_ref, gain_ref,
                     dq_ref, dk_ref, dv_ref, do_ref, dot_ref, qgain_ref, kgain_ref):
    at = 0
    parts = (p0_ref, p1_ref, p2_ref, p3_ref)
    total = jnp.zeros((dq_ref.shape[0], 1), F32)
    for out_ref, w_ref in ((dq_ref, q_ref), (dk_ref, k_ref), (dv_ref, v_ref), (do_ref, None)):
        size = out_ref.shape[1] // 4
        for d, ref in enumerate(parts):
            there = pl.ds(pl.multiple_of(jnp.bitwise_xor(me_ref[0], d) * size, size), size)
            part = ref[:, at:at + size].astype(F32)
            out_ref[:, there] = part
            if w_ref is not None:
                total = total + jnp.sum(part * w_ref[:, there].astype(F32), axis=1, keepdims=True)
        at += size
    dot_ref[...] = divided_row(total, gain_ref)
    gains = jnp.zeros((8, LANES), F32)
    for ref in parts:
        gains = gains + ref[0:16, at:].astype(F32)[:8]
    head_dim = qgain_ref.shape[1]
    gains = gains[:, :head_dim] + gains[:, head_dim:]
    qgain_ref[...] = gains[0:1]
    kgain_ref[...] = gains[1:2]


def join_last(me, parts, w_query, w_key, w_value, gain, out_width, head_dim):
    depth = w_query.shape[0]
    out = lambda c: jax.ShapeDtypeStruct((depth, c), F32)
    return pl.pallas_call(
        join_last_kernel,
        out_shape=(
            out(w_query.shape[1]), out(w_key.shape[1]), out(w_value.shape[1]), out(out_width),
            jax.ShapeDtypeStruct((1, depth), F32),
        ) + (jax.ShapeDtypeStruct((1, head_dim), F32),) * 2,
        in_specs=[smem()] + [vmem()] * 8,
        out_specs=(vmem(),) * 7,
        compiler_params=params(),
        cost_estimate=COST,
        name="join_last",
    )(me, *parts, w_query, w_key, w_value, gain[None])


def table_kernel(half, me_ref, lens_ref, order_ref, freq_ref, cos_ref, up_ref, down_ref, ocol_ref, orow_ref):
    all_rows = order_ref.shape[1]
    groups = LANES // half
    rows = all_rows // groups
    lane = lane_iota(rows, LANES)
    index = lane // half * rows + row_iota(rows, LANES)
    angles = (index - row_starts(lens_ref, index)).astype(F32) * freq_ref[...]
    cosine, sine = jnp.cos(angles), jnp.sin(angles)
    first = lane % (2 * half) < half
    for q in range(groups):

        def spread(table, q=q):
            one = jnp.where(lane < half, pltpu.roll(table, LANES - half * q, 1) if q else table, 0.0)
            return one + pltpu.roll(one, half, 1) + pltpu.roll(one, 2 * half, 1) + pltpu.roll(one, 3 * half, 1)

        here = slice(q * rows, (q + 1) * rows)
        cos_ref[here, :] = spread(cosine)
        wide = spread(sine)
        up_ref[here, :] = jnp.where(first, -wide, 0.0)
        down_ref[here, :] = jnp.where(first, 0.0, wide)
    relative = jnp.bitwise_xor(order_ref[...], me_ref[0] * (all_rows // 4))
    orow_ref[...] = relative
    for c in range(all_rows // LANES):
        here = slice(c * LANES, (c + 1) * LANES)
        across = jnp.broadcast_to(relative[:, here].astype(F32), (LANES, LANES))
        ocol_ref[here, :] = jnp.transpose(across).astype(jnp.int32)


def make_tables(me, lens, order, head_dim):
    all_rows = order.shape[1]
    half = head_dim // 2
    frequency = ROPE_BASE ** (-2.0 * jnp.arange(half, dtype=F32) / head_dim)
    out = lambda r, c, t: jax.ShapeDtypeStruct((r, c), t)
    return pl.pallas_call(
        functools.partial(table_kernel, half),
        out_shape=(out(all_rows, LANES, F32),) * 3 + (out(all_rows, LANES, jnp.int32), out(1, all_rows, jnp.int32)),
        in_specs=[smem(), smem(), vmem(), vmem()],
        out_specs=(vmem(),) * 5,
        compiler_params=params(),
        cost_estimate=COST,
        name="make_tables",
    )(me, lens, order, jnp.tile(frequency, LANES // half)[None, :])


def qkv_kernel(
    head_dim, x0_ref, x1_ref, x2_ref, x3a_ref, x3b_ref, w_ref, ocol_ref, cos_ref, su_ref, sd_ref,
    qg_ref, kg_ref, normed_ref, qx_ref, k_ref, v_ref, vx_ref, kt_ref, rawq_ref, rawk_ref, gain_ref, raw_ref,
):
    i = pl.program_id(0)
    tok = x0_ref.shape[0]
    all_rows, width = raw_ref.shape
    pairs = rawq_ref.shape[1] // LANES

    @pl.when(i == 0)
    def _():
        gain_ref[...] = jnp.transpose(w_ref[:, width:].astype(F32))[:8]

    def project(x, rows):
        x = x.astype(F32)
        r1 = lax.rsqrt(jnp.mean(x * x, axis=1, keepdims=True) + EPSILON)
        normed = (x * r1 * gain_ref[0:1, :]).astype(BF16)
        normed_ref[...] = normed
        raw_ref[rows, :] = dot_nn(normed, w_ref[:, :width]).astype(BF16)

    for d, refs in enumerate(((x0_ref,), (x1_ref,), (x2_ref,), (x3a_ref, x3b_ref))):

        @pl.when(i == d)
        def _(d=d, refs=refs):
            project(jnp.concatenate([ref[...] for ref in refs], axis=1), slice(d * tok, (d + 1) * tok))

    @pl.when(i >= 4)
    def _():
        ones = pair_ones(head_dim)
        low_lanes = lane_iota(tok, LANES) < head_dim
        pick = (ocol_ref[:, 0:1] == lane_iota(tok, all_rows)).astype(F32).astype(BF16)
        dealt = dot_nn(pick, raw_ref[...])
        cosine, su, sd = cos_ref[...], su_ref[...], sd_ref[...]
        for g in range(pairs):
            raw = dealt[:, g * LANES:(g + 1) * LANES]
            rawq_ref[:, g * LANES:(g + 1) * LANES] = raw.astype(BF16)
            rq = lax.rsqrt(head_mean(raw * raw, ones, head_dim) + EPSILON)
            pair = turn(raw * rq * qg_ref[...], cosine, su, sd, head_dim)
            for r, one in enumerate(spread_heads(pair, g, head_dim, low_lanes)):
                qx_ref[2 * g + r] = one.astype(BF16)
        raw = dealt[:, pairs * LANES:(pairs + 1) * LANES]
        rawk_ref[...] = raw.astype(BF16)
        rk = lax.rsqrt(head_mean(raw * raw, ones, head_dim) + EPSILON)
        keys = turn(raw * rk * kg_ref[...], cosine, su, sd, head_dim)
        k_ref[...] = keys.astype(BF16)
        kt_ref[...] = jnp.transpose(keys).astype(BF16)
        values = dealt[:, (pairs + 1) * LANES:]
        v_ref[...] = values.astype(BF16)
        vx_ref[0] = jnp.where(low_lanes, values, 1.0).astype(BF16)
        vx_ref[1] = jnp.where(low_lanes, 1.0, values).astype(BF16)


def fixed(array):
    return pl.BlockSpec(array.shape, lambda i: (0,) * array.ndim, pipeline_mode=pl.Buffered(1))


def qkv(xs, w, ocol, cosine, su, sd, qg, kg, head_dim):
    tok, width = xs[0].shape
    all_rows = 4 * tok
    out = lambda *dims: jax.ShapeDtypeStruct(dims, BF16)
    late = lambda c: pl.BlockSpec((tok, c), lambda i: (jnp.maximum(i - 4, 0), 0))
    heads = lambda n: pl.BlockSpec((n, tok, LANES), lambda i: (0, jnp.maximum(i - 4, 0), 0))
    return pl.pallas_call(
        functools.partial(qkv_kernel, head_dim),
        grid=(8,),
        out_shape=(
            out(all_rows, width), out(4, all_rows, LANES), out(all_rows, LANES), out(all_rows, LANES),
            out(2, all_rows, LANES), out(LANES, all_rows), out(all_rows, 2 * LANES), out(all_rows, LANES),
            jax.ShapeDtypeStruct((8, width), F32),
        ),
        in_specs=[fixed(x) for x in xs] + [fixed(w)] + [late(LANES)] * 4 + [fixed(qg), fixed(kg)],
        out_specs=(
            pl.BlockSpec((tok, width), lambda i: (jnp.minimum(i, 3), 0)),
            heads(4), late(LANES), late(LANES), heads(2),
            pl.BlockSpec((LANES, tok), lambda i: (0, jnp.maximum(i - 4, 0))), late(2 * LANES), late(LANES),
            pl.BlockSpec((8, width), lambda i: (0, 0)),
        ),
        scratch_shapes=[pltpu.VMEM((all_rows, 4 * LANES), BF16)],
        compiler_params=params(),
        cost_estimate=COST,
        name="qkv",
    )(*xs, w, ocol, cosine, su, sd, qg, kg)


def row_starts(lens_ref, index):
    start = jnp.zeros_like(index)
    end = lens_ref[0, 0]
    for s in range(1, lens_ref.shape[1]):
        start = jnp.where(index >= end, end, start)
        end = end + lens_ref[0, s]
    return start


def attend_kernel(head_dim, group, block, lens_ref, orow_ref, qx_ref, k_ref, vx_ref, *refs):
    given_ref, dealt_ref, lse_ref = refs[-3:]
    all_rows = k_ref.shape[0]
    scale = LOG2E * head_dim ** -0.5
    low_lanes = lane_iota(block, LANES) < head_dim
    mass_row = head_dim if group == 0 else 0

    def query_block(i, carry):
        rows = at_rows(i, block)
        q_index = i * block + row_iota(block, 1)
        start = row_starts(lens_ref, q_index)
        first = row_starts(lens_ref, i * block) // block
        clear = jnp.minimum((row_starts(lens_ref, i * block + block - 1) + block - 1) // block, i)
        queries = [qx_ref[r, rows, :] for r in range(2)]

        def step(j, state, masked):
            columns = at_rows(j, block)
            keys, values = k_ref[columns, :], vx_ref[0, columns, :]
            k_index = j * block + lane_iota(block, block)
            keep = (k_index <= q_index) & (k_index >= start)
            new = []
            for r in range(2):
                weights = jnp.exp2(dot_nt(queries[r], keys) * scale)
                if masked:
                    weights = jnp.where(keep, weights, 0.0)
                new.append(state[r] + dot_nn(weights.astype(BF16), values))
            return tuple(new)

        state = (jnp.zeros((block, LANES), F32),) * 2
        state = lax.fori_loop(first, clear, functools.partial(step, masked=True), state)
        state = lax.fori_loop(clear, i, functools.partial(step, masked=False), state)
        state = step(i, state, True)
        out = []
        for r in range(2):
            lse_ref[r:r + 1, rows] = jnp.log2(jnp.transpose(state[r])[mass_row:mass_row + 1, :])
            out.append(state[r] / pltpu.roll(state[r], head_dim, 1))
        if group == 0:
            pair = jnp.where(low_lanes, out[0], pltpu.roll(out[1], head_dim, 1))
        else:
            pair = jnp.where(low_lanes, pltpu.roll(out[0], head_dim, 1), out[1])
        dealt_ref[rows, :] = pair.astype(BF16)
        return carry

    lax.fori_loop(0, all_rows // block, query_block, 0)

    def undeal(i, carry):
        rows = at_rows(i, block)
        pick = (orow_ref[...] == i * block + row_iota(block, all_rows)).astype(F32).astype(BF16)
        given_ref[rows, :] = dot_nn(pick, dealt_ref[...]).astype(BF16)
        return carry

    lax.fori_loop(0, all_rows // block, undeal, 0)


def attend(group, lens, orow, qx, k, vx, head_dim, after):
    all_rows = k.shape[0]
    whole = lambda *dims: pl.BlockSpec(dims, lambda i: (0,) * len(dims))
    return pl.pallas_call(
        functools.partial(attend_kernel, head_dim, group, all_rows // 4),
        grid=(1,),
        out_shape=(
            jax.ShapeDtypeStruct((all_rows, LANES), BF16),
            jax.ShapeDtypeStruct((all_rows, LANES), BF16),
            jax.ShapeDtypeStruct((2, all_rows), F32),
        ),
        in_specs=[
            smem(), whole(1, all_rows),
            pl.BlockSpec((2, all_rows, LANES), lambda i: (group, 0, 0)),
            whole(all_rows, LANES),
            pl.BlockSpec((1, all_rows, LANES), lambda i: (group, 0, 0)),
        ] + anywhere(after),
        out_specs=(whole(all_rows, LANES), whole(all_rows, LANES), whole(2, all_rows)),
        compiler_params=params(),
        cost_estimate=COST,
        name="attend",
    )(lens, orow, qx, k, vx, *after)


def attend_back_kernel(head_dim, n_late, *refs):
    (lens_ref, ocol_ref, lse0_ref, lse1_ref, o0_ref, o1_ref, d0_ref, d1_ref, d2_ref, d3_ref, qg_ref, kg_ref) = refs[:12]
    late, refs = refs[12:12 + n_late], refs[-(2 + 5 + n_late + 1):]
    draw_ref, gain_ref, dgiven_ref, dx_ref, delta_ref, dk_ref, dv_ref = refs[:7]
    here, sems = refs[7:7 + n_late], refs[7 + n_late]
    qx_ref, k_ref, v_ref, kt_ref, rawq_ref, rawk_ref, cos_ref, su_ref, sd_ref = here
    copies = [pltpu.make_async_copy(late[n], here[n], sems.at[n]) for n in range(n_late)]
    for copy in copies:
        copy.start()
    all_rows = k_ref.shape[0]
    blocks = all_rows // ROWS
    exponent = LOG2E * head_dim ** -0.5
    scale = head_dim ** -0.5
    tok = d0_ref.shape[0]
    for d, ref in enumerate((d0_ref, d1_ref, d2_ref, d3_ref)):
        dgiven_ref[d * tok:(d + 1) * tok, :] = ref[...]
    dk_ref[...] = jnp.zeros_like(dk_ref)
    dv_ref[...] = jnp.zeros_like(dv_ref)
    gain_ref[...] = jnp.zeros_like(gain_ref)

    def deal(i, carry):
        rows = at_rows(i, tok)
        low_lanes = lane_iota(tok, LANES) < head_dim
        pick = (ocol_ref[rows, 0:1] == lane_iota(tok, all_rows)).astype(F32).astype(BF16)
        dealt = dot_nn(pick, dgiven_ref[...])
        for g, o_ref in enumerate((o0_ref, o1_ref)):
            pair = dealt[:, g * LANES:(g + 1) * LANES]
            for r, one in enumerate(spread_heads(pair, g, head_dim, low_lanes)):
                dx_ref[2 * g + r, rows, :] = one.astype(BF16)
            across = jnp.transpose(pair * o_ref[rows, :].astype(F32))
            for r in range(2):
                delta_ref[2 * g + r:2 * g + r + 1, rows] = jnp.sum(
                    across[r * head_dim:(r + 1) * head_dim], axis=0, keepdims=True
                )
        return carry

    lax.fori_loop(0, all_rows // tok, deal, 0)
    for copy in copies:
        copy.wait()
    ones = pair_ones(head_dim)

    def query_block(i, carry):
        rows = at_rows(i)
        q_index = i * ROWS + lane_iota(1, ROWS)
        start = row_starts(lens_ref, q_index)
        first = row_starts(lens_ref, i * ROWS) // ROWS
        count = (i + 2 - first) // 2
        base = jnp.maximum(i + 1 - 2 * count, 0)

        def step(n, state):
            at = base + 2 * n
            columns = pl.ds(pl.multiple_of(at * ROWS, ROWS), 2 * ROWS)
            k_index = at * ROWS + row_iota(2 * ROWS, ROWS)
            keep = (k_index <= q_index) & (k_index >= start)
            keys = k_ref[columns, :]
            values = v_ref[columns, :]
            new = []
            dk, dv = dk_ref[columns, :], dv_ref[columns, :]
            for h in range(4):
                g = h // 2
                queries = qx_ref[h, rows, :]
                grads = dx_ref[h, rows, :]
                lse = (lse0_ref, lse1_ref)[g][h % 2:h % 2 + 1, rows]
                weights = jnp.where(keep, jnp.exp2(dot_nt(keys, queries) * exponent - lse), 0.0)
                d_weights = dot_nt(values, grads)
                d_scores = (weights * (d_weights - delta_ref[h:h + 1, rows])).astype(BF16)
                dv = dv + dot_nn(weights.astype(BF16), grads)
                dk = dk + dot_nn(d_scores, queries)
                new.append(state[h] + dot_nn(kt_ref[g * head_dim:(g + 1) * head_dim, columns], d_scores))
            dk_ref[columns, :] = dk
            dv_ref[columns, :] = dv
            return tuple(new)

        state = lax.fori_loop(0, count, step, (jnp.zeros((head_dim, ROWS), F32),) * 4)
        cosine, su, sd = cos_ref[rows, :], su_ref[rows, :], sd_ref[rows, :]
        for g in range(2):
            pair = jnp.transpose(jnp.concatenate(state[2 * g:2 * g + 2], axis=0)) * scale
            lanes = slice(g * LANES, (g + 1) * LANES)
            draw, gain = norm_back(
                pair, rawq_ref[rows, lanes].astype(F32), qg_ref[...], cosine, su, sd, ones, head_dim
            )
            draw_ref[rows, lanes] = draw
            gain_ref[0:1, :] += gain
        return carry

    lax.fori_loop(0, blocks, query_block, 0)

    def key_block(i, carry):
        rows = at_rows(i, tok)
        cosine, su, sd = cos_ref[rows, :], su_ref[rows, :], sd_ref[rows, :]
        draw, gain = norm_back(
            dk_ref[rows, :] * scale, rawk_ref[rows, :].astype(F32), kg_ref[...], cosine, su, sd, ones, head_dim
        )
        draw_ref[rows, 2 * LANES:3 * LANES] = draw
        draw_ref[rows, 3 * LANES:] = dv_ref[rows, :].astype(BF16)
        gain_ref[1:2, :] += gain
        return carry

    lax.fori_loop(0, all_rows // tok, key_block, 0)


def rows_back_kernel(orow_ref, draw_ref, *refs):
    grad_ref, d_refs = refs[-5], refs[-4:]
    i = pl.program_id(0)
    all_rows = draw_ref.shape[0]
    rows = grad_ref.shape[0]
    pick = (orow_ref[...] == i * rows + row_iota(rows, all_rows)).astype(F32).astype(BF16)
    grads = dot_nn(pick, draw_ref[...]).astype(BF16)
    grad_ref[...] = grads
    for d, ref in enumerate(d_refs):

        @pl.when(i == d)
        def _(ref=ref):
            ref[...] = grads


def last_kernel(period, normed_ref, grads_ref, o0_ref, o1_ref, o2_ref, o3_ref, gain_ref, out_ref):
    width, extra = grads_ref.shape[1], o0_ref.shape[1]
    out_ref[:, :width] = dot_tn(normed_ref[...], grads_ref[...]).astype(BF16)
    total = o0_ref[...].astype(F32)
    for ref in (o1_ref, o2_ref, o3_ref):
        total = total + ref[...].astype(F32)
    out_ref[:, width:width + extra] = total.astype(BF16)
    place = row_iota(out_ref.shape[0], LANES) % period
    gains = jnp.where(place == 0, gain_ref[0:1, :], jnp.where(place == 1, gain_ref[1:2, :], 0.0))
    out_ref[:, width + extra:] = gains.astype(BF16)


def norm_back(pair, raw, gain, cosine, su, sd, ones, head_dim):
    pair = pair.astype(BF16).astype(F32)
    u = turn(pair, cosine, su, sd, head_dim, -1.0)
    r = lax.rsqrt(head_mean(raw * raw, ones, head_dim) + EPSILON)
    unit = raw * r
    scaled = u * gain
    draw = r * (scaled - unit * head_mean(scaled * unit, ones, head_dim))
    return draw.astype(BF16), jnp.sum(u * unit, axis=0, keepdims=True)


def anywhere(arrays):
    return [pl.BlockSpec(memory_space=pl.ANY)] * len(arrays)


def attend_back(lens, ocol, qx, k, v, kt, lses, dealts, grads, rawq, rawk, cosine, su, sd, qg, kg, head_dim):
    all_rows = k.shape[0]
    late = (qx, k, v, kt, rawq, rawk, cosine, su, sd)
    return pl.pallas_call(
        functools.partial(attend_back_kernel, head_dim, len(late)),
        out_shape=(
            jax.ShapeDtypeStruct((all_rows, 4 * LANES), BF16),
            jax.ShapeDtypeStruct((2, LANES), F32),
        ),
        in_specs=[smem()] + [vmem()] * 11 + anywhere(late),
        out_specs=(vmem(),) * 2,
        scratch_shapes=[
            pltpu.VMEM((all_rows, 2 * LANES), BF16),
            pltpu.VMEM((4, all_rows, LANES), BF16),
            pltpu.VMEM((4, all_rows), F32),
            pltpu.VMEM((all_rows, LANES), F32),
            pltpu.VMEM((all_rows, LANES), F32),
        ] + [pltpu.VMEM(a.shape, a.dtype) for a in late] + [pltpu.SemaphoreType.DMA((len(late),))],
        compiler_params=params(),
        cost_estimate=COST,
        name="attend_back",
    )(lens, ocol, *lses, *dealts, *grads, qg, kg, *late)


def rows_back(orow, draw, after):
    all_rows, width = draw.shape
    tok = all_rows // 4
    return pl.pallas_call(
        rows_back_kernel,
        grid=(4,),
        out_shape=(jax.ShapeDtypeStruct((all_rows, width), BF16),) + (jax.ShapeDtypeStruct((tok, width), BF16),) * 4,
        in_specs=[fixed(orow), fixed(draw)] + anywhere(after),
        out_specs=(pl.BlockSpec((tok, width), lambda i: (i, 0)),)
        + (pl.BlockSpec((tok, width), lambda i: (0, 0)),) * 4,
        compiler_params=params(),
        cost_estimate=COST,
        name="rows_back",
    )(orow, draw, *after)


def last_weights(normed, grads, parts, gains, shards):
    all_rows, width = grads.shape
    depth, extra = normed.shape[1], parts[0].shape[1]
    wide = width + extra + LANES
    block = lambda c: pl.BlockSpec((depth // 4, c), lambda i: (i, 0))
    return pl.pallas_call(
        functools.partial(last_kernel, depth // shards),
        grid=(4,),
        out_shape=jax.ShapeDtypeStruct((depth, wide), BF16),
        in_specs=[pl.BlockSpec((all_rows, depth // 4), lambda i: (0, i)), fixed(grads)]
        + [block(extra)] * 4 + [fixed(gains)],
        out_specs=block(wide),
        compiler_params=params(),
        cost_estimate=COST,
        name="last_weights",
    )(normed, grads, *parts, gains)


def tokens_kernel(me_ref, g0_ref, g1_ref, g2_ref, g3_ref, w_ref, x_ref, mid_ref, gain_ref, *refs):
    out_ref = refs[-1]
    me = me_ref[0]
    d_normed = jnp.zeros(x_ref.shape, F32)
    span, width = 2 * LANES, 8 * LANES
    for d, ref in enumerate((g0_ref, g1_ref, g2_ref, g3_ref)):
        other = jnp.bitwise_xor(me, d)
        take = lambda at, size: w_ref[:, pl.ds(pl.multiple_of(at + other * size, size), size)]
        weights = jnp.concatenate([take(0, span), take(width, LANES), take(width + 4 * LANES, LANES)], axis=1)
        d_normed = d_normed + dot_nt(ref[...], weights)
    x = x_ref[...].astype(F32)
    r1 = lax.rsqrt(jnp.mean(x * x, axis=1, keepdims=True) + EPSILON)
    scaled = d_normed * gain_ref[...]
    pull = jnp.mean(scaled * x, axis=1, keepdims=True)
    out_ref[...] = (mid_ref[...] + r1 * scaled - x * (r1 * r1 * r1 * pull)).astype(BF16)


def tokens_back(me, grads, w, x, d_middle, gain, after):
    tok, width = x.shape
    rows = lambda c: pl.BlockSpec((ROWS, c), lambda i: (i, 0))
    return pl.pallas_call(
        tokens_kernel,
        grid=(tok // ROWS,),
        out_shape=jax.ShapeDtypeStruct((tok, width), BF16),
        in_specs=[smem()] + [rows(grads[0].shape[1])] * 4 + [fixed(w), rows(width), rows(width), fixed(gain)] + anywhere(after),
        out_specs=rows(width),
        compiler_params=params(),
        cost_estimate=COST,
        name="tokens_back",
    )(me, *grads, w, x, d_middle, gain, *after)


def ffn_kernel(per, shards, blocks, n_carried, *refs):
    refs = list(refs)
    take = lambda n: [refs.pop(0) for _ in range(n)]
    me_ref = take(1)[0]
    att = [take(2 if d < 3 else 2 * len(blocks)) for d in range(4)]
    xs = [take(2 if d == 3 else 1) for d in blocks]
    cots = [take(2 if d == 3 else 1) for d in blocks]
    wo_ref, gain_ref, wg_ref, wu_ref, wd_ref = take(5)
    diag = take(4) if blocks == (1, 2) else None
    take(n_carried)
    nf_ref, hid_ref, dgu_ref, cot_ref = take(4)
    packed_ref, wd_ref = wd_ref, refs.pop()
    i = pl.program_id(0)
    me = me_ref[0]
    hidden_units = hid_ref.shape[1]
    which = i // per

    @pl.when(i == 0)
    def _():
        rows, piece = packed_ref.shape[0] // shards, wd_ref.shape[0] // shards
        for k in range(shards):
            block = packed_ref[k * rows:(k + 1) * rows, :]
            if piece % 16:
                block = block.astype(F32)
            wd_ref[k * piece:(k + 1) * piece, :] = unpack_rows(block, wd_ref.shape[1]).astype(BF16)

    def read(lists):
        parts = [jnp.concatenate([ref[...] for ref in one], axis=1) for one in lists]
        return parts[0] if len(parts) == 1 else jnp.where(which == 0, parts[0], parts[1])

    middle = read(xs).astype(F32)
    for d in range(4):
        block = read([att[d][2 * n:2 * n + 2] for n in range(len(att[d]) // 2)])
        middle = middle + dot_nn(block, wo_ref[at_rows(jnp.bitwise_xor(me, d), 2 * LANES), :middle.shape[1]])
    r2 = lax.rsqrt(jnp.mean(middle * middle, axis=1, keepdims=True) + EPSILON)
    nf = (middle * r2 * gain_ref[...]).astype(BF16)
    nf_ref[...] = nf
    cot = read(cots)
    cot_ref[...] = cot
    wg, wu = wg_ref[...], wu_ref[...]
    gate = dot_nn(nf, wg)
    up = dot_nn(nf, wu)
    s = jax.nn.sigmoid(gate)
    silu = gate * s
    hidden = (silu * up).astype(BF16)
    hid_ref[...] = hidden
    d_hidden = dot_nt(cot, wd_ref[...])
    d_gate = (d_hidden * up * s * (1.0 + gate * (1.0 - s))).astype(BF16)
    d_up = (d_hidden * silu).astype(BF16)
    dgu_ref[:, :hidden_units] = d_gate
    dgu_ref[:, hidden_units:] = d_up
    dn = dot_nt(d_gate, wg) + dot_nt(d_up, wu)
    bo = dot_nn(hidden, wd_ref[...])
    half = dn.shape[1] // 2
    if blocks == (3,):
        for ref, value in zip(take(4), (dn[:, :half], dn[:, half:], bo[:, :half], bo[:, half:])):
            ref[...] = value.astype(BF16)
    elif blocks == (0,):
        dn_ref, bo_ref, mid_ref = take(3)
        dn_ref[...] = dn.astype(BF16)
        bo_ref[...] = bo.astype(BF16)
        mid_ref[...] = middle
    else:
        dn1_ref, dn2_ref, bo1_ref, bo2_ref = take(4)

        @pl.when(which == 0)
        def _():
            for ref, value, extra in ((dn1_ref, dn, diag[1]), (bo1_ref, bo, diag[3])):
                ref[:, :half] = value[:, :half].astype(BF16)
                ref[:, half:] = (value[:, half:] + extra[...].astype(F32)).astype(BF16)

        @pl.when(which == 1)
        def _():
            for ref, value, extra in ((dn2_ref, dn, diag[0]), (bo2_ref, bo, diag[2])):
                ref[:, :half] = (value[:, :half] + extra[...].astype(F32)).astype(BF16)
                ref[:, half:] = value[:, half:].astype(BF16)


def ffn(me, blocks, att, xs, cots, gain, wide, shards, diag, carried, after):
    all_rows = att[0].shape[0]
    units, width = wide.shape[1] // 4, wide.shape[0]
    tok = all_rows // 4
    per = tok // ROWS
    block_of = lambda i: blocks[0] + (i // per) * (blocks[-1] - blocks[0])
    everywhere = lambda c: pl.BlockSpec((ROWS, c), lambda i: (block_of(i) * per + i % per, 0))
    crossed = lambda d: pl.BlockSpec(
        (ROWS, LANES), lambda i: (jnp.bitwise_xor(block_of(i), d) * per + i % per, 0)
    )
    held = lambda n, c: pl.BlockSpec((ROWS, c), lambda i: (jnp.clip(i - n * per, 0, per - 1), 0))
    halves = {0: 1, 1: 1, 2: 0, 3: 0}
    last = []
    for n, d in enumerate(blocks):
        local = lambda i, n=n, d=d: ((3 - d) % 2 * per + jnp.clip(i - n * per, 0, per - 1), 0)
        last += [(att[6], crossed(3)), (att[7 + halves[d]], pl.BlockSpec((ROWS, LANES), local))]
    weight = lambda n: pl.BlockSpec((wide.shape[0], units), lambda i: (0, n), pipeline_mode=pl.Buffered(1))
    out = lambda r, c, t=BF16: jax.ShapeDtypeStruct((r, c), t)
    pieces = lambda arrays: [held(n, a.shape[1]) for n, d in enumerate(blocks) for a in arrays[d]]
    shapes = [out(all_rows, width), out(all_rows, units), out(all_rows, 2 * units), out(all_rows, width)]
    specs = [everywhere(width), everywhere(units), everywhere(2 * units), everywhere(width)]
    if blocks == (3,):
        shapes += [out(tok, width // 2)] * 4
        specs += [held(0, width // 2)] * 4
    elif blocks == (0,):
        shapes += [out(tok, width)] * 2 + [out(tok, width, F32)]
        specs += [held(0, width)] * 3
    else:
        shapes += [out(tok, width)] * 4
        specs += [held(0, width), held(1, width)] * 2
    diag_specs = [held(1, width // 2), held(0, width // 2)] * 2 if diag else []
    operands = (
        [me] + list(att[:6]) + [a for a, _ in last] + [a for d in blocks for a in xs[d]] + [a for d in blocks for a in cots[d]]
        + [wide, gain, wide, wide, wide] + list(diag) + list(carried) + list(after)
    )
    first = len(operands) - len(carried) - len(after)
    return pl.pallas_call(
        functools.partial(ffn_kernel, per, shards, blocks, len(carried) + len(after)),
        grid=(len(blocks) * per,),
        out_shape=tuple(shapes),
        in_specs=[smem()] + [crossed(d) for d in range(3) for _ in range(2)] + [spec for _, spec in last]
        + pieces(xs) + pieces(cots) + [weight(3), fixed(gain), weight(0), weight(1), weight(2)] + diag_specs + anywhere(carried) + anywhere(after),
        out_specs=tuple(specs),
        input_output_aliases={first + n: n for n in range(len(carried))},
        scratch_shapes=[pltpu.VMEM((units, width), BF16)],
        compiler_params=params(),
        cost_estimate=COST,
        name="ffn",
    )(*operands)


DOWN_STEPS = 3


def weights_kernel(shards, nf_ref, dgu_from, hid_ref, cot_ref, out_ref, down_ref, dgu_ref, sem):
    i = pl.program_id(0)
    copy = pltpu.make_async_copy(dgu_from, dgu_ref, sem)

    @pl.when(i == 0)
    def _():
        copy.start()

    @pl.when(i < DOWN_STEPS)
    def _():
        down_ref[at_rows(i, hid_ref.shape[1]), :] = dot_tn(hid_ref[...], cot_ref[...])

    @pl.when(i == DOWN_STEPS)
    def _():
        copy.wait()

    @pl.when(i >= DOWN_STEPS)
    def _():
        out_ref[:, :dgu_ref.shape[1]] = dot_tn(nf_ref[...], dgu_ref[...]).astype(BF16)

    per, piece = shards // 4, down_ref.shape[0] // shards
    rows = out_ref.shape[0] // per
    for k in range(shards):

        @pl.when(i == DOWN_STEPS + k // per)
        def _(k=k):
            block = pack_rows(down_ref[k * piece:(k + 1) * piece, :], rows)
            at = k % per * rows
            out_ref[at:at + rows, dgu_ref.shape[1]:] = block.astype(BF16)


def weights_back(nf, d_gu, hidden, cot, shards):
    rows, depth = nf.shape
    late = lambda i: jnp.maximum(i - DOWN_STEPS, 0)
    units = hidden.shape[1]
    wide = d_gu.shape[1] + units
    return pl.pallas_call(
        functools.partial(weights_kernel, shards),
        grid=(DOWN_STEPS + 4,),
        out_shape=jax.ShapeDtypeStruct((depth, wide), BF16),
        in_specs=[
            pl.BlockSpec((rows, depth // 4), lambda i: (0, late(i))), pl.BlockSpec(memory_space=pl.ANY),
            pl.BlockSpec((rows, units // DOWN_STEPS), lambda i: (0, jnp.minimum(i, DOWN_STEPS - 1))), fixed(cot),
        ],
        out_specs=pl.BlockSpec((depth // 4, wide), lambda i: (late(i), 0)),
        scratch_shapes=[
            pltpu.VMEM((units, cot.shape[1]), F32), pltpu.VMEM(d_gu.shape, BF16), pltpu.SemaphoreType.DMA,
        ],
        compiler_params=params(),
        cost_estimate=COST,
        name="weights_back",
    )(nf, d_gu, hidden, cot)


def middle_kernel(*refs):
    me_ref, dn_refs = refs[0], refs[1:4]
    cot_ref, mid_ref, gain_ref, wide_ref = refs[4:8]
    dmid_ref, branch_ref, da_refs, wo_ref, sem = refs[-8], refs[-7], refs[-6:-2], refs[-2], refs[-1]
    at = wide_ref.shape[1] // 4 * 3
    copy = pltpu.make_async_copy(wide_ref.at[:, at:at + wo_ref.shape[1]], wo_ref, sem)
    copy.start()
    me = me_ref[0]
    tok = mid_ref.shape[0]

    def rows_of(i, carry):
        rows = at_rows(i)
        middle = mid_ref[rows, :]
        d_normed = dn_refs[0][rows, :].astype(F32)
        for ref in dn_refs[1:]:
            d_normed = d_normed + ref[rows, :].astype(F32)
        r2 = lax.rsqrt(jnp.mean(middle * middle, axis=1, keepdims=True) + EPSILON)
        scaled = d_normed * gain_ref[...]
        pull = jnp.mean(scaled * middle, axis=1, keepdims=True)
        d_middle = cot_ref[rows, :].astype(F32) + r2 * scaled - middle * (r2 * r2 * r2 * pull)
        dmid_ref[rows, :] = d_middle
        branch_ref[rows, :] = d_middle.astype(BF16)
        return carry

    lax.fori_loop(0, tok // ROWS, rows_of, 0)
    copy.wait()
    span = 2 * LANES
    for d in range(4):
        there = pl.ds(pl.multiple_of(jnp.bitwise_xor(me, d) * span, span), span)
        da_refs[d][...] = dot_nt(branch_ref[...], wo_ref[there, :branch_ref.shape[1]]).astype(BF16)


def out_kernel(me_ref, *refs):
    att_refs, branch_ref, outs = refs[:8], refs[8], refs[9:]
    span = 2 * LANES
    for d in range(4):
        there = pl.ds(pl.multiple_of(jnp.bitwise_xor(me_ref[0], d) * span, span), span)
        rows = jnp.concatenate([att_refs[2 * d][...], att_refs[2 * d + 1][...]], axis=1)
        for e in range(4):
            columns = pl.ds(pl.multiple_of(jnp.bitwise_xor(me_ref[0], e) * span, span), span)
            outs[e][there, :] = dot_tn(rows, branch_ref[:, columns]).astype(BF16)


def out_weights(me, att, branch):
    tok, width = branch.shape
    whole = lambda r, c: pl.BlockSpec((r, c), lambda i: (0, 0))
    own = lambda d: pl.BlockSpec((tok, LANES), lambda i: (d, 0))
    return pl.pallas_call(
        out_kernel,
        grid=(1,),
        out_shape=(jax.ShapeDtypeStruct((width, width // 4), BF16),) * 4,
        in_specs=[smem()] + [own(d) for d in (0, 0, 1, 1, 2, 2, 3, 1)] + [whole(tok, width)],
        out_specs=(whole(width, width // 4),) * 4,
        compiler_params=params(),
        cost_estimate=COST,
        name="out_weights",
    )(me, *att[:7], att[8], branch)


def middle_back(me, parts, cot, middle, gain, wide, after):
    tok, width = middle.shape
    whole = lambda r, c: pl.BlockSpec((r, c), lambda i: (0, 0))
    out = lambda r, c, t=BF16: jax.ShapeDtypeStruct((r, c), t)
    return pl.pallas_call(
        middle_kernel,
        grid=(1,),
        out_shape=(out(tok, width, F32), out(tok, width)) + (out(tok, 2 * LANES),) * 4,
        in_specs=[smem()] + [whole(tok, width)] * 5 + [whole(1, width)] + anywhere((wide,) + tuple(after)),
        out_specs=(whole(tok, width),) * 2 + (whole(tok, 2 * LANES),) * 4,
        scratch_shapes=[pltpu.VMEM((wide.shape[0], width), BF16), pltpu.SemaphoreType.DMA],
        compiler_params=params(),
        cost_estimate=COST,
        name="middle_back",
    )(me, *parts, cot, middle, gain, wide, *after)


def swap(array, distance):
    return lax.ppermute(array, "seq", [(s, s ^ distance) for s in range(4)])


def gather_rows(block, meanwhile):
    half = block.shape[1] // 2
    one, two = swap(block, 1), swap(block, 2)
    one, two, meanwhile = lax.optimization_barrier((one, two, meanwhile))
    return [meanwhile, [one], [two], [swap(one[:, :half], 2), swap(two[:, half:], 1)]]


def after(value, *others):
    return lax.optimization_barrier((value, others))[0]


def body(
    tokens, order, seq_lengths, attn_gain, w_query, w_key, w_value, query_gain, key_gain,
    w_out, ffn_gain, w_gate, w_up, w_down, cotangent,
):
    tok = tokens.shape[1]
    ways = lax.axis_size("seq")
    shards = lax.axis_size("shard")
    all_rows = tok * ways
    head_dim = query_gain.shape[0]
    me = lax.axis_index("seq")
    me_arr = me.astype(jnp.int32)[None]
    own = lambda a, axis: lax.dynamic_slice_in_dim(a, me * (a.shape[axis] // ways), a.shape[axis] // ways, axis)
    depth = w_gate.shape[0]
    units = w_gate.shape[1] // ways
    piece = units // shards

    cosine, sine_up, sine_down, ocol, orow = make_tables(me_arr, seq_lengths, order, head_dim)
    q_gain = jnp.tile(query_gain.astype(F32), LANES // head_dim)[None, :]
    k_gain = jnp.tile(key_gain.astype(F32), LANES // head_dim)[None, :]

    tables = (cosine, sine_up, sine_down, ocol, orow, q_gain, k_gain)

    xs = gather_rows(tokens[0], tables)
    w_first = first_weights(me_arr, w_query, w_key, w_value, attn_gain, ffn_gain)
    w_qkv = lax.all_gather(w_first, "shard", axis=0, tiled=True)
    w_cut = cut_weights(me_arr, w_gate, w_up, own(w_down, 0), w_out, shards)
    w_wide = lax.all_gather(after(w_cut, xs[1]), "shard", axis=0, tiled=True)

    cosine, sine_up, sine_down, ocol, orow, q_gain, k_gain = xs[0]
    xs = [[tokens[0]]] + xs[1:]
    normed, qx, k, v, vx, kt, rawq, rawk, gains = qkv(
        [x for one in xs for x in one], w_qkv, ocol, cosine, sine_up, sine_down, q_gain, k_gain, head_dim
    )
    cot = cotangent[0]
    cots = gather_rows(after(cot, xs[3]), gains)
    gains, cots = cots[0], [[cot]] + cots[1:]
    gain_a, gain_f = gains[0:1], gains[1:2]
    w_rows = jnp.concatenate(after([w_query, w_key, w_value], xs[3]), axis=1)
    w_all = lax.all_gather(w_rows, "shard", axis=0, tiled=True)

    att, dealts, lses = [], [], []
    for g in range(2):
        given, dealt, lse = attend(g, seq_lengths, orow, qx, k, vx, head_dim, [])
        one, two = swap(given, 1), swap(given, 2)
        half = given.shape[0] // 2
        three = [swap(one[:half], 2), swap(two[half:], 1)] if g else [swap(given, 3)]
        att.append([given, one, two] + three)
        dealts.append(dealt)
        lses.append(lse)
    att = [att[g][d] for d in range(3) for g in range(2)] + att[0][3:] + att[1][3:]

    feed = lambda blocks, diag, carried, after=(): ffn(
        me_arr, blocks, att, xs, cots, gain_f, w_wide, shards, diag, carried, after
    )
    *carried, dn3a, dn3b, bo3a, bo3b = feed((3,), (), (), att[8:])
    diag = (swap(dn3a, 1), swap(dn3b, 2), swap(bo3a, 1), swap(bo3b, 2))
    *carried, dn0, bo0, middle = feed((0,), (), carried)
    *carried, dn1, dn2, bo1, bo2 = feed((1, 2), diag, carried)
    nf, hidden, d_gu, cot_all = carried
    dn = (dn0, swap(dn1, 1), swap(dn2, 2))
    scatter = lambda a: lax.psum_scatter(a, "shard", scatter_dimension=0, tiled=True)
    p_ffn = weights_back(nf, d_gu, hidden, cot_all, shards)
    d_ffn = scatter(after(p_ffn, dn))

    d_middle, branch, *d_att = middle_back(me_arr, dn, cot, middle, gain_f, w_wide, (p_ffn, w_all))
    p_wo = out_weights(me_arr, att, branch)
    d_att = [d_att[0]] + [swap(d_att[d], d) for d in (1, 2, 3)]
    draw, head_gains = attend_back(
        seq_lengths, ocol, qx, k, v, kt, lses, dealts, d_att, rawq, rawk,
        cosine, sine_up, sine_down, q_gain, k_gain, head_dim,
    )
    bo1, bo2, *p_wo = after([bo1, bo2] + list(p_wo), d_att)
    bo = [bo0, swap(bo1, 1), swap(bo2, 2)]
    p_wo = [p_wo[0]] + [swap(p_wo[d], d) for d in (1, 2, 3)]
    grads, *d_raw = rows_back(orow, draw, bo[1:3])
    d_raw = [d_raw[0]] + [swap(d_raw[d], d) for d in (1, 2, 3)]
    p_last = last_weights(normed, grads, p_wo, head_gains, shards)
    block_out = (middle + sum(b.astype(F32) for b in after(bo, p_last))).astype(BF16)
    d_last = scatter(after(p_last, d_ffn, d_raw[:3]))
    d_tokens = tokens_back(me_arr, d_raw, w_all, tokens[0], d_middle, gain_a, (p_last,))
    d_ffn = after(d_ffn, d_raw, p_last)

    def two_stages(part):
        half = part.shape[1] // 2 // LANES * LANES
        one, two = swap(part, 1), swap(part, 2)
        return [part, one, two, swap(one[:, :half], 2), swap(two[:, half:], 1)]

    def parts_of(part):
        return [part] + [swap(part, d) for d in (1, 2, 3)]

    d_wg, d_wu, d_wd, d_ffn_gain = join_weights(me_arr, two_stages(d_ffn), w_gate, w_up, ffn_gain, w_down.shape, shards)
    d_wq, d_wk, d_wv, d_wo, d_attn_gain, d_query_gain, d_key_gain = join_last(
        me_arr, parts_of(after(d_last, d_ffn, d_tokens, block_out)), w_query, w_key, w_value, attn_gain,
        w_out.shape[1], head_dim,
    )
    return (
        block_out[None], d_tokens[None], d_attn_gain[0], d_wq, d_wk, d_wv, d_query_gain[0], d_key_gain[0],
        d_wo, d_ffn_gain[0], d_wg, d_wu, d_wd,
    )


def solution(mesh):
    rows, flat, wide = P("shard", None), P("shard"), P("shard", "seq", None)
    in_specs = (
        wide, rows, rows, flat, rows, rows, rows, P(), P(), rows, flat, rows, rows, rows, wide,
    )
    out_specs = (wide, wide, flat, rows, rows, rows, P(), P(), rows, flat, rows, rows, rows)
    return jax.shard_map(body, mesh=mesh, in_specs=in_specs, out_specs=out_specs, check_vma=False)
```
